32 devices in a mesh: batch: 8 (over z, x), head: 4 (over y, core).
Axes of the slice: x: 2, y: 2, z: 4, core: 2. Of those that a mesh axis runs over, the one named last changes fastest.
Arguments:
- low_patches: bfloat16 [16, 196, 768], P('batch')
- high_patches: bfloat16 [16, 576, 768], P('batch')
- interp: bfloat16 [576, 196], replicated, may hold values from 0 to 2
- labels: int32 [32], P('batch'), may hold values from 0 to 999
- partner: int32 [32], P('batch'), may hold values from 0 to 31, as said below
- pair_count: int32 [1], replicated, may hold values from 32 to 64
- w_patch: float32 [768, 768], P('batch'), may hold values from -0.21875 to 0.21875
- pos_table: float32 [197, 768], P(None, 'batch'), may hold values from -3 to 3
- vectors: float32 [10, 768], P(None, 'batch')
- head_w: float32 [768, 1256], P('batch'), may hold values from -0.4375 to 0.4375
- w_qkv: float32 [768, 2304], P('batch', 'head'), may hold values from -0.21875 to 0.21875
- w_out: float32 [768, 768], P('batch', 'head'), may hold values from -0.21875 to 0.21875
- w_up: float32 [768, 3072], P('batch', 'head'), may hold values from -0.21875 to 0.21875
- w_down: float32 [768, 3072], P('batch', 'head'), may hold values from -0.109375 to 0.109375
- mom_qkv: float32 [768, 2304], P('batch', 'head'), may hold values from -0.00067453353 to 0.00067453353
- mom_out: float32 [768, 768], P('batch', 'head'), may hold values from -0.00067453353 to 0.00067453353
- mom_up: float32 [768, 3072], P('batch', 'head'), may hold values from -0.00067453353 to 0.00067453353
- mom_down: float32 [768, 3072], P('batch', 'head'), may hold values from -0.00067453353 to 0.00067453353
- first_patch: float32 [768, 768], P('batch'), may hold values from -3.0517578e-05 to 3.0517578e-05
- second_patch: float32 [768, 768], P('batch'), may hold values from 1.4218609e-12 to 1.1374887e-11
- first_pos: float32 [197, 768], P(None, 'batch'), may hold values from -2.9802322e-07 to 2.9802322e-07
- second_pos: float32 [197, 768], P(None, 'batch'), may hold values from 2.637893e-16 to 1.0258472e-15
- first_vec: float32 [10, 768], P(None, 'batch'), may hold values from -0.00015258789 to 0.00015258789
- second_vec: float32 [10, 768], P(None, 'batch'), may hold values from 3.412466e-11 to 2.843722e-10
- first_head: float32 [768, 1256], P('batch'), may hold values from -3.0517578e-05 to 3.0517578e-05
- second_head: float32 [768, 1256], P('batch'), may hold values from 1.4218609e-12 to 1.1374887e-11
Outputs:
- new_patch: float32 [768, 768], P('batch')
- new_pos: float32 [197, 768], P(None, 'batch')
- new_vectors: float32 [10, 768], P(None, 'batch')
- new_head: float32 [768, 1256], P('batch')
- new_qkv: float32 [768, 2304], P('batch', 'head')
- new_out: float32 [768, 768], P('batch', 'head')
- new_up: float32 [768, 3072], P('batch', 'head')
- new_down: float32 [768, 3072], P('batch', 'head')
- moment_qkv: float32 [768, 2304], P('batch', 'head')
- moment_out: float32 [768, 768], P('batch', 'head')
- moment_up: float32 [768, 3072], P('batch', 'head')
- moment_down: float32 [768, 3072], P('batch', 'head')
- new_first_patch: float32 [768, 768], P('batch')
- new_first_pos: float32 [197, 768], P(None, 'batch')
- new_first_vec: float32 [10, 768], P(None, 'batch')
- new_first_head: float32 [768, 1256], P('batch')
- new_second_patch: float32 [768, 768], P('batch')
- new_second_pos: float32 [197, 768], P(None, 'batch')
- new_second_vec: float32 [10, 768], P(None, 'batch')
- new_second_head: float32 [768, 1256], P('batch')
- losses: float32 [2], replicated
- grad_norm: float32 [1], replicated
- moment_logs: float32 [4], replicated
The draws below stay inside these ranges and needn't reach their ends.
Inputs may be any that keep to these rules, and one draw needn't show every extreme that they name: partner[partner[i]] == i and partner[i] != i: the images fall into pairs of two views.
All inputs are finite; a program needn't handle non-finite values.
Results may differ from the reference program's by a relative error of at most 0.02.
Values may be sent and summed in bfloat16 or wider, within the bound.
No kernel may reach another device: no remote copies, remote signals or barrier semaphores. Data moves between devices by JAX's collectives and lax.ppermute only.
A program may use at most 192 MiB of HBM per device.

```python
import math
import jax
import jax.numpy as jnp
from jax import lax

D = 768
HEADS = 12
HD = 64
FF = 3072
CLS = 1000
PIX = 768
PROJ = 256
GRID_LOW = 196
GRID_HIGH = 576
LOW_DEV = 2
HIGH_DEV = 2
NS_STEPS = 3
STEP = 10
LOW_LEN = 197
IMG_LOW = 16
IMG_HIGH = 16
IMAGES = 32
NPARAM = 8791296
N_BATCH = 8
N_HEAD = 4


def draw_low_patches(key, part):
    key = jax.random.fold_in(key, 11)
    common = jax.random.normal(jax.random.fold_in(key, 1), (IMG_LOW, 1, PIX), jnp.float32)
    noise = jax.random.normal(jax.random.fold_in(key, 2), (IMG_LOW, GRID_LOW, PIX), jnp.float32)
    return (common + 0.8 * noise).astype(jnp.bfloat16)


def draw_high_patches(key, part):
    key = jax.random.fold_in(key, 12)
    common = jax.random.normal(jax.random.fold_in(key, 1), (IMG_HIGH, 1, PIX), jnp.float32)
    noise = jax.random.normal(jax.random.fold_in(key, 2), (IMG_HIGH, GRID_HIGH, PIX), jnp.float32)
    return (common + 0.8 * noise).astype(jnp.bfloat16)


def grid_weights(key, factor_lo, factor_hi):
    low_side = math.isqrt(GRID_LOW)
    high_side = math.isqrt(GRID_HIGH)
    stretch = (low_side - 1) / (high_side - 1)
    high_ids = jnp.arange(GRID_HIGH, dtype=jnp.int32)
    low_ids = jnp.arange(GRID_LOW, dtype=jnp.int32)
    row_at = (high_ids // high_side).astype(jnp.float32) * stretch
    col_at = (high_ids % high_side).astype(jnp.float32) * stretch
    low_row = (low_ids // low_side).astype(jnp.float32)
    low_col = (low_ids % low_side).astype(jnp.float32)
    tent_rows = jnp.maximum(0.0, 1.0 - jnp.abs(row_at[:, None] - low_row[None, :]))
    tent_cols = jnp.maximum(0.0, 1.0 - jnp.abs(col_at[:, None] - low_col[None, :]))
    factors = jax.random.uniform(jax.random.fold_in(key, 1), (GRID_HIGH, GRID_LOW), jnp.float32, factor_lo, factor_hi)
    background = jax.random.uniform(jax.random.fold_in(key, 2), (GRID_HIGH, GRID_LOW), jnp.float32, 0.0, 0.2 / GRID_LOW)
    return tent_rows * tent_cols * factors + background


def draw_interp(key, part):
    key = jax.random.fold_in(key, 15)
    return grid_weights(key, 0.5, 1.5).astype(jnp.bfloat16)


def draw_vectors(key, part):
    key = jax.random.fold_in(key, 13)
    row_ids = jnp.arange(10)[:, None]
    gains = jax.random.uniform(jax.random.fold_in(key, 1), (10, D), jnp.float32, 0.6, 1.4)
    shifts = 0.2 * jax.random.normal(jax.random.fold_in(key, 2), (10, D), jnp.float32)
    tokens = jax.random.normal(jax.random.fold_in(key, 3), (10, D), jnp.float32)
    is_gain = (row_ids == 0) | (row_ids == 2) | (row_ids == 4)
    return jnp.where(is_gain, gains, jnp.where(row_ids == 9, tokens, shifts))


def draw_partner(key, part):
    key = jax.random.fold_in(key, 14)
    order = jax.random.permutation(key, IMAGES).astype(jnp.int32).reshape(IMAGES // 2, 2)
    paired = jnp.zeros((IMAGES,), jnp.int32)
    paired = paired.at[order[:, 0]].set(order[:, 1])
    return paired.at[order[:, 1]].set(order[:, 0])


def ramped_moment(key, columns, row_top):
    base = jnp.clip(jax.random.normal(key, (D, columns), jnp.float32), -4.0, 4.0)
    row_factor = 1.0 + (row_top - 1.0) * jnp.arange(D, dtype=jnp.float32)[:, None] / (D - 1)
    column_factor = 1.0 + jnp.arange(columns, dtype=jnp.float32)[None, :] / (columns - 1)
    return 0.05 * NPARAM ** (-0.5) * base * row_factor * column_factor


def draw_mom_qkv(key, part):
    key = jax.random.fold_in(key, 21)
    return ramped_moment(key, 3 * D, 3.0)


def draw_mom_out(key, part):
    key = jax.random.fold_in(key, 22)
    return ramped_moment(key, D, 3.0)


def draw_mom_up(key, part):
    key = jax.random.fold_in(key, 23)
    return ramped_moment(key, FF, 3.0)


def draw_mom_down(key, part):
    key = jax.random.fold_in(key, 24)
    return ramped_moment(key, FF, 3.0)


def with_ends(entries, stream_key, low, largest):
    longest = entries.shape.index(max(entries.shape))
    spots = []
    for shift in (0, 1):
        where = [jax.random.randint(jax.random.fold_in(stream_key, axis), (), 0, length) for axis, length in enumerate(entries.shape)]
        where[longest] = (where[longest] + shift) % entries.shape[longest]
        spots.append(tuple(where))
    return entries.at[spots[0]].set(low).at[spots[1]].set(largest)


def level_of(stream_key, dims, pieces, least, top_value):
    level = 1.0
    for position, shards_of in pieces:
        heights = jax.random.uniform(jax.random.fold_in(jax.random.fold_in(stream_key, 6), position), (shards_of,), jnp.float32, least / len(pieces), top_value / len(pieces))
        level = level * jnp.repeat(jnp.exp(heights), dims[position] // shards_of).reshape((-1,) + (1,) * (len(dims) - 1 - position))
    return level


def normal_values(own_key, dims, deviation, bound, pieces=(), held_as=jnp.bfloat16):
    array = jax.random.normal(own_key, dims, jnp.float32) * deviation
    if len(pieces) > 0:
        array = level_of(own_key, dims, pieces, -0.22, 0.18) * array
    return jnp.clip(array, min=-bound, max=bound).astype(held_as)


def setup_inputs(seed: int = 0) -> dict:
    keys = jax.random.split(jax.random.key(seed), 27)
    return {
        "low_patches": draw_low_patches(jax.random.fold_in(keys[26], 71), 0),
        "high_patches": draw_high_patches(jax.random.fold_in(keys[26], 71), 0),
        "interp": draw_interp(jax.random.fold_in(keys[26], 71), 0),
        "labels": with_ends(jax.random.randint(keys[3], (IMAGES,), 0, CLS), jax.random.fold_in(keys[3], 1), 0, CLS - 1).astype(jnp.int32),
        "partner": draw_partner(jax.random.fold_in(keys[26], 71), 0),
        "pair_count": jax.random.randint(keys[5], (1,), IMAGES, 2 * IMAGES + 1).astype(jnp.int32),
        "w_patch": normal_values(keys[6], (PIX, D), PIX ** -0.5, 0.21875, ((0, 8),), jnp.float32),
        "pos_table": normal_values(keys[7], (LOW_LEN, D), 0.5, 3.0, ((1, 8),), jnp.float32),
        "vectors": draw_vectors(jax.random.fold_in(keys[26], 71), 0),
        "head_w": normal_values(keys[9], (D, CLS + PROJ), (D // 4) ** -0.5, 0.4375, ((0, 8),), jnp.float32),
        "w_qkv": normal_values(keys[10], (D, 3 * D), D ** -0.5, 0.21875, ((0, 8), (1, 4)), jnp.float32),
        "w_out": normal_values(keys[11], (D, D), D ** -0.5, 0.21875, ((0, 8), (1, 4)), jnp.float32),
        "w_up": normal_values(keys[12], (D, FF), D ** -0.5, 0.21875, ((0, 8), (1, 4)), jnp.float32),
        "w_down": normal_values(keys[13], (D, FF), FF ** -0.5, 0.109375, ((0, 8), (1, 4)), jnp.float32),
        "mom_qkv": draw_mom_qkv(jax.random.fold_in(keys[26], 71), 0),
        "mom_out": draw_mom_out(jax.random.fold_in(keys[26], 71), 0),
        "mom_up": draw_mom_up(jax.random.fold_in(keys[26], 71), 0),
        "mom_down": draw_mom_down(jax.random.fold_in(keys[26], 71), 0),
        "first_patch": normal_values(keys[18], (PIX, D), (0.006 * NPARAM ** -0.5), 3.0517578125e-05, ((0, 8),), jnp.float32),
        "second_patch": jnp.clip(jnp.exp(math.log(1.1374887143311696e-11) - 2.0794415 * jax.random.uniform(keys[19], (PIX, D), jnp.float32) ** level_of(keys[19], (PIX, D), ((0, 8),), -0.2, 0.2)), 1.421860892913962e-12, 1.1374887143311696e-11),
        "first_pos": normal_values(keys[20], (LOW_LEN, D), (0.012 * NPARAM ** -0.5 / LOW_LEN), 2.980232238769531e-07, ((1, 8),), jnp.float32),
        "second_pos": jnp.clip(jnp.exp(math.log(1.0258472140129587e-15) - 1.3581234 * jax.random.uniform(keys[21], (LOW_LEN, D), jnp.float32) ** level_of(keys[21], (LOW_LEN, D), ((1, 8),), -0.2, 0.2)), 2.637893002414794e-16, 1.0258472140129587e-15),
        "first_vec": normal_values(keys[22], (10, D), (0.03 * NPARAM ** -0.5), 0.00015258789, ((1, 8),), jnp.float32),
        "second_vec": jnp.clip(jnp.exp(math.log(2.843721924605802e-10) - 2.1202636 * jax.random.uniform(keys[23], (10, D), jnp.float32) ** level_of(keys[23], (10, D), ((1, 8),), -0.2, 0.2)), 3.412466142993509e-11, 2.843721924605802e-10),
        "first_head": normal_values(keys[24], (D, CLS + PROJ), (0.006 * NPARAM ** -0.5), 3.0517578125e-05, ((0, 8),), jnp.float32),
        "second_head": jnp.clip(jnp.exp(math.log(1.1374887143311696e-11) - 2.0794415 * jax.random.uniform(keys[25], (D, CLS + PROJ), jnp.float32) ** level_of(keys[25], (D, CLS + PROJ), ((0, 8),), -0.2, 0.2)), 1.421860892913962e-12, 1.1374887143311696e-11),
    }


PRECISE = lax.Precision.HIGHEST
POLY_ONE = 3.4445
POLY_TWO = -4.775
POLY_THREE = 2.0315
SOFTMAX_TEMP = 0.05
CLIP_NORM = 0.05
MOMENTUM = 0.95
MUON_RATE = 0.2
DECAY_RATE = 0.05
BETA_FIRST = 0.9
BETA_SECOND = 0.99
ADAM_FLOOR = 1e-08
ADAM_RATES = (0.08, 0.3, 0.5, 0.15)
ADAM_DECAYS = (0.05, 0.05, 0.0, 0.05)

@jax.custom_vjp
def low(v):
    return lax.optimization_barrier(v.astype(jnp.bfloat16)).astype(jnp.float32)

@jax.custom_vjp
def low_back(v):
    return v

def low_keep(v):
    return (low(v), None)

def low_pass(kept, grad):
    return (grad,)

def back_keep(v):
    return (v, None)

def back_low(kept, grad):
    return (low(grad),)
low.defvjp(low_keep, low_pass)
low_back.defvjp(back_keep, back_low)

def matrix_multiply(left_side, right_side):
    return jnp.matmul(left_side, right_side, precision=PRECISE)

def layer_norm(values, gain_row, shift_row):
    centred = values - lax.optimization_barrier(jnp.mean(values, -1, keepdims=True))
    return centred * lax.rsqrt(lax.optimization_barrier(jnp.mean(centred * centred, -1, keepdims=True)) + 1e-06) * gain_row + shift_row

def encode_image(patches, pos_rows, weights):
    w_patch, vectors, w_qkv, w_out, w_up, w_down = weights
    length = pos_rows.shape[0]
    group_heads = HEADS // N_HEAD
    span_width = group_heads * HD
    hidden_width = FF // N_HEAD
    embedded = low_back(matrix_multiply(patches, w_patch)) + vectors[6]
    initial = jnp.concatenate([vectors[9][None, :], embedded], 0) + pos_rows
    normed = low(layer_norm(initial, vectors[0], vectors[1]))
    branch = jnp.zeros((length, D), jnp.float32)
    for section in range(N_HEAD):
        packed = matrix_multiply(low_back(normed), w_qkv[:, section * 3 * span_width:(section + 1) * 3 * span_width])
        packed = packed.reshape(length, group_heads, 3, HD)
        queries = low_back(low(packed[:, :, 0]))
        key_rows = low_back(low(packed[:, :, 1]))
        value_rows = low_back(low(packed[:, :, 2]))
        scores = low_back(jnp.einsum('qhd,khd->hqk', queries, key_rows, precision=PRECISE) * HD ** (-0.5))
        soft_rows = low(jax.nn.softmax(scores, -1))
        blended = jnp.einsum('hqk,khd->qhd', soft_rows, value_rows, precision=PRECISE).reshape(length, span_width)
        blended = low_back(low(blended))
        columns = w_out[:, section * span_width:(section + 1) * span_width]
        branch = branch + low(low_back(matrix_multiply(blended, columns.T)))
    middle = initial + vectors[7] + branch
    normed_two = low(layer_norm(middle, vectors[2], vectors[3]))
    branch_two = jnp.zeros((length, D), jnp.float32)
    for section in range(N_HEAD):
        lower = section * hidden_width
        upper = (section + 1) * hidden_width
        upward = low_back(matrix_multiply(low_back(normed_two), w_up[:, lower:upper]))
        active = low(jax.nn.gelu(upward, approximate=False))
        branch_two = branch_two + low(low_back(matrix_multiply(active, w_down[:, lower:upper].T)))
    output_rows = middle + vectors[8] + branch_two
    return lax.optimization_barrier(jnp.mean(output_rows, 0))

def total_loss(params, low_patches, high_patches, interp, labels, partner, count):
    rounded = [low(weight) for weight in params]
    w_patch, pos_table, vectors, head_w, w_qkv, w_out, w_up, w_down = rounded
    weights = (w_patch, vectors, w_qkv, w_out, w_up, w_down)
    pos_high = jnp.concatenate([pos_table[:1], matrix_multiply(interp, pos_table[1:])], 0)
    encoder = jax.checkpoint(lambda patches, pos_rows: encode_image(patches, pos_rows, weights))
    pooled_low = lax.map(lambda patches: encoder(patches, pos_table), low_patches)
    pooled_high = lax.map(lambda patches: encoder(patches, pos_high), high_patches)
    pooled = jnp.concatenate([pooled_low.reshape(N_BATCH, LOW_DEV, D), pooled_high.reshape(N_BATCH, HIGH_DEV, D)], 1)
    pooled = pooled.reshape(IMAGES, D)
    features = low(layer_norm(pooled, vectors[4], vectors[5]))
    outputs = low_back(matrix_multiply(features, head_w))
    logits = outputs[:, :CLS]
    projected = outputs[:, CLS:]
    class_sum = jnp.sum(jax.nn.logsumexp(logits, -1) - jnp.take_along_axis(logits, labels[:, None], 1)[:, 0])
    normalized_rows = projected * lax.rsqrt(lax.optimization_barrier(jnp.sum(projected * projected, -1, keepdims=True)) + 1e-06)
    normalized_rows = low_back(low(normalized_rows))
    similarity_scores = low_back(matrix_multiply(normalized_rows, normalized_rows.T) / SOFTMAX_TEMP)
    indices = jnp.arange(IMAGES)
    masked = jnp.where(indices[:, None] == indices[None, :], -1e+30, similarity_scores)
    pair_sum = jnp.sum(jax.nn.logsumexp(masked, -1) - jnp.take_along_axis(similarity_scores, partner[:, None], 1)[:, 0])
    pair_loss = pair_sum / count
    class_loss = class_sum / IMAGES
    return (pair_loss + class_loss, jnp.stack([pair_sum, class_sum]))

def muon_direction(moment):
    iterate = moment / (jnp.sqrt(jnp.sum(moment * moment)) + 1e-07)
    for sweep in range(NS_STEPS):
        gram = matrix_multiply(iterate, iterate.T)
        iterate = POLY_ONE * iterate + matrix_multiply(POLY_TWO * gram + POLY_THREE * matrix_multiply(gram, gram), iterate)
    return iterate

def adam_update(weight, gradient, first, second, rate, decay):
    first = BETA_FIRST * first + (1.0 - BETA_FIRST) * gradient
    second = BETA_SECOND * second + (1.0 - BETA_SECOND) * gradient * gradient
    direction = first / (1.0 - BETA_FIRST ** STEP) / (jnp.sqrt(second / (1.0 - BETA_SECOND ** STEP)) + ADAM_FLOOR)
    return (weight - rate * (direction + decay * weight), first, second)

def reference(low_patches, high_patches, interp, labels, partner, pair_count, w_patch, pos_table, vectors, head_w, w_qkv, w_out, w_up, w_down, mom_qkv, mom_out, mom_up, mom_down, first_patch, second_patch, first_pos, second_pos, first_vec, second_vec, first_head, second_head):
    params = (w_patch, pos_table, vectors, head_w, w_qkv, w_out, w_up, w_down)
    count = pair_count[0].astype(jnp.float32)
    low_rows = low_patches.astype(jnp.float32)
    high_rows = high_patches.astype(jnp.float32)
    interp_rows = interp.astype(jnp.float32)

    def loss_of(weights):
        return total_loss(weights, low_rows, high_rows, interp_rows, labels, partner, count)
    loss, back, losses = jax.vjp(loss_of, params, has_aux=True)
    grads = back(jnp.ones((), jnp.float32))[0]
    norm = jnp.sqrt(sum((jnp.sum(gradient * gradient) for gradient in grads)))
    factor = jnp.minimum(1.0, CLIP_NORM / norm)
    clipped = [factor * gradient for gradient in grads]
    firsts = (first_patch, first_pos, first_vec, first_head)
    seconds = (second_patch, second_pos, second_vec, second_head)
    adam_new = [adam_update(params[index], clipped[index], firsts[index], seconds[index], ADAM_RATES[index], ADAM_DECAYS[index]) for index in range(4)]
    momenta = (mom_qkv, mom_out, mom_up, mom_down)
    new_moments = [MOMENTUM * momenta[index] + clipped[4 + index] for index in range(4)]
    moment_logs = jnp.log(jnp.stack([jnp.sum(moment * moment) for moment in new_moments]))
    new_muon = []
    for index in range(4):
        weight = params[4 + index]
        scale = 0.2 * jnp.sqrt(jnp.float32(max(D, weight.shape[1])))
        new_muon.append(weight - MUON_RATE * (scale * muon_direction(new_moments[index]) + DECAY_RATE * weight))
    return (adam_new[0][0], adam_new[1][0], adam_new[2][0], adam_new[3][0], new_muon[0], new_muon[1], new_muon[2], new_muon[3], new_moments[0], new_moments[1], new_moments[2], new_moments[3], adam_new[0][1], adam_new[1][1], adam_new[2][1], adam_new[3][1], adam_new[0][2], adam_new[1][2], adam_new[2][2], adam_new[3][2], losses, norm[None], moment_logs)
```

```python
import math

import jax
import jax.numpy as jnp
from jax import lax
from jax.sharding import PartitionSpec as P

D = 768
HD = 64
CLS = 1000
NS_STEPS = 3
STEP = 10

POLY_ONE = 3.4445
POLY_TWO = -4.775
POLY_THREE = 2.0315
SOFTMAX_TEMP = 0.05
CLIP_NORM = 0.05
MOMENTUM = 0.95
MUON_RATE = 0.2
DECAY_RATE = 0.05
BETA_FIRST = 0.9
BETA_SECOND = 0.99
ADAM_FLOOR = 1e-08
ADAM_RATES = (0.08, 0.3, 0.5, 0.15)
ADAM_DECAYS = (0.05, 0.05, 0.0, 0.05)

BF = jnp.bfloat16
F32 = jnp.float32


def up_to(size, step):
    return -(-size // step) * step


def dot(left, right, left_dim=1, right_dim=0, precision=None):
    return lax.dot_general(
        left,
        right,
        (((left_dim,), (right_dim,)), ((), ())),
        precision=precision,
        preferred_element_type=F32,
    )


def at(stacked, index):
    return lax.dynamic_index_in_dim(stacked, index, 0, keepdims=False)


def swap(values, axis, mask):
    count = lax.axis_size(axis)
    return lax.ppermute(values, axis, [(index, index ^ mask) for index in range(count)])


def swap_core(values):
    return swap(values, "head", 1)


def swap_side(values):
    return swap(values, "head", 2)


def swap_x(values):
    return swap(values, "batch", 1)


def pair_sum(values):
    low = values.astype(BF)
    return low.astype(F32) + swap_core(low).astype(F32)


def gather_rows(shard):
    rows, columns = shard.shape
    count = lax.axis_size("batch")
    if count != 8:
        own = lax.all_gather(shard, "batch", axis=0, tiled=True)
        return own, swap_side(own)
    here = lax.axis_index("batch")
    z, x = here // 2, here % 2
    half = rows // 2
    lines = jnp.stack([shard] + [swap(shard, "batch", 2 * mask) for mask in (1, 2, 3)])
    first, second = lines[:, :half], lines[:, half:]
    first = jnp.stack([first, swap_x(first)])
    second = jnp.stack([second, swap_side(second)])
    first = jnp.stack([first, swap_side(first)])
    second = jnp.stack([second, swap_x(second)])
    first = first.reshape(2, 8, half, columns)
    groups = []
    for side in range(2):
        pieces = []
        for z_to in range(4):
            for x_to in range(2):
                x_from, z_from = x ^ x_to, z ^ z_to
                pieces.append(at(first[side], x_from * 4 + z_from))
                pieces.append(at(second[:, side].reshape(8, half, columns), x_from * 4 + z_from))
        groups.append(jnp.concatenate(pieces, 0))
    return groups


def reduce_rows(own, other):
    count = lax.axis_size("batch")
    columns = own.shape[1]
    rows = own.shape[0] // count
    if count != 8:
        total = own + swap_side(other.astype(BF)).astype(F32)
        return lax.psum_scatter(total, "batch", scatter_dimension=0, tiled=True)
    here = lax.axis_index("batch")
    z, x = here // 2, here % 2
    half = rows // 2

    def pick_x(blocks, index):
        return lax.dynamic_index_in_dim(blocks, index, 1, keepdims=False)

    own = own.reshape(4, 2, rows, columns)
    other = other.reshape(4, 2, rows, columns)
    first = own[:, :, :half] + swap_side(other[:, :, :half].astype(BF)).astype(F32)
    first = pick_x(first, x) + swap_x(pick_x(first, 1 - x).astype(BF)).astype(F32)
    second = jnp.stack([own[:, :, half:], other[:, :, half:]])
    second = second.transpose(1, 2, 0, 3, 4)
    second = pick_x(second, x) + swap_x(pick_x(second, 1 - x).astype(BF)).astype(F32)
    second = second[:, 0] + swap_side(second[:, 1].astype(BF)).astype(F32)
    both = jnp.concatenate([first, second], 1)
    total = at(both, z)
    for mask in (1, 2, 3):
        total = total + swap(at(both, z ^ mask).astype(BF), "batch", 2 * mask).astype(F32)
    return total


def in_order(stacked, here, bits):
    tail = stacked.shape[1:]
    stacked = stacked.reshape((2,) * bits + tail)
    for bit in range(bits):
        axis = bits - 1 - bit
        flag = (here >> bit) % 2 == 1
        stacked = jnp.where(flag, jnp.flip(stacked, axis), stacked)
    return stacked.reshape((2**bits,) + tail)


def gather_small(values):
    count = lax.axis_size("batch")
    if count != 8:
        return lax.all_gather(values, "batch", axis=0, tiled=False)
    pair = jnp.stack([values, swap_x(values)])
    lines = jnp.stack([pair] + [swap(pair, "batch", 2 * mask) for mask in (1, 2, 3)])
    return in_order(lines.reshape((8,) + values.shape), lax.axis_index("batch"), 3)


def sum_everywhere(values):
    for axis in ("head", "batch"):
        mask = 1
        while mask < lax.axis_size(axis):
            values = values + swap(values, axis, mask)
            mask *= 2
    return values


def sum_over_head(values):
    mask = 1
    while mask < lax.axis_size("head"):
        values = values + swap(values, "head", mask)
        mask *= 2
    return values


def all_quarters(own, other):
    pair = jnp.stack([own, other])
    four = jnp.concatenate([pair, swap_core(pair)])
    head = lax.axis_index("head")
    places = (0, 2, 1, 3)
    table = jnp.array(places, jnp.int32)
    return [at(four, table[head ^ index]) for index in range(4)]


def normalize(values):
    centred = values - jnp.mean(values, -1, keepdims=True)
    scale = lax.rsqrt(jnp.mean(centred * centred, -1, keepdims=True) + 1e-06)
    return centred * scale, scale


def normalize_back(grad, unit, scale, gain):
    grad_unit = grad * gain
    return scale * (
        grad_unit
        - jnp.mean(grad_unit, -1, keepdims=True)
        - unit * jnp.mean(grad_unit * unit, -1, keepdims=True)
    )


def attend(packed, length):
    tokens = packed.shape[0]
    queries, keys, values = packed[:, :, 0], packed[:, :, 1], packed[:, :, 2]
    scores = jnp.einsum("qhd,khd->hqk", queries, keys, preferred_element_type=F32)
    scores = scores * HD ** (-0.5)
    scores = jnp.where(jnp.arange(tokens) < length, scores, -1e30)
    top = jnp.max(scores, -1, keepdims=True)
    log_total = top + jnp.log(jnp.sum(jnp.exp(scores - top), -1, keepdims=True))
    soft = jnp.exp(scores - log_total).astype(BF)
    blended = jnp.einsum("hqk,khd->qhd", soft, values, preferred_element_type=F32)
    return blended.astype(BF), log_total, soft


def attend_back(packed, length, log_total, soft, grad):
    tokens = packed.shape[0]
    queries, keys, values = packed[:, :, 0], packed[:, :, 1], packed[:, :, 2]
    scale = HD ** (-0.5)
    grad_values = jnp.einsum("hqk,qhd->khd", soft, grad, preferred_element_type=F32)
    grad_soft = jnp.einsum("qhd,khd->hqk", grad, values, preferred_element_type=F32)
    scores = jnp.einsum("qhd,khd->hqk", queries, keys, preferred_element_type=F32) * scale
    scores = jnp.where(jnp.arange(tokens) < length, scores, -1e30)
    probs = jnp.exp(scores - log_total)
    grad_scores = probs * (grad_soft - jnp.sum(probs * grad_soft, -1, keepdims=True))
    grad_scores = grad_scores.astype(BF)
    grad_queries = (
        jnp.einsum("hqk,khd->qhd", grad_scores, keys, preferred_element_type=F32) * scale
    )
    grad_keys = (
        jnp.einsum("hqk,qhd->khd", grad_scores, queries, preferred_element_type=F32) * scale
    )
    return jnp.stack([grad_queries, grad_keys, grad_values], 2).astype(BF)


def adam_update(weight, gradient, first, second, rate, decay):
    first = BETA_FIRST * first + (1.0 - BETA_FIRST) * gradient
    second = BETA_SECOND * second + (1.0 - BETA_SECOND) * gradient * gradient
    direction = (
        first
        / (1.0 - BETA_FIRST**STEP)
        / (jnp.sqrt(second / (1.0 - BETA_SECOND**STEP)) + ADAM_FLOOR)
    )
    return (weight - rate * (direction + decay * weight), first, second)


def gram_blocks(matrix):
    step = D // 3
    rows = [matrix[index * step : (index + 1) * step] for index in range(3)]
    top = dot(rows[0], matrix, 1, 1)
    middle = dot(rows[1], matrix[step:], 1, 1)
    last = dot(rows[2], rows[2], 1, 1)
    return jnp.stack(
        [
            top[:, :step],
            top[:, step : 2 * step],
            top[:, 2 * step :],
            middle[:, :step],
            middle[:, step:],
            last,
        ]
    )


def whole_gram(blocks):
    aa, ab, ac, bb, bc, cc = [blocks[index] for index in range(6)]
    return jnp.concatenate(
        [
            jnp.concatenate([aa, ab, ac], 1),
            jnp.concatenate([ab.T, bb, bc], 1),
            jnp.concatenate([ac.T, bc.T, cc], 1),
        ],
        0,
    )


def body(
    low_patches,
    high_patches,
    interp,
    labels,
    partner,
    pair_count,
    w_patch,
    pos_table,
    vectors,
    head_w,
    w_qkv,
    w_out,
    w_up,
    w_down,
    mom_qkv,
    mom_out,
    mom_up,
    mom_down,
    first_patch,
    second_patch,
    first_pos,
    second_pos,
    first_vec,
    second_vec,
    first_head,
    second_head,
):
    batch = lax.axis_index("batch")
    head = lax.axis_index("head")
    side = head // 2
    batch_size = lax.axis_size("batch")
    head_size = lax.axis_size("head")
    rows_here = w_patch.shape[0]
    grid_low, grid_high = low_patches.shape[1], high_patches.shape[1]
    low_rows = up_to(grid_low + 1, 16)
    high_rows = up_to(grid_high + 1, 16)
    tokens = low_rows + high_rows
    qkv_width, out_width = w_qkv.shape[1], w_out.shape[1]
    hidden = w_up.shape[1]
    patch_width = D // head_size
    extra_width = 64
    head_columns = head_w.shape[1]
    head_padded = up_to(head_columns, 64 * head_size)
    head_width = head_padded // head_size
    table_rows = extra_width * head_size

    table = jnp.concatenate([pos_table[1:], pos_table[:1], vectors], 0).astype(BF)
    table = jnp.pad(table, ((0, table_rows - table.shape[0]), (0, 0))).T
    quarter_patch = lax.dynamic_slice_in_dim(w_patch, head * patch_width, patch_width, 1)
    quarter_table = lax.dynamic_slice_in_dim(table, head * extra_width, extra_width, 1)
    padded_head = jnp.pad(head_w.astype(BF), ((0, 0), (0, head_padded - head_columns)))
    quarter_head = lax.dynamic_slice_in_dim(padded_head, head * head_width, head_width, 1)
    chunk_one = jnp.concatenate(
        [quarter_patch.astype(BF), quarter_table, w_qkv.astype(BF), w_out.astype(BF)], 1
    )
    chunk_two = w_up.astype(BF)
    chunk_three = jnp.concatenate([w_down.astype(BF), quarter_head], 1)
    one = gather_rows(chunk_one)
    two = gather_rows(chunk_two)
    three = gather_rows(chunk_three)
    small = patch_width + extra_width
    quarters = all_quarters(one[0][:, :small], one[1][:, :small])
    full_patch = jnp.concatenate([quarter[:, :patch_width] for quarter in quarters], 1)
    table = jnp.concatenate([quarter[:, patch_width:] for quarter in quarters], 1).T
    full_qkv = jnp.concatenate([part[:, small : small + qkv_width] for part in one], 1)
    full_out = jnp.concatenate([part[:, small + qkv_width :] for part in one], 1)
    full_up = jnp.concatenate(two, 1)
    full_down = jnp.concatenate([part[:, :hidden] for part in three], 1)
    quarters = all_quarters(three[0][:, hidden:], three[1][:, hidden:])
    full_head = jnp.concatenate(quarters, 1)[:, :head_columns]

    class_row = grid_low
    vec = table[grid_low + 1 : grid_low + 11].astype(F32)
    pos_low = table[:low_rows].astype(F32)
    pos_high = dot(interp, table[:grid_low])
    row_low = jnp.arange(low_rows)[:, None]
    row_high = jnp.arange(high_rows)[:, None]
    class_add = table[class_row].astype(F32) + vec[9]
    add_low = jnp.where(
        row_low < grid_low, pos_low + vec[6], jnp.where(row_low == grid_low, class_add, 0.0)
    )
    pos_high = jnp.pad(pos_high, ((0, high_rows - grid_high), (0, 0)))
    add_high = jnp.where(
        row_high < grid_high, pos_high + vec[6], jnp.where(row_high == grid_high, class_add, 0.0)
    )
    added = jnp.concatenate([add_low, add_high], 0)
    is_patch = jnp.concatenate([row_low < grid_low, row_high < grid_high], 0)
    is_token = jnp.concatenate([row_low <= grid_low, row_high <= grid_high], 0)
    patches = jnp.concatenate(
        [
            jnp.pad(at(low_patches, side), ((0, low_rows - grid_low), (0, 0))),
            jnp.pad(at(high_patches, side), ((0, high_rows - grid_high), (0, 0))),
        ],
        0,
    )
    initial = dot(patches, full_patch) + added
    unit_one, scale_one = normalize(initial)
    normed = (unit_one * vec[0] + vec[1]).astype(BF)
    group_heads = 2 * qkv_width // (3 * HD)
    packed = dot(normed, full_qkv).astype(BF).reshape(tokens, group_heads, 3, HD)
    blend_low, logs_low, soft_low = attend(packed[:low_rows], grid_low + 1)
    blend_high, logs_high, soft_high = attend(packed[low_rows:], grid_high + 1)
    blended = jnp.concatenate([blend_low, blend_high], 0).reshape(tokens, group_heads * HD)
    middle = initial + vec[7] + pair_sum(dot(blended, full_out, 1, 1))
    unit_two, scale_two = normalize(middle)
    normed_two = (unit_two * vec[2] + vec[3]).astype(BF)
    upward = dot(normed_two, full_up)
    cumulative = 0.5 * (1.0 + lax.erf(upward * (0.5**0.5)))
    active = (upward * cumulative).astype(BF).astype(F32)
    slope = cumulative + upward * jnp.exp(-0.5 * upward * upward) * (2.0 * math.pi) ** (-0.5)

    def per_image(values):
        values = jnp.where(is_token, values, 0.0)
        return jnp.stack([jnp.sum(values[:low_rows], 0), jnp.sum(values[low_rows:], 0)])

    lengths = jnp.array([[grid_low + 1.0], [grid_high + 1.0]], F32)
    active_sums = per_image(active)
    active_means = active_sums / lengths
    means_high = active_means.astype(BF)
    means_low = (active_means - means_high.astype(F32)).astype(BF)
    down_parts = dot(jnp.concatenate([means_high, means_low]), full_down, 1, 1)
    down_part = down_parts[:2] + down_parts[2:]
    down_part = down_part + swap_core(down_part)
    pooled_own = per_image(middle) / lengths + vec[8] + down_part

    ids = jnp.stack([side, low_patches.shape[0] + side])
    tags = jnp.stack([labels[ids], partner[ids]], 1).astype(F32)
    sent = jnp.concatenate([pooled_own, jnp.pad(tags, ((0, 0), (0, 126)))], 1)
    both_sides = in_order(jnp.stack([sent, swap_side(sent)]), side, 1)
    everyone = gather_small(both_sides.transpose(1, 0, 2))
    images = batch_size * 4
    everyone = everyone.reshape(images, D + 128)
    pooled = everyone[:, :D]
    all_labels = everyone[:, D].astype(jnp.int32)
    all_partners = everyone[:, D + 1].astype(jnp.int32)
    unit_final, scale_final = normalize(pooled)
    features = (unit_final * vec[4] + vec[5]).astype(BF)
    outputs = dot(features, full_head)
    logits, projected = outputs[:, :CLS], outputs[:, CLS:]
    picked = jnp.arange(CLS)[None, :] == all_labels[:, None]
    logit_top = jnp.max(logits, -1, keepdims=True)
    logit_log = logit_top + jnp.log(jnp.sum(jnp.exp(logits - logit_top), -1, keepdims=True))
    class_total = jnp.sum(logit_log[:, 0] - jnp.sum(jnp.where(picked, logits, 0.0), -1))
    grad_logits = (jnp.exp(logits - logit_log) - picked.astype(F32)) * (1.0 / images)
    length_inverse = lax.rsqrt(jnp.sum(projected * projected, -1, keepdims=True) + 1e-06)
    embedded = (projected * length_inverse).astype(BF)
    similar = dot(embedded, embedded, 1, 1) / SOFTMAX_TEMP
    image_ids = jnp.arange(images, dtype=jnp.int32)
    masked = jnp.where(image_ids[:, None] == image_ids[None, :], -1e30, similar)
    similar_top = jnp.max(masked, -1, keepdims=True)
    similar_log = similar_top + jnp.log(jnp.sum(jnp.exp(masked - similar_top), -1, keepdims=True))
    target = image_ids[None, :] == all_partners[:, None]
    pair_total = jnp.sum(similar_log[:, 0] - jnp.sum(jnp.where(target, similar, 0.0), -1))
    count = pair_count[0].astype(F32)
    grad_similar = ((jnp.exp(masked - similar_log) - target.astype(F32)) / count).astype(BF)
    grad_embedded = (dot(grad_similar, embedded) + dot(grad_similar, embedded, 0, 0)) / SOFTMAX_TEMP
    grad_embedded = grad_embedded.astype(BF).astype(F32)
    grad_projected = length_inverse * grad_embedded - projected * (
        length_inverse**3 * jnp.sum(grad_embedded * projected, -1, keepdims=True)
    )
    grad_outputs = jnp.concatenate([grad_logits, grad_projected], 1).astype(BF)
    features_here = lax.dynamic_slice_in_dim(features, batch * rows_here, rows_here, 1)
    grad_head = dot(features_here, grad_outputs, 0, 0)
    grad_features = dot(grad_outputs, full_head, 1, 1)
    grad_pooled = normalize_back(grad_features, unit_final, scale_final, vec[4])
    complete_rows = jnp.stack(
        [
            jnp.sum(grad_features * unit_final, 0),
            jnp.sum(grad_features, 0),
            jnp.sum(grad_pooled, 0),
        ]
    )
    is_low = (image_ids % 4) < 2
    grad_token = grad_pooled / jnp.where(is_low, grid_low + 1.0, grid_high + 1.0)[:, None]
    own_rows = [batch * 4 + side, batch * 4 + 2 + side]
    grad_own = jnp.stack([at(grad_token, index) for index in own_rows])
    grad_own_low = grad_own.astype(BF)

    def spread(pair, mask):
        rows = jnp.concatenate(
            [
                jnp.broadcast_to(pair[0], (low_rows, pair.shape[1])),
                jnp.broadcast_to(pair[1], (high_rows, pair.shape[1])),
            ],
            0,
        )
        return jnp.where(mask, rows, 0.0)

    grad_active = dot(grad_own_low, full_down)
    grad_upward = (spread(grad_active, is_token) * slope).astype(BF)
    grad_up = dot(normed_two, grad_upward, 0, 0)
    grad_normed_two = pair_sum(dot(grad_upward, full_up, 1, 1))
    gain_two = jnp.sum(grad_normed_two * unit_two, 0)
    shift_two = jnp.sum(grad_normed_two, 0)
    grad_middle = normalize_back(grad_normed_two, unit_two, scale_two, vec[2])
    grad_middle = grad_middle + spread(grad_own, is_token)
    grad_middle_low = grad_middle.astype(BF)
    grad_out = dot(grad_middle_low, blended, 0, 0)
    grad_blend = dot(grad_middle_low, full_out).astype(BF).reshape(tokens, group_heads, HD)
    grad_packed = jnp.concatenate(
        [
            attend_back(packed[:low_rows], grid_low + 1, logs_low, soft_low, grad_blend[:low_rows]),
            attend_back(
                packed[low_rows:], grid_high + 1, logs_high, soft_high, grad_blend[low_rows:]
            ),
        ],
        0,
    ).reshape(tokens, 2 * qkv_width)
    grad_qkv = dot(normed, grad_packed, 0, 0)
    grad_normed = pair_sum(dot(grad_packed, full_qkv, 1, 1))
    gain_one = jnp.sum(grad_normed * unit_one, 0)
    shift_one = jnp.sum(grad_normed, 0)
    grad_initial = normalize_back(grad_normed, unit_one, scale_one, vec[0]) + grad_middle
    grad_embed = jnp.where(is_patch, grad_initial, 0.0)
    grad_embed_low = grad_embed.astype(BF)
    initial_low = grad_initial.astype(BF)
    grad_low_tokens = grad_initial[: grid_low + 1]
    from_high = dot(interp, initial_low[low_rows : low_rows + grid_high], 0, 0)
    class_high = grad_initial[low_rows + grid_high][None]
    zero_row = jnp.zeros((1, D), F32)
    class_both = grad_low_tokens[grid_low:] + class_high
    table_grad = jnp.concatenate(
        [
            grad_low_tokens[:grid_low] + from_high,
            class_both,
            gain_one[None],
            shift_one[None],
            gain_two[None],
            shift_two[None],
            zero_row,
            zero_row,
            jnp.sum(grad_embed, 0)[None],
            jnp.sum(grad_middle, 0)[None],
            zero_row,
            class_both,
            jnp.zeros((table_rows - grid_low - 11, D), F32),
        ],
        0,
    ).T

    def quarter_grads(index):
        columns = lax.dynamic_slice_in_dim(grad_embed_low, index * patch_width, patch_width, 1)
        return [
            dot(patches, columns, 0, 0),
            lax.dynamic_slice_in_dim(table_grad, index * extra_width, extra_width, 1),
        ]

    def group(values, width, index):
        return values[:, index * width : (index + 1) * width]

    reduced_up = reduce_rows(group(grad_up, hidden, 0), group(grad_up, hidden, 1))
    tails = [
        jnp.concatenate(
            [
                group(grad_qkv, qkv_width, index),
                group(grad_out, out_width, index),
            ]
            + quarter_grads(owner),
            1,
        )
        for index, owner in ((0, head), (1, head ^ 2))
    ]
    reduced_tail = reduce_rows(tails[0], tails[1])
    own_width = qkv_width + out_width
    reduced_qkv = reduced_tail[:, :qkv_width]
    reduced_out = reduced_tail[:, qkv_width:own_width]
    quarter = reduced_tail[:, own_width:].astype(BF)
    quarters = all_quarters(quarter, swap_side(quarter))
    reduced_patch = jnp.concatenate([part[:, :patch_width] for part in quarters], 1).astype(F32)
    reduced_table = (
        jnp.concatenate([part[:, patch_width:] for part in quarters], 1).T.astype(F32)
    )
    reduced_pos = jnp.concatenate(
        [reduced_table[grid_low : grid_low + 1], reduced_table[:grid_low]], 0
    )
    complete_here = lax.dynamic_slice_in_dim(complete_rows, batch * rows_here, rows_here, 1)
    partial_vec = reduced_table[grid_low + 1 : grid_low + 11]
    reduced_vec = jnp.concatenate(
        [partial_vec[:4], complete_here[:2], partial_vec[6:8], complete_here[2:], partial_vec[9:]],
        0,
    )
    side_sums = jnp.stack([active_sums[:, :hidden], swap_side(active_sums[:, hidden:])])
    all_sums = gather_small(in_order(side_sums, side, 1).transpose(1, 0, 2)).reshape(images, hidden)
    sums_high = all_sums.astype(BF)
    sums_low = (all_sums - sums_high.astype(F32)).astype(BF)
    grad_token_low = grad_token.astype(BF)
    full_grad_down = dot(
        jnp.concatenate([grad_token_low, grad_token_low]),
        jnp.concatenate([sums_high, sums_low]),
        0,
        0,
    )
    reduced_down = lax.dynamic_slice_in_dim(full_grad_down, batch * rows_here, rows_here, 0)

    muon_grads = (reduced_qkv, reduced_out, reduced_up, reduced_down)
    adam_grads = (reduced_patch, reduced_pos, reduced_vec, grad_head)
    squares = sum(jnp.sum(gradient * gradient) for gradient in muon_grads)
    squares = squares + sum(jnp.sum(gradient * gradient) for gradient in adam_grads) / head_size
    norm = jnp.sqrt(sum_everywhere(jnp.broadcast_to(squares, (8, 128)))[0, 0])
    factor = jnp.minimum(1.0, CLIP_NORM / norm)
    losses = jnp.stack([pair_total, class_total])
    adam_weights = (w_patch, pos_table, vectors, head_w)
    firsts = (first_patch, first_pos, first_vec, first_head)
    seconds = (second_patch, second_pos, second_vec, second_head)
    adam_new = [
        adam_update(
            adam_weights[index],
            factor * adam_grads[index],
            firsts[index],
            seconds[index],
            ADAM_RATES[index],
            ADAM_DECAYS[index],
        )
        for index in range(4)
    ]

    old_moments = (mom_qkv, mom_out, mom_up, mom_down)
    old_weights = (w_qkv, w_out, w_up, w_down)
    moments = [MOMENTUM * old_moments[index] + factor * muon_grads[index] for index in range(4)]
    held = jnp.concatenate(old_moments, 1).astype(BF)
    held, _ = lax.optimization_barrier((held, full_up))
    full_old = lax.all_gather(held, "batch", axis=0, tiled=True)
    sent = jnp.concatenate([reduced_qkv, reduced_out, reduced_up], 1).astype(BF)
    full_grads = lax.all_gather(sent, "batch", axis=0, tiled=True)
    starts = (0, qkv_width, own_width, own_width + hidden, own_width + 2 * hidden)
    full_moments = []
    for index in range(4):
        low, top = starts[index], starts[index + 1]
        gradient = full_grad_down if index == 3 else full_grads[:, low:top].astype(F32)
        full_moments.append(
            (MOMENTUM * full_old[:, low:top].astype(F32) + factor * gradient)
        )
    own_squares = jnp.stack([jnp.sum(moment * moment) for moment in full_moments])
    totals = sum_over_head(jnp.broadcast_to(own_squares[:, None], (4, 128)))[:, 0]
    moment_logs = jnp.log(totals)
    inverse = 1.0 / (jnp.sqrt(totals) + 1e-07)
    full_moments = [moment.astype(BF) for moment in full_moments]
    blocks = jnp.stack([gram_blocks(moment) for moment in full_moments])
    kept = jnp.stack([at(blocks, head), at(blocks, head ^ 2)])
    given = jnp.stack([at(blocks, head ^ 1), at(blocks, head ^ 3)])
    kept = kept + swap_core(given.astype(BF)).astype(F32)
    mine = kept[0] + swap_side(kept[1].astype(BF)).astype(F32)
    inverse_here = at(inverse, head)
    gram = whole_gram(mine * (inverse_here * inverse_here))
    row_start = batch * rows_here

    def fine(left, right):
        return jnp.dot(left, right, precision=lax.Precision.HIGH)

    eye = jnp.eye(D, dtype=F32)
    polynomials = []
    for sweep in range(NS_STEPS):
        last = sweep == NS_STEPS - 1
        if last:
            gram_rows = lax.dynamic_slice_in_dim(gram, row_start, rows_here, 0)
            eye_rows = lax.dynamic_slice_in_dim(eye, row_start, rows_here, 0)
            rows = (
                POLY_ONE * eye_rows + POLY_TWO * gram_rows + POLY_THREE * fine(gram_rows, gram)
            )
        else:
            factor_here = POLY_ONE * eye + POLY_TWO * gram + POLY_THREE * fine(gram, gram)
            polynomials.append(factor_here)
            gram = fine(fine(gram, factor_here), factor_here)
    for polynomial in polynomials[::-1]:
        rows = fine(rows, polynomial)
    rows = rows.astype(BF)
    pair = jnp.stack([rows, swap_side(rows)])
    four = jnp.concatenate([pair, swap_core(pair)])
    order = jnp.array((0, 2, 1, 3), jnp.int32)
    new_muon = []
    for index in range(4):
        weight = old_weights[index]
        scale = 0.2 * math.sqrt(max(D, weight.shape[1] * head_size))
        iterate = dot(at(four, order[head ^ index]), full_moments[index]) * inverse[index]
        new_muon.append(weight - MUON_RATE * (scale * iterate + DECAY_RATE * weight))
    return (
        adam_new[0][0],
        adam_new[1][0],
        adam_new[2][0],
        adam_new[3][0],
        new_muon[0],
        new_muon[1],
        new_muon[2],
        new_muon[3],
        moments[0],
        moments[1],
        moments[2],
        moments[3],
        adam_new[0][1],
        adam_new[1][1],
        adam_new[2][1],
        adam_new[3][1],
        adam_new[0][2],
        adam_new[1][2],
        adam_new[2][2],
        adam_new[3][2],
        losses,
        norm[None],
        moment_logs,
    )


def solution(mesh):
    placed = (
        P("batch", None, None),
        P("batch", None, None),
        P(),
        P("batch"),
        P("batch"),
        P(),
        P("batch", None),
        P(None, "batch"),
        P(None, "batch"),
        P("batch", None),
        P("batch", "head"),
        P("batch", "head"),
        P("batch", "head"),
        P("batch", "head"),
        P("batch", "head"),
        P("batch", "head"),
        P("batch", "head"),
        P("batch", "head"),
        P("batch", None),
        P("batch", None),
        P(None, "batch"),
        P(None, "batch"),
        P(None, "batch"),
        P(None, "batch"),
        P("batch", None),
        P("batch", None),
    )
    return jax.shard_map(
        body,
        mesh=mesh,
        in_specs=placed,
        out_specs=(
            P("batch", None),
            P(None, "batch"),
            P(None, "batch"),
            P("batch", None),
            P("batch", "head"),
            P("batch", "head"),
            P("batch", "head"),
            P("batch", "head"),
            P("batch", "head"),
            P("batch", "head"),
            P("batch", "head"),
            P("batch", "head"),
            P("batch", None),
            P(None, "batch"),
            P(None, "batch"),
            P("batch", None),
            P("batch", None),
            P(None, "batch"),
            P(None, "batch"),
            P("batch", None),
            P(),
            P(),
            P(),
        ),
        check_vma=False,
    )
```

```python
import math

import jax
import jax.numpy as jnp
from jax import lax
from jax.experimental import pallas as pl
from jax.experimental.pallas import tpu as pltpu
from jax.sharding import PartitionSpec as P

D = 768
HD = 64
CLS = 1000
NS_STEPS = 3
STEP = 10

POLY_ONE = 3.4445
POLY_TWO = -4.775
POLY_THREE = 2.0315
SOFTMAX_TEMP = 0.05
CLIP_NORM = 0.05
MOMENTUM = 0.95
MUON_RATE = 0.2
DECAY_RATE = 0.05
BETA_FIRST = 0.9
BETA_SECOND = 0.99
ADAM_FLOOR = 1e-08
ADAM_RATES = (0.08, 0.3, 0.5, 0.15)
ADAM_DECAYS = (0.05, 0.05, 0.0, 0.05)

BF = jnp.bfloat16
F32 = jnp.float32


def up_to(size, step):
    return -(-size // step) * step


def dot(left, right, left_dim=1, right_dim=0, precision=None):
    return lax.dot_general(
        left,
        right,
        (((left_dim,), (right_dim,)), ((), ())),
        precision=precision,
        preferred_element_type=F32,
    )


def at(stacked, index):
    return lax.dynamic_index_in_dim(stacked, index, 0, keepdims=False)


def swap(values, axis, mask):
    count = lax.axis_size(axis)
    return lax.ppermute(values, axis, [(index, index ^ mask) for index in range(count)])


def swap_core(values):
    return swap(values, "head", 1)


def swap_side(values):
    return swap(values, "head", 2)


def swap_x(values):
    return swap(values, "batch", 1)


def pair_sum(values):
    low = values.astype(BF)
    return low.astype(F32) + swap_core(low).astype(F32)


def place_kernel(splits, position, own, own_x, own_side, near, far, *outs):
    x = position[1]
    corner = jnp.where((position[0] ^ pl.program_id(0)) < 2, near[...], far[...])
    parts = ((own[...], x, 0), (own_x[...], 1 - x, 0), (own_side[...], x, 1), (corner, 1 - x, 1))
    for part, where, group in parts:
        start = 0
        for width, out in zip(splits, outs):
            out[0, pl.ds(where, 1), :, group * width : (group + 1) * width] = part[
                :, :, start : start + width
            ]
            start += width


def place(parts, splits):
    here = lax.axis_index("batch")
    position = jnp.stack([here // 2, here % 2]).astype(jnp.int32)
    _, rows, columns = parts[0].shape

    def block(pick_line):
        return pl.BlockSpec(
            (1, rows, columns), lambda step, spot: (pick_line(spot[0] ^ step), 0, 0)
        )

    whole = block(lambda line: line)
    near, far = block(lambda line: line & 1), block(lambda line: line & 1)
    outs = pl.pallas_call(
        lambda *refs: place_kernel(splits, *refs),
        grid_spec=pltpu.PrefetchScalarGridSpec(
            num_scalar_prefetch=1,
            grid=(4,),
            in_specs=[whole, whole, whole, near, far],
            out_specs=[
                pl.BlockSpec((1, 2, rows, 2 * width), lambda step, spot: (step, 0, 0, 0))
                for width in splits
            ],
        ),
        out_shape=[
            jax.ShapeDtypeStruct((4, 2, rows, 2 * width), parts[0].dtype) for width in splits
        ],
        compiler_params=pltpu.CompilerParams(vmem_limit_bytes=32 * 1024 * 1024),
    )(position, *parts)
    return [out.reshape(8 * rows, out.shape[-1]) for out in outs]


def tie(*values):
    return lax.optimization_barrier(values)


def gather_lines(shard):
    if lax.axis_size("batch") != 8:
        return lax.all_gather(shard, "batch", axis=0, tiled=True)
    return jnp.stack([shard] + [swap(shard, "batch", 2 * mask) for mask in (1, 2, 3)])


def gather_batch(lines):
    if lax.axis_size("batch") != 8:
        return lines
    here = lax.axis_index("batch")
    position = jnp.stack([here // 2, here % 2]).astype(jnp.int32)
    _, rows, columns = lines.shape

    def kernel(spot, own, own_x, out):
        out[0, pl.ds(spot[1], 1)] = own[...]
        out[0, pl.ds(1 - spot[1], 1)] = own_x[...]

    line = pl.BlockSpec((1, rows, columns), lambda step, spot: (spot[0] ^ step, 0, 0))
    out = pl.pallas_call(
        kernel,
        grid_spec=pltpu.PrefetchScalarGridSpec(
            num_scalar_prefetch=1,
            grid=(4,),
            in_specs=[line, line],
            out_specs=pl.BlockSpec((1, 2, rows, columns), lambda step, spot: (step, 0, 0, 0)),
        ),
        out_shape=jax.ShapeDtypeStruct((4, 2, rows, columns), lines.dtype),
        compiler_params=pltpu.CompilerParams(vmem_limit_bytes=32 * 1024 * 1024),
    )(position, lines, swap_x(lines))
    return out.reshape(8 * rows, columns)


def gather_planes(lines):
    if lax.axis_size("batch") != 8:
        return lines, swap_side(lines)
    return lines, swap_x(lines), swap_side(lines)


def gather_ends(planes):
    if lax.axis_size("batch") != 8:
        return ()
    return swap_side(planes[1][:2]), swap_x(planes[2][2:])


def gather_last(planes, ends, splits):
    if lax.axis_size("batch") != 8:
        own, other = planes
        outs, start = [], 0
        for width in splits:
            pair = [own[:, start : start + width], other[:, start : start + width]]
            outs.append(jnp.concatenate(pair, 1))
            start += width
        return outs
    return place([*planes, *ends], splits)


def pick(blocks, index, axis):
    return lax.dynamic_index_in_dim(blocks, index, axis, keepdims=False)


def reduce_start(own, other):
    count = lax.axis_size("batch")
    if count != 8:
        return own.astype(F32) + swap_side(other).astype(F32), own
    rows, columns = own.shape[0] // count, own.shape[1]
    half = rows // 2
    x = lax.axis_index("batch") % 2
    own = own.reshape(4, 2, rows, columns)
    other = other.reshape(4, 2, rows, columns)
    first = own[:, :, :half].astype(F32) + swap_side(other[:, :, :half]).astype(F32)
    second = jnp.stack([own[:, :, half:], other[:, :, half:]], 2)
    second = pick(second, x, 1).astype(F32) + swap_x(pick(second, 1 - x, 1)).astype(F32)
    return first, second


def reduce_middle(first, second):
    if lax.axis_size("batch") != 8:
        return first
    x = lax.axis_index("batch") % 2
    first = pick(first, x, 1) + swap_x(pick(first, 1 - x, 1).astype(BF)).astype(F32)
    second = second[:, 0] + swap_side(second[:, 1].astype(BF)).astype(F32)
    return jnp.concatenate([first, second], 1)


def reduce_end(both):
    if lax.axis_size("batch") != 8:
        return lax.psum_scatter(both, "batch", scatter_dimension=0, tiled=True)
    z = lax.axis_index("batch") // 2
    total = at(both, z)
    for mask in (1, 2, 3):
        total = total + swap(at(both, z ^ mask).astype(BF), "batch", 2 * mask).astype(F32)
    return total


def in_order(stacked, here, bits):
    tail = stacked.shape[1:]
    stacked = stacked.reshape((2,) * bits + tail)
    for bit in range(bits):
        axis = bits - 1 - bit
        flag = (here >> bit) % 2 == 1
        stacked = jnp.where(flag, jnp.flip(stacked, axis), stacked)
    return stacked.reshape((2**bits,) + tail)


def gather_small(values):
    count = lax.axis_size("batch")
    if count != 8:
        return lax.all_gather(values, "batch", axis=0, tiled=False)
    pair = jnp.stack([values, swap_x(values)])
    lines = jnp.stack([pair] + [swap(pair, "batch", 2 * mask) for mask in (1, 2, 3)])
    return in_order(lines.reshape((8,) + values.shape), lax.axis_index("batch"), 3)


def sum_everywhere(values):
    for axis in ("head", "batch"):
        mask = 1
        while mask < lax.axis_size(axis):
            values = values + swap(values, axis, mask)
            mask *= 2
    return values


def sum_over_head(values):
    mask = 1
    while mask < lax.axis_size("head"):
        values = values + swap(values, "head", mask)
        mask *= 2
    return values


def order_kernel(turned, position, mine, theirs, *outs):
    core, side = position[0], position[1]
    width = mine.shape[1] // 2
    plain = width - turned
    for index in range(4):
        same_core = core == index % 2
        same_side = side == index // 2
        kept = jnp.where(same_core, mine[:, :width], theirs[:, :width])
        other = jnp.where(same_core, mine[:, width:], theirs[:, width:])
        quarter = jnp.where(same_side, kept, other)
        outs[0][:, index * plain : (index + 1) * plain] = quarter[:, :plain]
        if turned:
            outs[1][index * turned : (index + 1) * turned, :] = (
                quarter[:, plain:].astype(F32).T.astype(BF)
            )


def all_quarters(mine, turned=0):
    head = lax.axis_index("head")
    theirs = swap_core(mine)
    rows, both = mine.shape
    shapes = [jax.ShapeDtypeStruct((rows, 2 * both - 4 * turned), BF)]
    if turned:
        shapes.append(jax.ShapeDtypeStruct((4 * turned, rows), BF))
    return pl.pallas_call(
        lambda *refs: order_kernel(turned, *refs),
        in_specs=[pl.BlockSpec(memory_space=pltpu.SMEM)]
        + [pl.BlockSpec(memory_space=pltpu.VMEM)] * 2,
        out_specs=[pl.BlockSpec(memory_space=pltpu.VMEM)] * len(shapes),
        out_shape=shapes,
        compiler_params=pltpu.CompilerParams(vmem_limit_bytes=32 * 1024 * 1024),
    )(jnp.stack([head % 2, head // 2]).astype(jnp.int32), mine, theirs)


def normalize(values):
    centred = values - jnp.mean(values, -1, keepdims=True)
    scale = lax.rsqrt(jnp.mean(centred * centred, -1, keepdims=True) + 1e-06)
    return centred * scale, scale


def normalize_back(grad, unit, scale, gain):
    grad_unit = grad * gain
    return scale * (
        grad_unit
        - jnp.mean(grad_unit, -1, keepdims=True)
        - unit * jnp.mean(grad_unit * unit, -1, keepdims=True)
    )


def soft_columns(keys, queries, length):
    scores = dot(keys, queries, 1, 1)
    places = lax.broadcasted_iota(jnp.int32, (keys.shape[0], 1), 0)
    scores = jnp.where(places < length, scores, -1e30)
    scores = jnp.exp(scores - jnp.max(scores, 0, keepdims=True))
    return scores * (1.0 / jnp.sum(scores, 0, keepdims=True))


def parts_of(packed, spans):
    for head in range(packed.shape[1] // (3 * HD)):
        base = head * 3 * HD
        for start, rows, length in spans:
            span = slice(start, start + rows)
            queries = packed[span, base : base + HD] * HD ** (-0.5)
            keys = packed[span, base + HD : base + 2 * HD]
            values = packed[span, base + 2 * HD : base + 3 * HD]
            yield head, base, span, length, queries, keys, values


def attend_kernel(spans, packed, out):
    for head, _, span, length, queries, keys, values in parts_of(packed, spans):
        soft = soft_columns(keys, queries, length).astype(BF)
        out[span, head * HD : (head + 1) * HD] = dot(values, soft, 0, 0).T.astype(BF)


def attend_back_kernel(spans, packed, grad, out):
    for head, base, span, length, queries, keys, values in parts_of(packed, spans):
        grads = grad[span, head * HD : (head + 1) * HD]
        soft = soft_columns(keys, queries, length)
        out[span, base + 2 * HD : base + 3 * HD] = dot(soft.astype(BF), grads).astype(BF)
        grad_soft = dot(values, grads, 1, 1)
        grad_scores = soft * (grad_soft - jnp.sum(soft * grad_soft, 0, keepdims=True))
        grad_scores = grad_scores.astype(BF)
        grad_queries = dot(keys, grad_scores, 0, 0).T * HD ** (-0.5)
        out[span, base : base + HD] = grad_queries.astype(BF)
        out[span, base + HD : base + 2 * HD] = dot(grad_scores, queries).astype(BF)


def attention(kernel, spans, packed, *grads):
    tokens, width = packed.shape
    wide = pl.BlockSpec((tokens, 6 * HD), lambda step: (0, step))
    narrow = pl.BlockSpec((tokens, 2 * HD), lambda step: (0, step))
    return pl.pallas_call(
        lambda *refs: kernel(spans, *refs),
        grid=(width // (6 * HD),),
        in_specs=[wide] + [narrow] * len(grads),
        out_specs=wide if grads else narrow,
        out_shape=jax.ShapeDtypeStruct((tokens, width if grads else width // 3), BF),
        compiler_params=pltpu.CompilerParams(vmem_limit_bytes=40 * 1024 * 1024),
    )(packed, *grads)


def adam_update(weight, gradient, first, second, rate, decay):
    first = BETA_FIRST * first + (1.0 - BETA_FIRST) * gradient
    second = BETA_SECOND * second + (1.0 - BETA_SECOND) * gradient * gradient
    direction = (
        first
        / (1.0 - BETA_FIRST**STEP)
        / (jnp.sqrt(second / (1.0 - BETA_SECOND**STEP)) + ADAM_FLOOR)
    )
    return (weight - rate * (direction + decay * weight), first, second)


def gram_blocks(matrix):
    step = D // 3
    rows = [matrix[index * step : (index + 1) * step] for index in range(3)]
    top = dot(rows[0], matrix, 1, 1)
    middle = dot(rows[1], matrix[step:], 1, 1)
    last = dot(rows[2], rows[2], 1, 1)
    return jnp.stack(
        [
            top[:, :step],
            top[:, step : 2 * step],
            top[:, 2 * step :],
            middle[:, :step],
            middle[:, step:],
            last,
        ]
    )


def whole_gram(blocks):
    aa, ab, ac, bb, bc, cc = [blocks[index] for index in range(6)]
    return jnp.concatenate(
        [
            jnp.concatenate([aa, ab, ac], 1),
            jnp.concatenate([ab.T, bb, bc], 1),
            jnp.concatenate([ac.T, bc.T, cc], 1),
        ],
        0,
    )


def body(
    low_patches,
    high_patches,
    interp,
    labels,
    partner,
    pair_count,
    w_patch,
    pos_table,
    vectors,
    head_w,
    w_qkv,
    w_out,
    w_up,
    w_down,
    mom_qkv,
    mom_out,
    mom_up,
    mom_down,
    first_patch,
    second_patch,
    first_pos,
    second_pos,
    first_vec,
    second_vec,
    first_head,
    second_head,
):
    batch = lax.axis_index("batch")
    head = lax.axis_index("head")
    side = head // 2
    batch_size = lax.axis_size("batch")
    head_size = lax.axis_size("head")
    rows_here = w_patch.shape[0]
    grid_low, grid_high = low_patches.shape[1], high_patches.shape[1]
    low_rows = up_to(grid_low + 1, 16)
    high_rows = up_to(grid_high + 1, 16)
    tokens = low_rows + high_rows
    qkv_width, out_width = w_qkv.shape[1], w_out.shape[1]
    hidden = w_up.shape[1]
    patch_width = D // head_size
    extra_width = 64
    head_columns = head_w.shape[1]
    head_padded = up_to(head_columns, 64 * head_size)
    head_width = head_padded // head_size
    table_rows = extra_width * head_size

    table = jnp.concatenate([pos_table[1:], pos_table[:1], vectors], 0).astype(BF)
    table = jnp.pad(table, ((0, table_rows - table.shape[0]), (0, 0))).T
    quarter_patch = lax.dynamic_slice_in_dim(w_patch, head * patch_width, patch_width, 1)
    quarter_table = lax.dynamic_slice_in_dim(table, head * extra_width, extra_width, 1)
    padded_head = jnp.pad(head_w.astype(BF), ((0, 0), (0, head_padded - head_columns)))
    quarter_head = lax.dynamic_slice_in_dim(padded_head, head * head_width, head_width, 1)
    small = patch_width + extra_width
    chunk_one = jnp.concatenate([quarter_patch.astype(BF), quarter_table, w_qkv.astype(BF)], 1)
    chunk_two = jnp.concatenate([w_out.astype(BF), w_up.astype(BF)], 1)
    chunk_three = jnp.concatenate([w_down.astype(BF), quarter_head], 1)
    lines = gather_lines(chunk_one)
    chunk_two, lines = tie(chunk_two, lines)
    planes = gather_planes(lines)
    lines_two = gather_lines(chunk_two)
    planes, lines_two = tie(planes, lines_two)
    ends = gather_ends(planes)
    planes_two = gather_planes(lines_two)
    both_small, full_qkv = gather_last(planes, ends, (small, qkv_width))
    full_patch, table = all_quarters(both_small, extra_width)
    chunk_three, full_patch = tie(chunk_three, full_patch)
    lines_three = gather_lines(chunk_three)

    class_row = grid_low
    vec = table[grid_low + 1 : grid_low + 11].astype(F32)
    pos_low = table[:low_rows].astype(F32)
    pos_high = dot(interp, table[:grid_low])
    row_low = jnp.arange(low_rows)[:, None]
    row_high = jnp.arange(high_rows)[:, None]
    class_add = table[class_row].astype(F32) + vec[9]
    add_low = jnp.where(
        row_low < grid_low, pos_low + vec[6], jnp.where(row_low == grid_low, class_add, 0.0)
    )
    pos_high = jnp.pad(pos_high, ((0, high_rows - grid_high), (0, 0)))
    add_high = jnp.where(
        row_high < grid_high, pos_high + vec[6], jnp.where(row_high == grid_high, class_add, 0.0)
    )
    added = jnp.concatenate([add_low, add_high], 0)
    is_patch = jnp.concatenate([row_low < grid_low, row_high < grid_high], 0)
    is_token = jnp.concatenate([row_low <= grid_low, row_high <= grid_high], 0)
    patches = jnp.concatenate(
        [
            jnp.pad(at(low_patches, side), ((0, low_rows - grid_low), (0, 0))),
            jnp.pad(at(high_patches, side), ((0, high_rows - grid_high), (0, 0))),
        ],
        0,
    )
    initial = dot(patches, full_patch) + added
    unit_one, scale_one = normalize(initial)
    normed = (unit_one * vec[0] + vec[1]).astype(BF)
    packed = dot(normed, full_qkv).astype(BF)
    packed, planes_two = tie(packed, planes_two)
    ends_two = gather_ends(planes_two)
    spans = ((0, low_rows, grid_low + 1), (low_rows, high_rows, grid_high + 1))
    blended = attention(attend_kernel, spans, packed)
    blended, ends_two, lines_three = tie(blended, ends_two, lines_three)
    planes_three = gather_planes(lines_three)
    full_out, full_up = gather_last(planes_two, ends_two, (out_width, hidden))
    middle = initial + vec[7] + pair_sum(dot(blended, full_out, 1, 1))
    unit_two, scale_two = normalize(middle)
    normed_two = (unit_two * vec[2] + vec[3]).astype(BF)
    upward = dot(normed_two, full_up)
    upward, planes_three = tie(upward, planes_three)
    ends_three = gather_ends(planes_three)
    full_down, both_head = gather_last(planes_three, ends_three, (hidden, head_width))
    (full_head,) = all_quarters(both_head)
    cumulative = 0.5 * (1.0 + lax.erf(upward * (0.5**0.5)))
    active = (upward * cumulative).astype(BF).astype(F32)
    slope = cumulative + upward * jnp.exp(-0.5 * upward * upward) * (2.0 * math.pi) ** (-0.5)

    def per_image(values):
        values = jnp.where(is_token, values, 0.0)
        return jnp.stack([jnp.sum(values[:low_rows], 0), jnp.sum(values[low_rows:], 0)])

    lengths = jnp.array([[grid_low + 1.0], [grid_high + 1.0]], F32)
    active_sums = per_image(active)
    active_means = active_sums / lengths
    means_high = active_means.astype(BF)
    means_low = (active_means - means_high.astype(F32)).astype(BF)
    down_parts = dot(jnp.concatenate([means_high, means_low]), full_down, 1, 1)
    down_part = down_parts[:2] + down_parts[2:]
    down_part = down_part + swap_core(down_part)
    pooled_own = per_image(middle) / lengths + vec[8] + down_part

    ids = jnp.stack([side, low_patches.shape[0] + side])
    own_labels, own_partners = labels[ids], partner[ids]
    tags = jnp.stack([own_labels // 8, own_labels % 8, own_partners // 8, own_partners % 8], 1)
    pooled_high = pooled_own.astype(BF)
    pooled_low = (pooled_own - pooled_high.astype(F32)).astype(BF)
    tags = jnp.pad(tags.astype(BF), ((0, 0), (0, 124)))
    common = jnp.concatenate([pooled_high, pooled_low, tags], 1)
    active_low = active_sums.astype(BF)
    came = swap_side(jnp.concatenate([common, active_low[:, hidden:]], 1))
    mine = jnp.concatenate([common, active_low[:, :hidden]], 1)
    both_sides = in_order(jnp.stack([mine, came]), side, 1)
    everyone = gather_small(both_sides.transpose(1, 0, 2))
    images = batch_size * 4
    everyone = everyone.reshape(images, 2 * D + 128 + hidden)
    pooled = everyone[:, :D].astype(F32) + everyone[:, D : 2 * D].astype(F32)
    all_tags = everyone[:, 2 * D : 2 * D + 4].astype(jnp.int32)
    all_labels = all_tags[:, 0] * 8 + all_tags[:, 1]
    all_partners = all_tags[:, 2] * 8 + all_tags[:, 3]
    all_sums = everyone[:, 2 * D + 128 :]
    unit_final, scale_final = normalize(pooled)
    features = (unit_final * vec[4] + vec[5]).astype(BF)
    outputs = dot(features, full_head)
    logits, projected = outputs[:, :CLS], outputs[:, CLS:head_columns]
    picked = jnp.arange(CLS)[None, :] == all_labels[:, None]
    logit_top = jnp.max(logits, -1, keepdims=True)
    logit_log = logit_top + jnp.log(jnp.sum(jnp.exp(logits - logit_top), -1, keepdims=True))
    class_total = jnp.sum(logit_log[:, 0] - jnp.sum(jnp.where(picked, logits, 0.0), -1))
    grad_logits = (jnp.exp(logits - logit_log) - picked.astype(F32)) * (1.0 / images)
    length_inverse = lax.rsqrt(jnp.sum(projected * projected, -1, keepdims=True) + 1e-06)
    embedded = (projected * length_inverse).astype(BF)
    similar = dot(embedded, embedded, 1, 1) / SOFTMAX_TEMP
    image_ids = jnp.arange(images, dtype=jnp.int32)
    masked = jnp.where(image_ids[:, None] == image_ids[None, :], -1e30, similar)
    similar_top = jnp.max(masked, -1, keepdims=True)
    similar_log = similar_top + jnp.log(jnp.sum(jnp.exp(masked - similar_top), -1, keepdims=True))
    target = image_ids[None, :] == all_partners[:, None]
    pair_total = jnp.sum(similar_log[:, 0] - jnp.sum(jnp.where(target, similar, 0.0), -1))
    count = pair_count[0].astype(F32)
    grad_similar = ((jnp.exp(masked - similar_log) - target.astype(F32)) / count).astype(BF)
    grad_embedded = (dot(grad_similar, embedded) + dot(grad_similar, embedded, 0, 0)) / SOFTMAX_TEMP
    grad_embedded = grad_embedded.astype(BF).astype(F32)
    grad_projected = length_inverse * grad_embedded - projected * (
        length_inverse**3 * jnp.sum(grad_embedded * projected, -1, keepdims=True)
    )
    grad_outputs = jnp.concatenate([grad_logits, grad_projected], 1).astype(BF)
    grad_outputs = jnp.pad(grad_outputs, ((0, 0), (0, head_padded - head_columns)))
    features_here = lax.dynamic_slice_in_dim(features, batch * rows_here, rows_here, 1)
    grad_head = dot(features_here, grad_outputs, 0, 0)[:, :head_columns]
    grad_features = dot(grad_outputs, full_head, 1, 1)
    grad_pooled = normalize_back(grad_features, unit_final, scale_final, vec[4])
    complete_rows = jnp.stack(
        [
            jnp.sum(grad_features * unit_final, 0),
            jnp.sum(grad_features, 0),
            jnp.sum(grad_pooled, 0),
        ]
    )
    is_low = (image_ids % 4) < 2
    grad_token = grad_pooled / jnp.where(is_low, grid_low + 1.0, grid_high + 1.0)[:, None]
    own_rows = [batch * 4 + side, batch * 4 + 2 + side]
    grad_own = jnp.stack([at(grad_token, index) for index in own_rows])
    grad_own_low = grad_own.astype(BF)

    def spread(pair, mask):
        rows = jnp.concatenate(
            [
                jnp.broadcast_to(pair[0], (low_rows, pair.shape[1])),
                jnp.broadcast_to(pair[1], (high_rows, pair.shape[1])),
            ],
            0,
        )
        return jnp.where(mask, rows, 0.0)

    held = jnp.concatenate([mom_qkv, mom_out, mom_up, mom_down], 1).astype(BF)
    held, _ = tie(held, full_down)
    full_old = lax.all_gather(held, "batch", axis=0, tiled=True)
    grad_active = dot(grad_own_low, full_down)
    grad_upward = (spread(grad_active, is_token) * slope).astype(BF)
    grad_up = dot(normed_two, grad_upward, 0, 0).astype(BF)
    sums_up = reduce_start(grad_up[:, :hidden], grad_up[:, hidden:])
    grad_normed_two = pair_sum(dot(grad_upward, full_up, 1, 1))
    gain_two = jnp.sum(grad_normed_two * unit_two, 0)
    shift_two = jnp.sum(grad_normed_two, 0)
    grad_middle = normalize_back(grad_normed_two, unit_two, scale_two, vec[2])
    grad_middle = grad_middle + spread(grad_own, is_token)
    grad_middle_low = grad_middle.astype(BF)
    grad_middle_low, sums_up = tie(grad_middle_low, sums_up)
    sums_up = reduce_middle(*sums_up)
    grad_out = dot(grad_middle_low, blended, 0, 0).astype(BF)
    grad_blend = dot(grad_middle_low, full_out).astype(BF)
    grad_packed = attention(attend_back_kernel, spans, packed, grad_blend)
    grad_packed, sums_up = tie(grad_packed, sums_up)
    reduced_up = reduce_end(sums_up)
    grad_qkv = dot(normed, grad_packed, 0, 0).astype(BF)
    tails = [
        jnp.concatenate(
            [
                grad_qkv[:, index * qkv_width : (index + 1) * qkv_width],
                grad_out[:, index * out_width : (index + 1) * out_width],
            ],
            1,
        )
        for index in range(2)
    ]
    sums_tail = reduce_start(*tails)
    grad_normed = pair_sum(dot(grad_packed, full_qkv, 1, 1))
    grad_normed, reduced_up, full_old = tie(grad_normed, reduced_up, full_old)
    full_grad_up = lax.all_gather(reduced_up.astype(BF), "batch", axis=0, tiled=True)
    gain_one = jnp.sum(grad_normed * unit_one, 0)
    shift_one = jnp.sum(grad_normed, 0)
    grad_initial = normalize_back(grad_normed, unit_one, scale_one, vec[0]) + grad_middle
    grad_embed = jnp.where(is_patch, grad_initial, 0.0)
    grad_embed_low = grad_embed.astype(BF)
    initial_low = grad_initial.astype(BF)
    grad_low_tokens = grad_initial[: grid_low + 1]
    from_high = dot(interp, initial_low[low_rows : low_rows + grid_high], 0, 0)
    class_high = grad_initial[low_rows + grid_high][None]
    zero_row = jnp.zeros((1, D), F32)
    class_both = grad_low_tokens[grid_low:] + class_high
    table_grad = jnp.concatenate(
        [
            grad_low_tokens[:grid_low] + from_high,
            class_both,
            gain_one[None],
            shift_one[None],
            gain_two[None],
            shift_two[None],
            zero_row,
            zero_row,
            jnp.sum(grad_embed, 0)[None],
            jnp.sum(grad_middle, 0)[None],
            zero_row,
            class_both,
            jnp.zeros((table_rows - grid_low - 11, D), F32),
        ],
        0,
    ).T

    table_grad = table_grad.astype(BF)

    def quarter_grads(index):
        columns = lax.dynamic_slice_in_dim(grad_embed_low, index * patch_width, patch_width, 1)
        quarter = lax.dynamic_slice_in_dim(table_grad, index * extra_width, extra_width, 1)
        return jnp.concatenate([dot(patches, columns, 0, 0).astype(BF), quarter], 1)

    sums_small = reduce_start(quarter_grads(head), quarter_grads(head ^ 2))
    sums_tail = [jnp.concatenate(pair, -1) for pair in zip(sums_tail, sums_small)]
    reduced_tail = reduce_end(reduce_middle(*sums_tail))
    own_width = qkv_width + out_width
    lines_tail = gather_lines(reduced_tail[:, :own_width].astype(BF))
    reduced_qkv = reduced_tail[:, :qkv_width]
    reduced_out = reduced_tail[:, qkv_width:own_width]
    quarter = reduced_tail[:, own_width:].astype(BF)
    reduced_patch, reduced_table = all_quarters(
        jnp.concatenate([quarter, swap_side(quarter)], 1), extra_width
    )
    reduced_patch, reduced_table = reduced_patch.astype(F32), reduced_table.astype(F32)
    reduced_pos = jnp.concatenate(
        [reduced_table[grid_low : grid_low + 1], reduced_table[:grid_low]], 0
    )
    complete_here = lax.dynamic_slice_in_dim(complete_rows, batch * rows_here, rows_here, 1)
    partial_vec = reduced_table[grid_low + 1 : grid_low + 11]
    reduced_vec = jnp.concatenate(
        [partial_vec[:4], complete_here[:2], partial_vec[6:8], complete_here[2:], partial_vec[9:]],
        0,
    )
    full_grad_down = dot(grad_token.astype(BF), all_sums, 0, 0)
    reduced_down = lax.dynamic_slice_in_dim(full_grad_down, batch * rows_here, rows_here, 0)

    muon_grads = (reduced_qkv, reduced_out, reduced_up, reduced_down)
    adam_grads = (reduced_patch, reduced_pos, reduced_vec, grad_head)
    squares = sum(jnp.sum(gradient * gradient) for gradient in muon_grads)
    squares = squares + sum(jnp.sum(gradient * gradient) for gradient in adam_grads) / head_size
    squares, lines_tail, full_grad_up = tie(squares, lines_tail, full_grad_up)
    full_tail = gather_batch(lines_tail)
    norm = jnp.sqrt(sum_everywhere(jnp.broadcast_to(squares, (8, 128)))[0, 0])
    factor = jnp.minimum(1.0, CLIP_NORM / norm)
    factor, full_tail = tie(factor, full_tail)
    losses = jnp.stack([pair_total, class_total])
    adam_weights = (w_patch, pos_table, vectors, head_w)
    firsts = (first_patch, first_pos, first_vec, first_head)
    seconds = (second_patch, second_pos, second_vec, second_head)
    adam_new = [
        adam_update(
            adam_weights[index],
            factor * adam_grads[index],
            firsts[index],
            seconds[index],
            ADAM_RATES[index],
            ADAM_DECAYS[index],
        )
        for index in range(4)
    ]

    old_moments = (mom_qkv, mom_out, mom_up, mom_down)
    old_weights = (w_qkv, w_out, w_up, w_down)
    moments = [MOMENTUM * old_moments[index] + factor * muon_grads[index] for index in range(4)]
    starts = (0, qkv_width, own_width, own_width + hidden, own_width + 2 * hidden)

    def full_moment(index, gradient):
        old = full_old[:, starts[index] : starts[index + 1]].astype(F32)
        return (MOMENTUM * old + factor * gradient.astype(F32)).astype(BF)

    gradients = (full_tail[:, :qkv_width], full_tail[:, qkv_width:], full_grad_up, full_grad_down)
    full_moments = [full_moment(index, gradients[index]) for index in range(4)]
    blocks = jnp.stack([gram_blocks(moment).astype(BF) for moment in full_moments])
    kept = jnp.stack([at(blocks, head), at(blocks, head ^ 2)])
    given = jnp.stack([at(blocks, head ^ 1), at(blocks, head ^ 3)])
    kept = kept.astype(F32) + swap_core(given).astype(F32)
    mine = kept[0] + swap_side(kept[1].astype(BF)).astype(F32)
    diagonal = jnp.arange(D // 3)[:, None] == jnp.arange(D // 3)[None, :]
    total_here = jnp.sum(jnp.where(diagonal, mine[0] + mine[3] + mine[5], 0.0))
    inverse_here = 1.0 / (jnp.sqrt(total_here) + 1e-07)
    slots = jnp.arange(8)[:, None] == head
    totals = sum_over_head(jnp.where(slots, jnp.broadcast_to(total_here, (8, 128)), 0.0))
    moment_logs = jnp.log(totals[:4, 0])
    gram = whole_gram(mine * (inverse_here * inverse_here))
    row_start = batch * rows_here

    def fine(left, right):
        return jnp.dot(left, right, precision=lax.Precision.DEFAULT)

    eye = jnp.eye(D, dtype=F32)
    polynomials = []
    for sweep in range(NS_STEPS):
        last = sweep == NS_STEPS - 1
        if last:
            gram_rows = lax.dynamic_slice_in_dim(gram, row_start, rows_here, 0)
            eye_rows = lax.dynamic_slice_in_dim(eye, row_start, rows_here, 0)
            rows = (
                POLY_ONE * eye_rows + POLY_TWO * gram_rows + POLY_THREE * fine(gram_rows, gram)
            )
        else:
            factor_here = POLY_ONE * eye + POLY_TWO * gram + POLY_THREE * fine(gram, gram)
            polynomials.append(factor_here)
            gram = fine(fine(gram, factor_here), factor_here)
    for polynomial in polynomials[::-1]:
        rows = fine(rows, polynomial)
    rows = (rows * inverse_here).astype(BF)
    pair = jnp.stack([rows, swap_side(rows)])
    four = jnp.concatenate([pair, swap_core(pair)])
    order = jnp.array((0, 2, 1, 3), jnp.int32)
    new_muon = []
    for index in range(4):
        weight = old_weights[index]
        scale = 0.2 * math.sqrt(max(D, weight.shape[1] * head_size))
        iterate = dot(at(four, order[head ^ index]), full_moments[index])
        new_muon.append(weight - MUON_RATE * (scale * iterate + DECAY_RATE * weight))
    return (
        adam_new[0][0],
        adam_new[1][0],
        adam_new[2][0],
        adam_new[3][0],
        new_muon[0],
        new_muon[1],
        new_muon[2],
        new_muon[3],
        moments[0],
        moments[1],
        moments[2],
        moments[3],
        adam_new[0][1],
        adam_new[1][1],
        adam_new[2][1],
        adam_new[3][1],
        adam_new[0][2],
        adam_new[1][2],
        adam_new[2][2],
        adam_new[3][2],
        losses,
        norm[None],
        moment_logs,
    )


def solution(mesh):
    placed = (
        P("batch", None, None),
        P("batch", None, None),
        P(),
        P("batch"),
        P("batch"),
        P(),
        P("batch", None),
        P(None, "batch"),
        P(None, "batch"),
        P("batch", None),
        P("batch", "head"),
        P("batch", "head"),
        P("batch", "head"),
        P("batch", "head"),
        P("batch", "head"),
        P("batch", "head"),
        P("batch", "head"),
        P("batch", "head"),
        P("batch", None),
        P("batch", None),
        P(None, "batch"),
        P(None, "batch"),
        P(None, "batch"),
        P(None, "batch"),
        P("batch", None),
        P("batch", None),
    )
    return jax.shard_map(
        body,
        mesh=mesh,
        in_specs=placed,
        out_specs=(
            P("batch", None),
            P(None, "batch"),
            P(None, "batch"),
            P("batch", None),
            P("batch", "head"),
            P("batch", "head"),
            P("batch", "head"),
            P("batch", "head"),
            P("batch", "head"),
            P("batch", "head"),
            P("batch", "head"),
            P("batch", "head"),
            P("batch", None),
            P(None, "batch"),
            P(None, "batch"),
            P("batch", None),
            P("batch", None),
            P(None, "batch"),
            P(None, "batch"),
            P("batch", None),
            P(),
            P(),
            P(),
        ),
        check_vma=False,
    )
```

```python
import math

import jax
import jax.numpy as jnp
from jax import lax
from jax.experimental import pallas as pl
from jax.experimental.pallas import tpu as pltpu
from jax.sharding import PartitionSpec as P

D = 768
HD = 64
CLS = 1000
NS_STEPS = 3
STEP = 10

POLY_ONE = 3.4445
POLY_TWO = -4.775
POLY_THREE = 2.0315
SOFTMAX_TEMP = 0.05
CLIP_NORM = 0.05
MOMENTUM = 0.95
MUON_RATE = 0.2
DECAY_RATE = 0.05
BETA_FIRST = 0.9
BETA_SECOND = 0.99
ADAM_FLOOR = 1e-08
ADAM_RATES = (0.08, 0.3, 0.5, 0.15)
ADAM_DECAYS = (0.05, 0.05, 0.0, 0.05)

BF = jnp.bfloat16
F32 = jnp.float32


def up_to(size, step):
    return -(-size // step) * step


def dot(left, right, left_dim=1, right_dim=0, precision=None):
    return lax.dot_general(
        left,
        right,
        (((left_dim,), (right_dim,)), ((), ())),
        precision=precision,
        preferred_element_type=F32,
    )


def at(stacked, index):
    return lax.dynamic_index_in_dim(stacked, index, 0, keepdims=False)


def swap(values, axis, mask):
    count = lax.axis_size(axis)
    return lax.ppermute(values, axis, [(index, index ^ mask) for index in range(count)])


def swap_core(values):
    return swap(values, "head", 1)


def swap_side(values):
    return swap(values, "head", 2)


def swap_x(values):
    return swap(values, "batch", 1)


def place_kernel(splits, position, own, own_x, own_side, near, far, *outs):
    x = position[1]
    corner = jnp.where((position[0] ^ pl.program_id(0)) < 2, near[...], far[...])
    parts = ((own[...], x, 0), (own_x[...], 1 - x, 0), (own_side[...], x, 1), (corner, 1 - x, 1))
    for part, where, group in parts:
        start = 0
        for width, out in zip(splits, outs):
            out[0, pl.ds(where, 1), :, group * width : (group + 1) * width] = part[
                :, :, start : start + width
            ]
            start += width


def place(parts, splits):
    here = lax.axis_index("batch")
    position = jnp.stack([here // 2, here % 2]).astype(jnp.int32)
    _, rows, columns = parts[0].shape

    def block(pick_line):
        return pl.BlockSpec(
            (1, rows, columns), lambda step, spot: (pick_line(spot[0] ^ step), 0, 0)
        )

    whole = block(lambda line: line)
    near, far = block(lambda line: line & 1), block(lambda line: line & 1)
    outs = pl.pallas_call(
        lambda *refs: place_kernel(splits, *refs),
        grid_spec=pltpu.PrefetchScalarGridSpec(
            num_scalar_prefetch=1,
            grid=(4,),
            in_specs=[whole, whole, whole, near, far],
            out_specs=[
                pl.BlockSpec((1, 2, rows, 2 * width), lambda step, spot: (step, 0, 0, 0))
                for width in splits
            ],
        ),
        out_shape=[
            jax.ShapeDtypeStruct((4, 2, rows, 2 * width), parts[0].dtype) for width in splits
        ],
        compiler_params=pltpu.CompilerParams(vmem_limit_bytes=32 * 1024 * 1024),
    )(position, *parts)
    return [out.reshape(8 * rows, out.shape[-1]) for out in outs]


def tie(*values):
    return lax.optimization_barrier(values)


def gather_lines(shard):
    if lax.axis_size("batch") != 8:
        return lax.all_gather(shard, "batch", axis=0, tiled=True)
    return jnp.stack([shard] + [swap(shard, "batch", 2 * mask) for mask in (1, 2, 3)])


def gather_batch(lines, lines_x):
    if lax.axis_size("batch") != 8:
        return lines
    here = lax.axis_index("batch")
    position = jnp.stack([here // 2, here % 2]).astype(jnp.int32)
    _, rows, columns = lines.shape

    def kernel(spot, own, own_x, out):
        out[0, pl.ds(spot[1], 1)] = own[...]
        out[0, pl.ds(1 - spot[1], 1)] = own_x[...]

    line = pl.BlockSpec((1, rows, columns), lambda step, spot: (spot[0] ^ step, 0, 0))
    out = pl.pallas_call(
        kernel,
        grid_spec=pltpu.PrefetchScalarGridSpec(
            num_scalar_prefetch=1,
            grid=(4,),
            in_specs=[line, line],
            out_specs=pl.BlockSpec((1, 2, rows, columns), lambda step, spot: (step, 0, 0, 0)),
        ),
        out_shape=jax.ShapeDtypeStruct((4, 2, rows, columns), lines.dtype),
        compiler_params=pltpu.CompilerParams(vmem_limit_bytes=32 * 1024 * 1024),
    )(position, lines, lines_x)
    return out.reshape(8 * rows, columns)


def gather_planes(lines):
    if lax.axis_size("batch") != 8:
        return lines, swap_side(lines)
    return lines, swap_x(lines), swap_side(lines)


def gather_ends(planes):
    if lax.axis_size("batch") != 8:
        return ()
    return swap_side(planes[1][:2]), swap_x(planes[2][2:])


def gather_last(planes, ends, splits):
    if lax.axis_size("batch") != 8:
        own, other = planes
        outs, start = [], 0
        for width in splits:
            pair = [own[:, start : start + width], other[:, start : start + width]]
            outs.append(jnp.concatenate(pair, 1))
            start += width
        return outs
    return place([*planes, *ends], splits)


def pick(blocks, index, axis):
    return lax.dynamic_index_in_dim(blocks, index, axis, keepdims=False)


def reduce_first(own, other):
    count = lax.axis_size("batch")
    if count != 8:
        return (own,), (swap_side(other),)
    rows, columns = own.shape[0] // count, own.shape[1]
    half = rows // 2
    x = lax.axis_index("batch") % 2
    own = own.reshape(4, 2, rows, columns)
    other = other.reshape(4, 2, rows, columns)
    kept = [pick(part[:, :, half:], x, 1) for part in (own, other)]
    sent = [pick(part[:, :, half:], 1 - x, 1) for part in (own, other)]
    came = swap_side(other[:, :, :half]), swap_x(jnp.stack(sent))
    return (own[:, :, :half], *kept), came


def reduce_second(kept, came):
    if lax.axis_size("batch") != 8:
        return (kept[0].astype(F32) + came[0].astype(F32),), ()
    x = lax.axis_index("batch") % 2
    first = kept[0].astype(F32) + came[0].astype(F32)
    second = kept[1].astype(F32) + came[1][0].astype(F32)
    sent = (kept[2].astype(F32) + came[1][1].astype(F32)).astype(BF)
    came = swap_x(pick(first, 1 - x, 1).astype(BF)), swap_side(sent)
    return (pick(first, x, 1), second), came


def reduce_third(kept, came):
    if lax.axis_size("batch") != 8:
        return (lax.psum_scatter(kept[0], "batch", scatter_dimension=0, tiled=True),), ()
    z = lax.axis_index("batch") // 2
    both = jnp.concatenate([part + got.astype(F32) for part, got in zip(kept, came)], 1)
    came = [swap(at(both, z ^ mask).astype(BF), "batch", 2 * mask) for mask in (1, 2, 3)]
    return (at(both, z),), came


def reduce_last(kept, came):
    total = kept[0]
    for got in came:
        total = total + got.astype(F32)
    return total


def in_order(stacked, here, bits):
    tail = stacked.shape[1:]
    stacked = stacked.reshape((2,) * bits + tail)
    for bit in range(bits):
        axis = bits - 1 - bit
        flag = (here >> bit) % 2 == 1
        stacked = jnp.where(flag, jnp.flip(stacked, axis), stacked)
    return stacked.reshape((2**bits,) + tail)


def gather_small(values):
    count = lax.axis_size("batch")
    if count != 8:
        return lax.all_gather(values, "batch", axis=0, tiled=False)
    pair = jnp.stack([values, swap_x(values)])
    lines = jnp.stack([pair] + [swap(pair, "batch", 2 * mask) for mask in (1, 2, 3)])
    return in_order(lines.reshape((8,) + values.shape), lax.axis_index("batch"), 3)


def sum_everywhere(values):
    for axis in ("head", "batch"):
        mask = 1
        while mask < lax.axis_size(axis):
            values = values + swap(values, axis, mask)
            mask *= 2
    return values


def sum_over_head(values):
    mask = 1
    while mask < lax.axis_size("head"):
        values = values + swap(values, "head", mask)
        mask *= 2
    return values


def order_kernel(turned, position, mine, theirs, *outs):
    core, side = position[0], position[1]
    width = mine.shape[1] // 2
    plain = width - turned
    for index in range(4):
        same_core = core == index % 2
        same_side = side == index // 2
        kept = jnp.where(same_core, mine[:, :width], theirs[:, :width])
        other = jnp.where(same_core, mine[:, width:], theirs[:, width:])
        quarter = jnp.where(same_side, kept, other)
        outs[0][:, index * plain : (index + 1) * plain] = quarter[:, :plain]
        if turned:
            outs[1][index * turned : (index + 1) * turned, :] = (
                quarter[:, plain:].astype(F32).T.astype(BF)
            )


def all_quarters(mine, turned=0, theirs=None):
    head = lax.axis_index("head")
    theirs = swap_core(mine) if theirs is None else theirs
    rows, both = mine.shape
    shapes = [jax.ShapeDtypeStruct((rows, 2 * both - 4 * turned), BF)]
    if turned:
        shapes.append(jax.ShapeDtypeStruct((4 * turned, rows), BF))
    return pl.pallas_call(
        lambda *refs: order_kernel(turned, *refs),
        in_specs=[pl.BlockSpec(memory_space=pltpu.SMEM)]
        + [pl.BlockSpec(memory_space=pltpu.VMEM)] * 2,
        out_specs=[pl.BlockSpec(memory_space=pltpu.VMEM)] * len(shapes),
        out_shape=shapes,
        compiler_params=pltpu.CompilerParams(vmem_limit_bytes=32 * 1024 * 1024),
    )(jnp.stack([head % 2, head // 2]).astype(jnp.int32), mine, theirs)


def normalize(values):
    centred = values - jnp.mean(values, -1, keepdims=True)
    scale = lax.rsqrt(jnp.mean(centred * centred, -1, keepdims=True) + 1e-06)
    return centred * scale, scale


def normalize_back(grad, unit, scale, gain):
    grad_unit = grad * gain
    return scale * (
        grad_unit
        - jnp.mean(grad_unit, -1, keepdims=True)
        - unit * jnp.mean(grad_unit * unit, -1, keepdims=True)
    )


def soft_columns(keys, queries, length):
    scores = dot(keys, queries, 1, 1)
    places = lax.broadcasted_iota(jnp.int32, (keys.shape[0], 1), 0)
    scores = jnp.where(places < length, scores, -1e30)
    scores = jnp.exp(scores - jnp.max(scores, 0, keepdims=True))
    return scores * (1.0 / jnp.sum(scores, 0, keepdims=True))


def parts_of(packed, spans):
    for head in range(packed.shape[1] // (3 * HD)):
        base = head * 3 * HD
        for start, rows, length in spans:
            span = slice(start, start + rows)
            queries = packed[span, base : base + HD] * HD ** (-0.5)
            keys = packed[span, base + HD : base + 2 * HD]
            values = packed[span, base + 2 * HD : base + 3 * HD]
            yield head, base, span, length, queries, keys, values


def attend_kernel(spans, packed, out):
    for head, _, span, length, queries, keys, values in parts_of(packed, spans):
        soft = soft_columns(keys, queries, length).astype(BF)
        out[span, head * HD : (head + 1) * HD] = dot(values, soft, 0, 0).T.astype(BF)


def attend_back_kernel(spans, packed, grad, out):
    for head, base, span, length, queries, keys, values in parts_of(packed, spans):
        grads = grad[span, head * HD : (head + 1) * HD]
        soft = soft_columns(keys, queries, length)
        out[span, base + 2 * HD : base + 3 * HD] = dot(soft.astype(BF), grads).astype(BF)
        grad_soft = dot(values, grads, 1, 1)
        grad_scores = soft * (grad_soft - jnp.sum(soft * grad_soft, 0, keepdims=True))
        grad_scores = grad_scores.astype(BF)
        grad_queries = dot(keys, grad_scores, 0, 0).T * HD ** (-0.5)
        out[span, base : base + HD] = grad_queries.astype(BF)
        out[span, base + HD : base + 2 * HD] = dot(grad_scores, queries).astype(BF)


def attention(kernel, spans, packed, *grads):
    tokens, width = packed.shape
    wide = pl.BlockSpec((tokens, 6 * HD), lambda step: (0, step))
    narrow = pl.BlockSpec((tokens, 2 * HD), lambda step: (0, step))
    return pl.pallas_call(
        lambda *refs: kernel(spans, *refs),
        grid=(width // (6 * HD),),
        in_specs=[wide] + [narrow] * len(grads),
        out_specs=wide if grads else narrow,
        out_shape=jax.ShapeDtypeStruct((tokens, width if grads else width // 3), BF),
        compiler_params=pltpu.CompilerParams(vmem_limit_bytes=40 * 1024 * 1024),
    )(packed, *grads)


def row_kind(first, rows, spans):
    places = first + lax.broadcasted_iota(jnp.int32, (rows, 1), 0)
    return [(places >= start) & (places < start + length) for start, _, length in spans]


def row_grid(kernel, spans, inputs, rows, tables, outs):
    tokens, width = inputs[0].shape

    def body(*refs):
        first = pl.program_id(0) * rows
        kinds = row_kind(first, rows, spans)
        sums = refs[-1]

        @pl.when(pl.program_id(0) == 0)
        def _():
            sums[...] = jnp.zeros_like(sums)

        kernel(first, kinds, *refs)

    block = pl.BlockSpec((rows, width), lambda step: (step, 0))
    return pl.pallas_call(
        body,
        grid=(tokens // rows,),
        in_specs=[block] * len(inputs)
        + [pl.BlockSpec(table.shape, lambda step: (0, 0)) for table in tables],
        out_specs=[block] * len(outs) + [pl.BlockSpec((8, width), lambda step: (0, 0))],
        out_shape=[jax.ShapeDtypeStruct((tokens, width), kind) for kind in outs]
        + [jax.ShapeDtypeStruct((8, width), F32)],
        compiler_params=pltpu.CompilerParams(vmem_limit_bytes=32 * 1024 * 1024),
    )(*inputs, *tables)


def add_row(sums, index, values):
    sums[index : index + 1, :] += jnp.sum(values, 0, keepdims=True)


def middle_kernel(first, kinds, initial, mine, theirs, vec, middle, normed, sums):
    branch = mine[...].astype(F32) + theirs[...].astype(F32)
    values = initial[...] + vec[7:8, :] + branch
    unit, _ = normalize(values)
    middle[...] = values
    normed[...] = (unit * vec[2:3, :] + vec[3:4, :]).astype(BF)
    for index, kind in enumerate(kinds):
        add_row(sums, index, jnp.where(kind, values, 0.0))


def middle_back_kernel(first, kinds, middle, mine, theirs, vec, rows, out, sums):
    grad = mine[...].astype(F32) + theirs[...].astype(F32)
    unit, scale = normalize(middle[...])
    back = normalize_back(grad, unit, scale, vec[2:3, :])
    back = back + jnp.where(kinds[0], rows[0:1, :], jnp.where(kinds[1], rows[1:2, :], 0.0))
    out[...] = back.astype(BF)
    add_row(sums, 0, grad * unit)
    add_row(sums, 1, grad)
    add_row(sums, 2, back)


def initial_back_kernel(spans, first, kinds, initial, mine, theirs, middle, vec, out, sums):
    grad = mine[...].astype(F32) + theirs[...].astype(F32)
    unit, scale = normalize(initial[...])
    back = normalize_back(grad, unit, scale, vec[0:1, :]) + middle[...].astype(F32)
    out[...] = back.astype(BF)
    places = first + lax.broadcasted_iota(jnp.int32, (back.shape[0], 1), 0)
    is_class = (places == spans[0][0] + spans[0][2] - 1) | (places == spans[1][0] + spans[1][2] - 1)
    of_class = jnp.where(is_class, back, 0.0)
    add_row(sums, 0, grad * unit)
    add_row(sums, 1, grad)
    add_row(sums, 2, jnp.where(kinds[0] | kinds[1], back, 0.0) - of_class)
    add_row(sums, 3, of_class)


def hidden_kernel(spans, normed, weight, slope, sums):
    upward = dot(normed[...], weight[...])
    cumulative = 0.5 * (1.0 + lax.erf(upward * (0.5**0.5)))
    bell = jnp.exp(-0.5 * upward * upward) * (2.0 * math.pi) ** (-0.5)
    slope[...] = (cumulative + upward * bell).astype(BF)
    active = (upward * cumulative).astype(BF).astype(F32)
    sums[...] = jnp.zeros_like(sums)
    for index, (start, _, length) in enumerate(spans):
        rows = up_to(length, 16)
        part = active[start : start + rows]
        kept = lax.broadcasted_iota(jnp.int32, (rows, 1), 0) < length
        sums[index : index + 1, :] = jnp.sum(jnp.where(kept, part, 0.0), 0, keepdims=True)


def hidden_layer(spans, normed, weight):
    tokens, width = normed.shape
    columns = weight.shape[1]
    step = 256
    return pl.pallas_call(
        lambda *refs: hidden_kernel(spans, *refs),
        grid=(columns // step,),
        in_specs=[
            pl.BlockSpec((tokens, width), lambda index: (0, 0)),
            pl.BlockSpec((width, step), lambda index: (0, index)),
        ],
        out_specs=[
            pl.BlockSpec((tokens, step), lambda index: (0, index)),
            pl.BlockSpec((8, step), lambda index: (0, index)),
        ],
        out_shape=[
            jax.ShapeDtypeStruct((tokens, columns), BF),
            jax.ShapeDtypeStruct((8, columns), F32),
        ],
        compiler_params=pltpu.CompilerParams(vmem_limit_bytes=40 * 1024 * 1024),
    )(normed, weight)


def iterate_kernel(start, blocks, rows_out, total_out):
    step = D // 3
    rows = rows_out.shape[0]
    same = lax.broadcasted_iota(jnp.int32, (step, step), 0) == lax.broadcasted_iota(
        jnp.int32, (step, step), 1
    )
    total = jnp.sum(jnp.where(same, blocks[0] + blocks[3] + blocks[5], 0.0))
    inverse = 1.0 / (jnp.sqrt(jnp.full((1, 1), total, F32)) + 1e-07)
    total_out[...] = jnp.full(total_out.shape, total, F32)
    aa, ab, ac, bb, bc, cc = [blocks[index] * (inverse * inverse) for index in range(6)]
    gram = jnp.concatenate(
        [
            jnp.concatenate([aa, ab, ac], 1),
            jnp.concatenate([ab.T, bb, bc], 1),
            jnp.concatenate([ac.T, bc.T, cc], 1),
        ],
        0,
    )
    eye = (
        lax.broadcasted_iota(jnp.int32, (D, D), 0) == lax.broadcasted_iota(jnp.int32, (D, D), 1)
    ).astype(F32)
    chosen = (
        lax.broadcasted_iota(jnp.int32, (rows, D), 0) + start[0]
        == lax.broadcasted_iota(jnp.int32, (rows, D), 1)
    ).astype(F32)
    polynomials = []
    for _ in range(NS_STEPS - 1):
        low = gram.astype(BF)
        polynomial = POLY_ONE * eye + POLY_TWO * gram + POLY_THREE * dot(low, low)
        polynomial = polynomial.astype(BF)
        polynomials.append(polynomial)
        gram = dot(dot(low, polynomial).astype(BF), polynomial)
    low = gram.astype(BF)
    gram_rows = dot(chosen.astype(BF), low)
    out = POLY_ONE * chosen + POLY_TWO * gram_rows + POLY_THREE * dot(gram_rows.astype(BF), low)
    for polynomial in polynomials[::-1]:
        out = dot(out.astype(BF), polynomial)
    rows_out[...] = (out * inverse).astype(BF)


def iterate_gram(start, blocks, rows):
    return pl.pallas_call(
        iterate_kernel,
        in_specs=[
            pl.BlockSpec(memory_space=pltpu.SMEM),
            pl.BlockSpec(memory_space=pltpu.VMEM),
        ],
        out_specs=[pl.BlockSpec(memory_space=pltpu.VMEM)] * 2,
        out_shape=[
            jax.ShapeDtypeStruct((rows, D), BF),
            jax.ShapeDtypeStruct((8, 128), F32),
        ],
        compiler_params=pltpu.CompilerParams(vmem_limit_bytes=48 * 1024 * 1024),
    )(jnp.reshape(start, (1,)).astype(jnp.int32), blocks)


def adam_update(weight, gradient, first, second, rate, decay):
    first = BETA_FIRST * first + (1.0 - BETA_FIRST) * gradient
    second = BETA_SECOND * second + (1.0 - BETA_SECOND) * gradient * gradient
    direction = (
        first
        / (1.0 - BETA_FIRST**STEP)
        / (jnp.sqrt(second / (1.0 - BETA_SECOND**STEP)) + ADAM_FLOOR)
    )
    return (weight - rate * (direction + decay * weight), first, second)


def moment_kernel(pieces, count, factor, *refs):
    olds, grads, moments = (refs[index * count : (index + 1) * count] for index in range(3))
    blocks = refs[-1]
    step = D // 3
    place = 0
    for old, grad, moment in zip(olds, grads, moments):
        before = old[...].astype(F32)
        moment[...] = (MOMENTUM * before + factor[0] * grad[...].astype(F32)).astype(BF)
        for low, top in pieces:
            matrix = moment[:, low:top]
            for row, column in ((0, 0), (0, 1), (0, 2), (1, 1), (1, 2), (2, 2)):
                left = matrix[row * step : (row + 1) * step]
                right = matrix[column * step : (column + 1) * step]
                blocks[place // 6, place % 6] = dot(left, right, 1, 1).astype(BF)
                place += 1


def moment_grams(factor, old, block, grads, pieces):
    count, rows = len(grads), old.shape[0]
    width = grads[0].shape[1]
    whole = pl.BlockSpec((rows, width), lambda step: (0, 0))
    olds = [
        pl.BlockSpec((rows, width), lambda step, index=block + place: (0, index))
        for place in range(count)
    ]
    shape = (count * len(pieces), 6, D // 3, D // 3)
    *moments, blocks = pl.pallas_call(
        lambda *refs: moment_kernel(pieces, count, *refs),
        grid=(1,),
        in_specs=[pl.BlockSpec(memory_space=pltpu.SMEM)] + olds + [whole] * count,
        out_specs=[whole] * count + [pl.BlockSpec(shape, lambda step: (0, 0, 0, 0))],
        out_shape=[jax.ShapeDtypeStruct((rows, width), BF)] * count
        + [jax.ShapeDtypeStruct(shape, BF)],
        compiler_params=pltpu.CompilerParams(vmem_limit_bytes=56 * 1024 * 1024),
    )(jnp.reshape(factor, (1,)), *[old] * count, *grads)
    return moments, blocks


def body(
    low_patches,
    high_patches,
    interp,
    labels,
    partner,
    pair_count,
    w_patch,
    pos_table,
    vectors,
    head_w,
    w_qkv,
    w_out,
    w_up,
    w_down,
    mom_qkv,
    mom_out,
    mom_up,
    mom_down,
    first_patch,
    second_patch,
    first_pos,
    second_pos,
    first_vec,
    second_vec,
    first_head,
    second_head,
):
    batch = lax.axis_index("batch")
    head = lax.axis_index("head")
    side = head // 2
    batch_size = lax.axis_size("batch")
    head_size = lax.axis_size("head")
    rows_here = w_patch.shape[0]
    grid_low, grid_high = low_patches.shape[1], high_patches.shape[1]
    low_rows = up_to(grid_low + 1, 16)
    high_rows = up_to(grid_high + 1, 16)
    tokens = low_rows + high_rows
    qkv_width, out_width = w_qkv.shape[1], w_out.shape[1]
    hidden = w_up.shape[1]
    patch_width = D // head_size
    extra_width = 64
    head_columns = head_w.shape[1]
    head_padded = up_to(head_columns, 64 * head_size)
    head_width = head_padded // head_size
    table_rows = extra_width * head_size

    table = jnp.concatenate([pos_table[1:], pos_table[:1], vectors], 0).astype(BF)
    table = jnp.pad(table, ((0, table_rows - table.shape[0]), (0, 0))).T
    quarter_patch = lax.dynamic_slice_in_dim(w_patch, head * patch_width, patch_width, 1)
    quarter_table = lax.dynamic_slice_in_dim(table, head * extra_width, extra_width, 1)
    padded_head = jnp.pad(head_w.astype(BF), ((0, 0), (0, head_padded - head_columns)))
    quarter_head = lax.dynamic_slice_in_dim(padded_head, head * head_width, head_width, 1)
    small = patch_width + extra_width
    chunk_one = jnp.concatenate([quarter_patch.astype(BF), quarter_table, w_qkv.astype(BF)], 1)
    chunk_two = jnp.concatenate([w_out.astype(BF), w_up.astype(BF)], 1)
    chunk_three = jnp.concatenate([w_down.astype(BF), quarter_head], 1)
    lines = gather_lines(chunk_one)
    chunk_two, lines = tie(chunk_two, lines)
    planes = gather_planes(lines)
    lines_two = gather_lines(chunk_two)
    planes, lines_two = tie(planes, lines_two)
    ends = gather_ends(planes)
    planes_two = gather_planes(lines_two)
    both_small, full_qkv = gather_last(planes, ends, (small, qkv_width))
    full_patch, table = all_quarters(both_small, extra_width)
    chunk_three, full_patch = tie(chunk_three, full_patch)
    lines_three = gather_lines(chunk_three)

    class_row = grid_low
    vec = table[grid_low + 1 : grid_low + 11].astype(F32)
    pos_low = table[:low_rows].astype(F32)
    pos_high = dot(interp, table[:grid_low])
    row_low = jnp.arange(low_rows)[:, None]
    row_high = jnp.arange(high_rows)[:, None]
    class_add = table[class_row].astype(F32) + vec[9]
    add_low = jnp.where(
        row_low < grid_low, pos_low + vec[6], jnp.where(row_low == grid_low, class_add, 0.0)
    )
    pos_high = jnp.pad(pos_high, ((0, high_rows - grid_high), (0, 0)))
    add_high = jnp.where(
        row_high < grid_high, pos_high + vec[6], jnp.where(row_high == grid_high, class_add, 0.0)
    )
    added = jnp.concatenate([add_low, add_high], 0)
    is_patch = jnp.concatenate([row_low < grid_low, row_high < grid_high], 0)
    is_token = jnp.concatenate([row_low <= grid_low, row_high <= grid_high], 0)
    patches = jnp.concatenate(
        [
            jnp.pad(at(low_patches, side), ((0, low_rows - grid_low), (0, 0))),
            jnp.pad(at(high_patches, side), ((0, high_rows - grid_high), (0, 0))),
        ],
        0,
    )
    initial = dot(patches, full_patch) + added
    unit_one, _ = normalize(initial)
    normed = (unit_one * vec[0] + vec[1]).astype(BF)
    packed = dot(normed, full_qkv).astype(BF)
    packed, planes_two, lines_three = tie(packed, planes_two, lines_three)
    ends_two = gather_ends(planes_two)
    planes_three = gather_planes(lines_three)
    spans = ((0, low_rows, grid_low + 1), (low_rows, high_rows, grid_high + 1))
    blended = attention(attend_kernel, spans, packed)
    full_out, full_up = gather_last(planes_two, ends_two, (out_width, hidden))
    branch = dot(blended, full_out, 1, 1).astype(BF)
    block_rows = 160
    middle, normed_two, middle_sums = row_grid(
        middle_kernel, spans, (initial, branch, swap_core(branch)), block_rows, (vec,), (F32, BF)
    )
    held = jnp.concatenate([mom_qkv, mom_out, mom_up, mom_down], 1).astype(BF)
    held, normed_two, planes_three = tie(held, normed_two, planes_three)
    full_old = lax.all_gather(held, "batch", axis=0, tiled=True)
    ends_three = gather_ends(planes_three)
    slope, active_sums = hidden_layer(spans, normed_two, full_up)
    active_sums = active_sums[:2]
    full_down, both_head = gather_last(planes_three, ends_three, (hidden, head_width))
    (full_head,) = all_quarters(both_head)

    lengths = jnp.array([[grid_low + 1.0], [grid_high + 1.0]], F32)
    active_means = active_sums / lengths
    means_high = active_means.astype(BF)
    means_low = (active_means - means_high.astype(F32)).astype(BF)
    down_parts = dot(jnp.concatenate([means_high, means_low]), full_down, 1, 1)
    down_part = down_parts[:2] + down_parts[2:]
    down_part = down_part + swap_core(down_part)
    pooled_own = middle_sums[:2] / lengths + vec[8] + down_part

    ids = jnp.stack([side, low_patches.shape[0] + side])
    own_labels, own_partners = labels[ids], partner[ids]
    tags = jnp.stack([own_labels // 8, own_labels % 8, own_partners // 8, own_partners % 8], 1)
    pooled_high = pooled_own.astype(BF)
    pooled_low = (pooled_own - pooled_high.astype(F32)).astype(BF)
    tags = jnp.pad(tags.astype(BF), ((0, 0), (0, 124)))
    common = jnp.concatenate([pooled_high, pooled_low, tags], 1)
    active_low = active_sums.astype(BF)
    came = swap_side(jnp.concatenate([common, active_low[:, hidden:]], 1))
    came, full_head = tie(came, full_head)
    mine = jnp.concatenate([common, active_low[:, :hidden]], 1)
    both_sides = in_order(jnp.stack([mine, came]), side, 1)
    everyone = gather_small(both_sides.transpose(1, 0, 2))
    images = batch_size * 4
    everyone = everyone.reshape(images, 2 * D + 128 + hidden)
    pooled = everyone[:, :D].astype(F32) + everyone[:, D : 2 * D].astype(F32)
    all_tags = everyone[:, 2 * D : 2 * D + 4].astype(jnp.int32)
    all_labels = all_tags[:, 0] * 8 + all_tags[:, 1]
    all_partners = all_tags[:, 2] * 8 + all_tags[:, 3]
    all_sums = everyone[:, 2 * D + 128 :]
    unit_final, scale_final = normalize(pooled)
    features = (unit_final * vec[4] + vec[5]).astype(BF)
    outputs = dot(features, full_head)
    logits, projected = outputs[:, :CLS], outputs[:, CLS:head_columns]
    picked = jnp.arange(CLS)[None, :] == all_labels[:, None]
    logit_top = jnp.max(logits, -1, keepdims=True)
    logit_log = logit_top + jnp.log(jnp.sum(jnp.exp(logits - logit_top), -1, keepdims=True))
    class_total = jnp.sum(logit_log[:, 0] - jnp.sum(jnp.where(picked, logits, 0.0), -1))
    grad_logits = (jnp.exp(logits - logit_log) - picked.astype(F32)) * (1.0 / images)
    length_inverse = lax.rsqrt(jnp.sum(projected * projected, -1, keepdims=True) + 1e-06)
    embedded = (projected * length_inverse).astype(BF)
    similar = dot(embedded, embedded, 1, 1) / SOFTMAX_TEMP
    image_ids = jnp.arange(images, dtype=jnp.int32)
    masked = jnp.where(image_ids[:, None] == image_ids[None, :], -1e30, similar)
    similar_top = jnp.max(masked, -1, keepdims=True)
    similar_log = similar_top + jnp.log(jnp.sum(jnp.exp(masked - similar_top), -1, keepdims=True))
    target = image_ids[None, :] == all_partners[:, None]
    pair_total = jnp.sum(similar_log[:, 0] - jnp.sum(jnp.where(target, similar, 0.0), -1))
    count = pair_count[0].astype(F32)
    grad_similar = ((jnp.exp(masked - similar_log) - target.astype(F32)) / count).astype(BF)
    grad_embedded = (dot(grad_similar, embedded) + dot(grad_similar, embedded, 0, 0)) / SOFTMAX_TEMP
    grad_embedded = grad_embedded.astype(BF).astype(F32)
    grad_projected = length_inverse * grad_embedded - projected * (
        length_inverse**3 * jnp.sum(grad_embedded * projected, -1, keepdims=True)
    )
    grad_outputs = jnp.concatenate([grad_logits, grad_projected], 1).astype(BF)
    grad_outputs = jnp.pad(grad_outputs, ((0, 0), (0, head_padded - head_columns)))
    features_here = lax.dynamic_slice_in_dim(features, batch * rows_here, rows_here, 1)
    grad_head = dot(features_here, grad_outputs, 0, 0)[:, :head_columns]
    grad_features = dot(grad_outputs, full_head, 1, 1)
    grad_pooled = normalize_back(grad_features, unit_final, scale_final, vec[4])
    complete_rows = jnp.stack(
        [
            jnp.sum(grad_features * unit_final, 0),
            jnp.sum(grad_features, 0),
            jnp.sum(grad_pooled, 0),
        ]
    )
    is_low = (image_ids % 4) < 2
    grad_token = grad_pooled / jnp.where(is_low, grid_low + 1.0, grid_high + 1.0)[:, None]
    own_rows = [batch * 4 + side, batch * 4 + 2 + side]
    grad_own = jnp.stack([at(grad_token, index) for index in own_rows])
    grad_own_low = grad_own.astype(BF)

    def spread(pair, mask):
        rows = jnp.concatenate(
            [
                jnp.broadcast_to(pair[0], (low_rows, pair.shape[1])),
                jnp.broadcast_to(pair[1], (high_rows, pair.shape[1])),
            ],
            0,
        )
        return jnp.where(mask, rows, 0.0)

    grad_active = dot(grad_own_low, full_down)
    grad_upward = (spread(grad_active, is_token) * slope.astype(F32)).astype(BF)
    grad_normed_two = dot(grad_upward, full_up, 1, 1).astype(BF)
    grad_up = dot(normed_two, grad_upward, 0, 0).astype(BF)
    kept_up, came_up = reduce_first(grad_up[:, :hidden], grad_up[:, hidden:])
    grad_middle, middle_row_sums = row_grid(
        middle_back_kernel,
        spans,
        (middle, grad_normed_two, swap_core(grad_normed_two)),
        block_rows,
        (vec, jnp.pad(grad_own, ((0, 6), (0, 0)))),
        (BF,),
    )
    grad_blend = dot(grad_middle, full_out).astype(BF)
    grad_out = dot(grad_middle, blended, 0, 0).astype(BF)
    grad_packed = attention(attend_back_kernel, spans, packed, grad_blend)
    grad_packed, came_up = tie(grad_packed, came_up)
    kept_up, came_up = reduce_second(kept_up, came_up)
    grad_normed = dot(grad_packed, full_qkv, 1, 1).astype(BF)
    grad_qkv = dot(normed, grad_packed, 0, 0).astype(BF)
    tails = [
        jnp.concatenate(
            [
                grad_qkv[:, index * qkv_width : (index + 1) * qkv_width],
                grad_out[:, index * out_width : (index + 1) * out_width],
            ],
            1,
        )
        for index in range(2)
    ]
    kept_tail, came_tail = reduce_first(*tails)
    grad_initial, initial_row_sums = row_grid(
        lambda *refs: initial_back_kernel(spans, *refs),
        spans,
        (initial, grad_normed, swap_core(grad_normed), grad_middle),
        block_rows,
        (vec,),
        (BF,),
    )
    grad_initial, came_up, full_old = tie(grad_initial, came_up, full_old)
    kept_up, came_up = reduce_third(kept_up, came_up)
    from_high = dot(interp, grad_initial[low_rows : low_rows + grid_high], 0, 0)
    zero_row = jnp.zeros((1, D), F32)
    class_both = initial_row_sums[3:4]
    table_grad = jnp.concatenate(
        [
            grad_initial[:grid_low].astype(F32) + from_high,
            class_both,
            initial_row_sums[:2],
            middle_row_sums[:2],
            zero_row,
            zero_row,
            initial_row_sums[2:3],
            middle_row_sums[2:3],
            zero_row,
            class_both,
            jnp.zeros((table_rows - grid_low - 11, D), F32),
        ],
        0,
    )
    table_grad = table_grad.astype(BF).T

    def quarter_grads(index):
        columns = lax.dynamic_slice_in_dim(grad_initial, index * patch_width, patch_width, 1)
        quarter = lax.dynamic_slice_in_dim(table_grad, index * extra_width, extra_width, 1)
        return jnp.concatenate([dot(patches, columns, 0, 0).astype(BF), quarter], 1)

    kept_small, came_small = reduce_first(quarter_grads(head), quarter_grads(head ^ 2))
    came_small, came_tail = tie(came_small, came_tail)

    def beside(left, right):
        return [jnp.concatenate(pair, -1) for pair in zip(left, right)]

    kept_tail, came_tail = reduce_second(
        beside(kept_tail, kept_small), beside(came_tail, came_small)
    )
    came_tail, came_up = tie(came_tail, came_up)
    reduced_up = reduce_last(kept_up, came_up)
    full_grad_up = lax.all_gather(reduced_up.astype(BF), "batch", axis=0, tiled=True)
    kept_tail, came_tail = reduce_third(kept_tail, came_tail)
    reduced_tail = reduce_last(kept_tail, came_tail)
    own_width = qkv_width + out_width
    lines_tail = gather_lines(reduced_tail[:, :own_width].astype(BF))
    reduced_qkv = reduced_tail[:, :qkv_width]
    reduced_out = reduced_tail[:, qkv_width:own_width]
    full_grad_down = dot(grad_token.astype(BF), all_sums, 0, 0)
    reduced_down = lax.dynamic_slice_in_dim(full_grad_down, batch * rows_here, rows_here, 0)

    quarter = reduced_tail[:, own_width:]
    complete_here = lax.dynamic_slice_in_dim(complete_rows, batch * rows_here, rows_here, 1)
    muon_grads = (reduced_qkv, reduced_out, reduced_up, reduced_down)
    squares = sum(jnp.sum(gradient * gradient) for gradient in (*muon_grads, quarter))
    same = jnp.sum(grad_head * grad_head) + jnp.sum(complete_here * complete_here)
    squares = jnp.broadcast_to(squares + same / head_size, (8, 128))
    for axis, mask in (("head", 1), ("head", 2), ("batch", 1)):
        squares = squares + swap(squares, axis, mask)
    quarter = quarter.astype(BF)
    quarters = jnp.concatenate([quarter, swap_side(quarter)], 1)
    partner_quarters = swap_core(quarters)
    squares, lines_tail, partner_quarters = tie(squares, lines_tail, partner_quarters)
    tail_x = swap_x(lines_tail) if batch_size == 8 else lines_tail
    mask = 2
    while mask < batch_size:
        squares = squares + swap(squares, "batch", mask)
        mask *= 2
    norm = jnp.sqrt(squares[0, 0])
    factor = jnp.minimum(1.0, CLIP_NORM / norm)
    factor, full_grad_up = tie(factor, full_grad_up)
    losses = jnp.stack([pair_total, class_total])
    old_moments = (mom_qkv, mom_out, mom_up, mom_down)
    old_weights = (w_qkv, w_out, w_up, w_down)
    owned = (0, 2, 1, 3)
    starts = (0, qkv_width, own_width)
    moments = [MOMENTUM * old_moments[index] + factor * muon_grads[index] for index in range(4)]
    new_head = adam_update(
        head_w, factor * grad_head, first_head, second_head, ADAM_RATES[3], ADAM_DECAYS[3]
    )
    (moment_up, moment_down), pair = moment_grams(
        factor, full_old, 1, (full_grad_up, full_grad_down), ((0, hidden),)
    )
    pair, tail_x = tie(pair, tail_x)
    full_tail = gather_batch(lines_tail, tail_x)

    def to_owner(pair, core):
        count = lax.axis_size("head")
        there = [(index, index ^ 1) for index in range(count) if index % 2 != core]
        pair = pair.astype(F32) + lax.ppermute(pair, "head", there).astype(F32)
        across = [(index, index ^ 2) for index in range(count) if index % 2 == core]
        sent = at(pair, 1 - side).astype(BF)
        return at(pair, side), lax.ppermute(sent, "head", across)

    early, came_early = to_owner(pair, 1)
    full_tail, early, moments, new_head = tie(full_tail, early, moments, new_head)
    (moment_tail,), pair = moment_grams(
        factor, full_old, 0, (full_tail,), ((0, qkv_width), (qkv_width, own_width))
    )
    late, came_late = to_owner(pair, 0)
    late, late_factor, quarters, firsts, seconds, adam_weights = tie(
        late,
        factor,
        quarters,
        (first_patch, first_pos, first_vec),
        (second_patch, second_pos, second_vec),
        (w_patch, pos_table, vectors),
    )
    reduced_patch, reduced_table = all_quarters(quarters, extra_width, partner_quarters)
    reduced_patch, reduced_table = reduced_patch.astype(F32), reduced_table.astype(F32)
    reduced_pos = jnp.concatenate(
        [reduced_table[grid_low : grid_low + 1], reduced_table[:grid_low]], 0
    )
    partial_vec = reduced_table[grid_low + 1 : grid_low + 11]
    reduced_vec = jnp.concatenate(
        [partial_vec[:4], complete_here[:2], partial_vec[6:8], complete_here[2:], partial_vec[9:]],
        0,
    )
    adam_grads = (reduced_patch, reduced_pos, reduced_vec)
    adam_new = [
        adam_update(
            adam_weights[index],
            late_factor * adam_grads[index],
            firsts[index],
            seconds[index],
            ADAM_RATES[index],
            ADAM_DECAYS[index],
        )
        for index in range(3)
    ]
    adam_new.append(new_head)
    mine = jnp.where(
        head % 2 == 0, late + came_late.astype(F32), early + came_early.astype(F32)
    )
    rows, total_here = iterate_gram(batch * rows_here, mine, rows_here)
    slots = jnp.arange(8)[:, None] == jnp.array(owned, jnp.int32)[head]
    totals = sum_over_head(jnp.where(slots, total_here, 0.0))
    moment_logs = jnp.log(totals[:4, 0])
    pair = jnp.stack([rows, swap_side(rows)])
    four = jnp.concatenate([pair, swap_core(pair)])
    order = jnp.array((0, 2, 1, 3), jnp.int32)
    parts = (moment_tail[:, :qkv_width], moment_tail[:, qkv_width:], moment_up, moment_down)
    new_muon = []
    for index in range(4):
        weight = old_weights[index]
        scale = 0.2 * math.sqrt(max(D, weight.shape[1] * head_size))
        iterate = dot(at(four, order[head ^ owned.index(index)]), parts[index])
        new_muon.append(weight - MUON_RATE * (scale * iterate + DECAY_RATE * weight))
    return (
        adam_new[0][0],
        adam_new[1][0],
        adam_new[2][0],
        adam_new[3][0],
        new_muon[0],
        new_muon[1],
        new_muon[2],
        new_muon[3],
        moments[0],
        moments[1],
        moments[2],
        moments[3],
        adam_new[0][1],
        adam_new[1][1],
        adam_new[2][1],
        adam_new[3][1],
        adam_new[0][2],
        adam_new[1][2],
        adam_new[2][2],
        adam_new[3][2],
        losses,
        norm[None],
        moment_logs,
    )


def solution(mesh):
    placed = (
        P("batch", None, None),
        P("batch", None, None),
        P(),
        P("batch"),
        P("batch"),
        P(),
        P("batch", None),
        P(None, "batch"),
        P(None, "batch"),
        P("batch", None),
        P("batch", "head"),
        P("batch", "head"),
        P("batch", "head"),
        P("batch", "head"),
        P("batch", "head"),
        P("batch", "head"),
        P("batch", "head"),
        P("batch", "head"),
        P("batch", None),
        P("batch", None),
        P(None, "batch"),
        P(None, "batch"),
        P(None, "batch"),
        P(None, "batch"),
        P("batch", None),
        P("batch", None),
    )
    return jax.shard_map(
        body,
        mesh=mesh,
        in_specs=placed,
        out_specs=(
            P("batch", None),
            P(None, "batch"),
            P(None, "batch"),
            P("batch", None),
            P("batch", "head"),
            P("batch", "head"),
            P("batch", "head"),
            P("batch", "head"),
            P("batch", "head"),
            P("batch", "head"),
            P("batch", "head"),
            P("batch", "head"),
            P("batch", None),
            P(None, "batch"),
            P(None, "batch"),
            P("batch", None),
            P("batch", None),
            P(None, "batch"),
            P(None, "batch"),
            P("batch", None),
            P(),
            P(),
            P(),
        ),
        check_vma=False,
    )
```

```python
import math

import jax
import jax.numpy as jnp
from jax import lax
from jax.experimental import pallas as pl
from jax.experimental.pallas import tpu as pltpu
from jax.sharding import PartitionSpec as P

D = 768
HD = 64
CLS = 1000
NS_STEPS = 3
STEP = 10

POLY_ONE = 3.4445
POLY_TWO = -4.775
POLY_THREE = 2.0315
SOFTMAX_TEMP = 0.05
CLIP_NORM = 0.05
MOMENTUM = 0.95
MUON_RATE = 0.2
DECAY_RATE = 0.05
BETA_FIRST = 0.9
BETA_SECOND = 0.99
ADAM_FLOOR = 1e-08
ADAM_RATES = (0.08, 0.3, 0.5, 0.15)
ADAM_DECAYS = (0.05, 0.05, 0.0, 0.05)

BF = jnp.bfloat16
F32 = jnp.float32


def up_to(size, step):
    return -(-size // step) * step


def dot(left, right, left_dim=1, right_dim=0, precision=None):
    return lax.dot_general(
        left,
        right,
        (((left_dim,), (right_dim,)), ((), ())),
        precision=precision,
        preferred_element_type=F32,
    )


def at(stacked, index):
    return lax.dynamic_index_in_dim(stacked, index, 0, keepdims=False)


def swap(values, axis, mask):
    count = lax.axis_size(axis)
    return lax.ppermute(values, axis, [(index, index ^ mask) for index in range(count)])


def swap_core(values):
    return swap(values, "head", 1)


def swap_side(values):
    return swap(values, "head", 2)


def swap_x(values):
    return swap(values, "batch", 1)


def place_kernel(splits, position, own, own_x, own_side, near, far, *outs):
    x = position[1]
    corner = jnp.where((position[0] ^ pl.program_id(0)) < 2, near[...], far[...])
    parts = ((own[...], x, 0), (own_x[...], 1 - x, 0), (own_side[...], x, 1), (corner, 1 - x, 1))
    for part, where, group in parts:
        start = 0
        for width, out in zip(splits, outs):
            out[0, pl.ds(where, 1), :, group * width : (group + 1) * width] = part[
                :, :, start : start + width
            ]
            start += width


def place(parts, splits):
    here = lax.axis_index("batch")
    position = jnp.stack([here // 2, here % 2]).astype(jnp.int32)
    _, rows, columns = parts[0].shape

    def block(pick_line):
        return pl.BlockSpec(
            (1, rows, columns), lambda step, spot: (pick_line(spot[0] ^ step), 0, 0)
        )

    whole = block(lambda line: line)
    near, far = block(lambda line: line & 1), block(lambda line: line & 1)
    outs = pl.pallas_call(
        lambda *refs: place_kernel(splits, *refs),
        grid_spec=pltpu.PrefetchScalarGridSpec(
            num_scalar_prefetch=1,
            grid=(4,),
            in_specs=[whole, whole, whole, near, far],
            out_specs=[
                pl.BlockSpec((1, 2, rows, 2 * width), lambda step, spot: (step, 0, 0, 0))
                for width in splits
            ],
        ),
        out_shape=[
            jax.ShapeDtypeStruct((4, 2, rows, 2 * width), parts[0].dtype) for width in splits
        ],
        compiler_params=pltpu.CompilerParams(vmem_limit_bytes=32 * 1024 * 1024),
    )(position, *parts)
    return [out.reshape(8 * rows, out.shape[-1]) for out in outs]


def tie(*values):
    return lax.optimization_barrier(values)


def gather_lines(shard):
    if lax.axis_size("batch") != 8:
        return lax.all_gather(shard, "batch", axis=0, tiled=True)
    return jnp.stack([shard] + [swap(shard, "batch", 2 * mask) for mask in (1, 2, 3)])


def gather_batch(lines, lines_x):
    if lax.axis_size("batch") != 8:
        return lines
    here = lax.axis_index("batch")
    position = jnp.stack([here // 2, here % 2]).astype(jnp.int32)
    _, rows, columns = lines.shape

    def kernel(spot, own, own_x, out):
        out[0, pl.ds(spot[1], 1)] = own[...]
        out[0, pl.ds(1 - spot[1], 1)] = own_x[...]

    line = pl.BlockSpec((1, rows, columns), lambda step, spot: (spot[0] ^ step, 0, 0))
    out = pl.pallas_call(
        kernel,
        grid_spec=pltpu.PrefetchScalarGridSpec(
            num_scalar_prefetch=1,
            grid=(4,),
            in_specs=[line, line],
            out_specs=pl.BlockSpec((1, 2, rows, columns), lambda step, spot: (step, 0, 0, 0)),
        ),
        out_shape=jax.ShapeDtypeStruct((4, 2, rows, columns), lines.dtype),
        compiler_params=pltpu.CompilerParams(vmem_limit_bytes=32 * 1024 * 1024),
    )(position, lines, lines_x)
    return out.reshape(8 * rows, columns)


def gather_planes(lines):
    if lax.axis_size("batch") != 8:
        return lines, swap_side(lines)
    return lines, swap_x(lines), swap_side(lines)


def gather_ends(planes):
    if lax.axis_size("batch") != 8:
        return ()
    return swap_side(planes[1][:2]), swap_x(planes[2][2:])


def gather_last(planes, ends, splits):
    if lax.axis_size("batch") != 8:
        own, other = planes
        outs, start = [], 0
        for width in splits:
            pair = [own[:, start : start + width], other[:, start : start + width]]
            outs.append(jnp.concatenate(pair, 1))
            start += width
        return outs
    return place([*planes, *ends], splits)


def swapped(index):
    return (index % 2) * 2 + index // 2


def pick(blocks, index, axis):
    return lax.dynamic_index_in_dim(blocks, index, axis, keepdims=False)


def reduce_first(own, other):
    count = lax.axis_size("batch")
    if count != 8:
        return (own,), (swap_side(other),)
    rows, columns = own.shape[0] // count, own.shape[1]
    half = rows // 2
    x = lax.axis_index("batch") % 2
    own = own.reshape(4, 2, rows, columns)
    other = other.reshape(4, 2, rows, columns)
    kept = [pick(part[:, :, half:], x, 1) for part in (own, other)]
    sent = [pick(part[:, :, half:], 1 - x, 1) for part in (own, other)]
    came = swap_side(other[:, :, :half]), swap_x(jnp.stack(sent))
    return (own[:, :, :half], *kept), came


def reduce_second(kept, came):
    if lax.axis_size("batch") != 8:
        return (kept[0].astype(F32) + came[0].astype(F32),), ()
    x = lax.axis_index("batch") % 2
    first = kept[0].astype(F32) + came[0].astype(F32)
    second = kept[1].astype(F32) + came[1][0].astype(F32)
    sent = (kept[2].astype(F32) + came[1][1].astype(F32)).astype(BF)
    came = swap_x(pick(first, 1 - x, 1).astype(BF)), swap_side(sent)
    return (pick(first, x, 1), second), came


def reduce_third(kept, came):
    if lax.axis_size("batch") != 8:
        return (lax.psum_scatter(kept[0], "batch", scatter_dimension=0, tiled=True),), ()
    z = lax.axis_index("batch") // 2
    both = jnp.concatenate([part + got.astype(F32) for part, got in zip(kept, came)], 1)
    came = [swap(at(both, z ^ mask).astype(BF), "batch", 2 * mask) for mask in (1, 2, 3)]
    return (at(both, z),), came


def reduce_last(kept, came):
    total = kept[0]
    for got in came:
        total = total + got.astype(F32)
    return total


def reduce_line(kept, came, step):
    if lax.axis_size("batch") != 8:
        return reduce_second(kept, came) if step == 1 else reduce_third(kept, came)
    total = kept[0].astype(F32) + came[0].astype(F32)
    here = lax.axis_index("batch")
    if step == 1:
        total = total.reshape(4, 2, -1, total.shape[-1])
        sent = pick(total, 1 - here % 2, 1).astype(BF)
        return (pick(total, here % 2, 1),), (swap_x(sent),)
    z = here // 2
    came = [swap(at(total, z ^ mask).astype(BF), "batch", 2 * mask) for mask in (1, 2, 3)]
    return (at(total, z),), came


def in_order(stacked, here, bits):
    tail = stacked.shape[1:]
    stacked = stacked.reshape((2,) * bits + tail)
    for bit in range(bits):
        axis = bits - 1 - bit
        flag = (here >> bit) % 2 == 1
        stacked = jnp.where(flag, jnp.flip(stacked, axis), stacked)
    return stacked.reshape((2**bits,) + tail)


def gather_small(values):
    count = lax.axis_size("batch")
    if count != 8:
        return lax.all_gather(values, "batch", axis=0, tiled=False)
    pair = jnp.stack([values, swap_x(values)])
    lines = jnp.stack([pair] + [swap(pair, "batch", 2 * mask) for mask in (1, 2, 3)])
    return in_order(lines.reshape((8,) + values.shape), lax.axis_index("batch"), 3)


def sum_everywhere(values):
    for axis in ("head", "batch"):
        mask = 1
        while mask < lax.axis_size(axis):
            values = values + swap(values, axis, mask)
            mask *= 2
    return values


def sum_over_head(values):
    mask = 1
    while mask < lax.axis_size("head"):
        values = values + swap(values, "head", mask)
        mask *= 2
    return values


def order_kernel(turned, turn, position, mine, theirs, *outs):
    core, side = position[0], position[1]
    width = mine.shape[1] // 2
    plain = width - turned
    for index in range(4):
        same_core = core == index % 2
        same_side = side == index // 2
        kept = jnp.where(same_core, mine[:, :width], theirs[:, :width])
        other = jnp.where(same_core, mine[:, width:], theirs[:, width:])
        quarter = jnp.where(same_side, kept, other)
        outs[0][:, index * plain : (index + 1) * plain] = quarter[:, :plain]
        if turned and not turn:
            outs[1][:, index * turned : (index + 1) * turned] = quarter[:, plain:]
        elif turned:
            outs[1][index * turned : (index + 1) * turned, :] = (
                quarter[:, plain:].astype(F32).T.astype(BF)
            )


def all_quarters(mine, turned=0, theirs=None, turn=True):
    head = lax.axis_index("head")
    theirs = swap_core(mine) if theirs is None else theirs
    rows, both = mine.shape
    shapes = [jax.ShapeDtypeStruct((rows, 2 * both - 4 * turned), BF)]
    if turned:
        shapes.append(jax.ShapeDtypeStruct((4 * turned, rows) if turn else (rows, 4 * turned), BF))
    return pl.pallas_call(
        lambda *refs: order_kernel(turned, turn, *refs),
        in_specs=[pl.BlockSpec(memory_space=pltpu.SMEM)]
        + [pl.BlockSpec(memory_space=pltpu.VMEM)] * 2,
        out_specs=[pl.BlockSpec(memory_space=pltpu.VMEM)] * len(shapes),
        out_shape=shapes,
        compiler_params=pltpu.CompilerParams(vmem_limit_bytes=32 * 1024 * 1024),
    )(jnp.stack([head % 2, head // 2]).astype(jnp.int32), mine, theirs)


def normalize(values):
    centred = values - jnp.mean(values, -1, keepdims=True)
    scale = lax.rsqrt(jnp.mean(centred * centred, -1, keepdims=True) + 1e-06)
    return centred * scale, scale


def normalize_back(grad, unit, scale, gain):
    grad_unit = grad * gain
    return scale * (
        grad_unit
        - jnp.mean(grad_unit, -1, keepdims=True)
        - unit * jnp.mean(grad_unit * unit, -1, keepdims=True)
    )


def soft_columns(keys, queries, length):
    scores = dot(keys, queries, 1, 1)
    places = lax.broadcasted_iota(jnp.int32, (keys.shape[0], 1), 0)
    scores = jnp.where(places < length, scores, -1e30)
    scores = jnp.exp(scores - jnp.max(scores, 0, keepdims=True))
    return scores * (1.0 / jnp.sum(scores, 0, keepdims=True))


def parts_of(packed, spans):
    for head in range(packed.shape[1] // (3 * HD)):
        base = head * 3 * HD
        for start, rows, length in spans:
            span = slice(start, start + rows)
            queries = packed[span, base : base + HD] * HD ** (-0.5)
            keys = packed[span, base + HD : base + 2 * HD]
            values = packed[span, base + 2 * HD : base + 3 * HD]
            yield head, base, span, length, queries, keys, values


def attend_kernel(spans, packed, out):
    for head, _, span, length, queries, keys, values in parts_of(packed, spans):
        soft = soft_columns(keys, queries, length).astype(BF)
        out[span, head * HD : (head + 1) * HD] = dot(values, soft, 0, 0).T.astype(BF)


def attend_back_kernel(spans, packed, grad, out):
    for head, base, span, length, queries, keys, values in parts_of(packed, spans):
        grads = grad[span, head * HD : (head + 1) * HD]
        soft = soft_columns(keys, queries, length)
        out[span, base + 2 * HD : base + 3 * HD] = dot(soft.astype(BF), grads).astype(BF)
        grad_soft = dot(values, grads, 1, 1)
        grad_scores = soft * (grad_soft - jnp.sum(soft * grad_soft, 0, keepdims=True))
        grad_scores = grad_scores.astype(BF)
        grad_queries = dot(keys, grad_scores, 0, 0).T * HD ** (-0.5)
        out[span, base : base + HD] = grad_queries.astype(BF)
        out[span, base + HD : base + 2 * HD] = dot(grad_scores, queries).astype(BF)


def attention(kernel, spans, packed, *grads, begin=0, stop=None, into=None):
    tokens, width = packed.shape
    stop = width // (6 * HD) if stop is None else stop
    wide = pl.BlockSpec((tokens, 6 * HD), lambda step: (0, step + begin))
    narrow = pl.BlockSpec((tokens, 2 * HD), lambda step: (0, step + begin))
    filled = [] if into is None else [into]
    count = 1 + len(grads)

    def run(*refs):
        kernel(spans, *refs[:count], refs[-1])

    return pl.pallas_call(
        run,
        grid=(stop - begin,),
        in_specs=[wide] + [narrow] * len(grads) + [pl.BlockSpec(memory_space=pl.ANY)] * len(filled),
        out_specs=wide if grads else narrow,
        out_shape=jax.ShapeDtypeStruct((tokens, width if grads else width // 3), BF),
        input_output_aliases={count: 0} if filled else {},
        compiler_params=pltpu.CompilerParams(vmem_limit_bytes=40 * 1024 * 1024),
    )(packed, *grads, *filled)


def row_kind(first, rows, spans):
    places = first + lax.broadcasted_iota(jnp.int32, (rows, 1), 0)
    return [(places >= start) & (places < start + length) for start, _, length in spans]


def row_grid(kernel, spans, inputs, rows, tables, outs):
    tokens, width = inputs[0].shape

    def body(*refs):
        first = pl.program_id(0) * rows
        kinds = row_kind(first, rows, spans)
        sums = refs[-1]

        @pl.when(pl.program_id(0) == 0)
        def _():
            sums[...] = jnp.zeros_like(sums)

        kernel(first, kinds, *refs)

    block = pl.BlockSpec((rows, width), lambda step: (step, 0))
    return pl.pallas_call(
        body,
        grid=(tokens // rows,),
        in_specs=[block] * len(inputs)
        + [pl.BlockSpec(table.shape, lambda step: (0, 0)) for table in tables],
        out_specs=[block] * len(outs) + [pl.BlockSpec((8, width), lambda step: (0, 0))],
        out_shape=[jax.ShapeDtypeStruct((tokens, width), kind) for kind in outs]
        + [jax.ShapeDtypeStruct((8, width), F32)],
        compiler_params=pltpu.CompilerParams(vmem_limit_bytes=32 * 1024 * 1024),
    )(*inputs, *tables)


def add_row(sums, index, values):
    sums[index : index + 1, :] += jnp.sum(values, 0, keepdims=True)


def middle_kernel(first, kinds, initial, mine, theirs, vec, middle, normed, sums):
    branch = mine[...].astype(F32) + theirs[...].astype(F32)
    values = initial[...] + vec[7:8, :] + branch
    unit, _ = normalize(values)
    middle[...] = values
    normed[...] = (unit * vec[2:3, :] + vec[3:4, :]).astype(BF)
    for index, kind in enumerate(kinds):
        add_row(sums, index, jnp.where(kind, values, 0.0))


def middle_back_kernel(first, kinds, middle, mine, theirs, vec, rows, out, sums):
    grad = mine[...].astype(F32) + theirs[...].astype(F32)
    unit, scale = normalize(middle[...])
    back = normalize_back(grad, unit, scale, vec[2:3, :])
    back = back + jnp.where(kinds[0], rows[0:1, :], jnp.where(kinds[1], rows[1:2, :], 0.0))
    out[...] = back.astype(BF)
    add_row(sums, 0, grad * unit)
    add_row(sums, 1, grad)
    add_row(sums, 2, back)


def initial_back_kernel(spans, first, kinds, initial, mine, theirs, middle, vec, out, sums):
    grad = mine[...].astype(F32) + theirs[...].astype(F32)
    unit, scale = normalize(initial[...])
    back = normalize_back(grad, unit, scale, vec[0:1, :]) + middle[...].astype(F32)
    out[...] = back.astype(BF)
    places = first + lax.broadcasted_iota(jnp.int32, (back.shape[0], 1), 0)
    is_class = (places == spans[0][0] + spans[0][2] - 1) | (places == spans[1][0] + spans[1][2] - 1)
    of_class = jnp.where(is_class, back, 0.0)
    add_row(sums, 0, grad * unit)
    add_row(sums, 1, grad)
    add_row(sums, 2, jnp.where(kinds[0] | kinds[1], back, 0.0) - of_class)
    add_row(sums, 3, of_class)


def hidden_kernel(spans, normed, weight, slope, sums):
    upward = dot(normed[...], weight[...])
    cumulative = 0.5 * (1.0 + lax.erf(upward * (0.5**0.5)))
    bell = jnp.exp(-0.5 * upward * upward) * (2.0 * math.pi) ** (-0.5)
    slope[...] = (cumulative + upward * bell).astype(BF)
    active = (upward * cumulative).astype(BF).astype(F32)
    sums[...] = jnp.zeros_like(sums)
    for index, (start, _, length) in enumerate(spans):
        rows = up_to(length, 16)
        part = active[start : start + rows]
        kept = lax.broadcasted_iota(jnp.int32, (rows, 1), 0) < length
        sums[index : index + 1, :] = jnp.sum(jnp.where(kept, part, 0.0), 0, keepdims=True)


def hidden_layer(spans, normed, weight):
    tokens, width = normed.shape
    columns = weight.shape[1]
    step = 256
    return pl.pallas_call(
        lambda *refs: hidden_kernel(spans, *refs),
        grid=(columns // step,),
        in_specs=[
            pl.BlockSpec((tokens, width), lambda index: (0, 0)),
            pl.BlockSpec((width, step), lambda index: (0, index)),
        ],
        out_specs=[
            pl.BlockSpec((tokens, step), lambda index: (0, index)),
            pl.BlockSpec((8, step), lambda index: (0, index)),
        ],
        out_shape=[
            jax.ShapeDtypeStruct((tokens, columns), BF),
            jax.ShapeDtypeStruct((8, columns), F32),
        ],
        compiler_params=pltpu.CompilerParams(vmem_limit_bytes=40 * 1024 * 1024),
    )(normed, weight)


def iterate_kernel(start, kept, came, came_side, rows_out, total_out):
    step = D // 3
    rows = rows_out.shape[0]
    parts = kept[start[1]], came[start[1]], came_side[...]
    blocks = [sum(part[index].astype(F32) for part in parts) for index in range(6)]
    same = lax.broadcasted_iota(jnp.int32, (step, step), 0) == lax.broadcasted_iota(
        jnp.int32, (step, step), 1
    )
    total = jnp.sum(jnp.where(same, blocks[0] + blocks[3] + blocks[5], 0.0))
    inverse = 1.0 / (jnp.sqrt(jnp.full((1, 1), total, F32)) + 1e-07)
    total_out[...] = jnp.full(total_out.shape, total, F32)
    aa, ab, ac, bb, bc, cc = [blocks[index] * (inverse * inverse) for index in range(6)]
    gram = jnp.concatenate(
        [
            jnp.concatenate([aa, ab, ac], 1),
            jnp.concatenate([ab.T, bb, bc], 1),
            jnp.concatenate([ac.T, bc.T, cc], 1),
        ],
        0,
    )
    eye = (
        lax.broadcasted_iota(jnp.int32, (D, D), 0) == lax.broadcasted_iota(jnp.int32, (D, D), 1)
    ).astype(F32)
    chosen = (
        lax.broadcasted_iota(jnp.int32, (rows, D), 0) + start[0]
        == lax.broadcasted_iota(jnp.int32, (rows, D), 1)
    ).astype(F32)
    polynomials = []
    for _ in range(NS_STEPS - 1):
        low = gram.astype(BF)
        polynomial = POLY_ONE * eye + POLY_TWO * gram + POLY_THREE * dot(low, low)
        polynomial = polynomial.astype(BF)
        polynomials.append(polynomial)
        gram = dot(dot(low, polynomial).astype(BF), polynomial)
    low = gram.astype(BF)
    gram_rows = dot(chosen.astype(BF), low)
    out = POLY_ONE * chosen + POLY_TWO * gram_rows + POLY_THREE * dot(gram_rows.astype(BF), low)
    for polynomial in polynomials[::-1]:
        out = dot(out.astype(BF), polynomial)
    rows_out[...] = (out * inverse).astype(BF)


def iterate_gram(start, kept, came, came_side, rows):
    vmem = pl.BlockSpec(memory_space=pltpu.VMEM)
    return pl.pallas_call(
        iterate_kernel,
        in_specs=[pl.BlockSpec(memory_space=pltpu.SMEM)] + [vmem] * 3,
        out_specs=[vmem] * 2,
        out_shape=[
            jax.ShapeDtypeStruct((rows, D), BF),
            jax.ShapeDtypeStruct((8, 128), F32),
        ],
        compiler_params=pltpu.CompilerParams(vmem_limit_bytes=48 * 1024 * 1024),
    )(start.astype(jnp.int32), kept, came, came_side)


def adam_update(weight, gradient, first, second, rate, decay):
    first = BETA_FIRST * first + (1.0 - BETA_FIRST) * gradient
    second = BETA_SECOND * second + (1.0 - BETA_SECOND) * gradient * gradient
    direction = (
        first
        / (1.0 - BETA_FIRST**STEP)
        / (jnp.sqrt(second / (1.0 - BETA_SECOND**STEP)) + ADAM_FLOOR)
    )
    return (weight - rate * (direction + decay * weight), first, second)


def square_sum(own, shared, count):
    arrays = (*own, *shared)

    def kernel(*refs):
        total = jnp.zeros((1, 1), F32)
        for index, ref in enumerate(refs[:-1]):
            values = ref[...]
            rows = jnp.sum(values * values, 1, keepdims=True)
            part = jnp.sum(rows, 0, keepdims=True)
            total = total + (part if index < len(own) else part / count)
        refs[-1][...] = jnp.broadcast_to(total, (8, 128))

    vmem = pl.BlockSpec(memory_space=pltpu.VMEM)
    return pl.pallas_call(
        kernel,
        in_specs=[vmem] * len(arrays),
        out_specs=vmem,
        out_shape=jax.ShapeDtypeStruct((8, 128), F32),
    )(*arrays)


def moment_kernel(pieces, count, factor, *refs):
    olds, grads, moments = (refs[index * count : (index + 1) * count] for index in range(3))
    blocks = refs[-1]
    step = D // 3
    place = 0
    for old, grad, moment in zip(olds, grads, moments):
        before = old[...].astype(F32)
        moment[...] = (MOMENTUM * before + factor[0] * grad[...].astype(F32)).astype(BF)
        for low, top in pieces:
            matrix = moment[:, low:top]
            for row, column in ((0, 0), (0, 1), (0, 2), (1, 1), (1, 2), (2, 2)):
                left = matrix[row * step : (row + 1) * step]
                right = matrix[column * step : (column + 1) * step]
                blocks[place // 6, place % 6] = dot(left, right, 1, 1).astype(BF)
                place += 1


def moment_grams(factor, old, block, grads, pieces):
    count, rows = len(grads), old.shape[0]
    width = grads[0].shape[1]
    whole = pl.BlockSpec((rows, width), lambda step: (0, 0))
    olds = [
        pl.BlockSpec((rows, width), lambda step, index=block + place: (0, index))
        for place in range(count)
    ]
    shape = (count * len(pieces), 6, D // 3, D // 3)
    *moments, blocks = pl.pallas_call(
        lambda *refs: moment_kernel(pieces, count, *refs),
        grid=(1,),
        in_specs=[pl.BlockSpec(memory_space=pltpu.SMEM)] + olds + [whole] * count,
        out_specs=[whole] * count + [pl.BlockSpec(shape, lambda step: (0, 0, 0, 0))],
        out_shape=[jax.ShapeDtypeStruct((rows, width), BF)] * count
        + [jax.ShapeDtypeStruct(shape, BF)],
        compiler_params=pltpu.CompilerParams(vmem_limit_bytes=56 * 1024 * 1024),
    )(jnp.reshape(factor, (1,)), *[old] * count, *grads)
    return moments, blocks


def body(
    low_patches,
    high_patches,
    interp,
    labels,
    partner,
    pair_count,
    w_patch,
    pos_table,
    vectors,
    head_w,
    w_qkv,
    w_out,
    w_up,
    w_down,
    mom_qkv,
    mom_out,
    mom_up,
    mom_down,
    first_patch,
    second_patch,
    first_pos,
    second_pos,
    first_vec,
    second_vec,
    first_head,
    second_head,
):
    batch = lax.axis_index("batch")
    head = lax.axis_index("head")
    side = head // 2
    batch_size = lax.axis_size("batch")
    head_size = lax.axis_size("head")
    rows_here = w_patch.shape[0]
    grid_low, grid_high = low_patches.shape[1], high_patches.shape[1]
    low_rows = up_to(grid_low + 1, 16)
    high_rows = up_to(grid_high + 1, 16)
    tokens = low_rows + high_rows
    qkv_width, out_width = w_qkv.shape[1], w_out.shape[1]
    hidden = w_up.shape[1]
    patch_width = D // head_size
    extra_width = 64
    head_columns = head_w.shape[1]
    head_padded = up_to(head_columns, 64 * head_size)
    head_width = head_padded // head_size
    table_rows = extra_width * head_size

    pos_turned, vec_turned = pos_table.T, vectors.T
    table = jnp.concatenate([pos_turned[:, 1:], pos_turned[:, :1], vec_turned], 1).astype(BF)
    table = jnp.pad(table, ((0, 0), (0, table_rows - table.shape[1])))
    quarter_patch = lax.dynamic_slice_in_dim(w_patch, head * patch_width, patch_width, 1)
    quarter_table = lax.dynamic_slice_in_dim(table, head * extra_width, extra_width, 1)
    padded_head = jnp.pad(head_w.astype(BF), ((0, 0), (0, head_padded - head_columns)))
    quarter_head = lax.dynamic_slice_in_dim(padded_head, head * head_width, head_width, 1)
    small = patch_width + extra_width
    chunk_one = jnp.concatenate([quarter_patch.astype(BF), quarter_table, w_qkv.astype(BF)], 1)
    chunk_two = jnp.concatenate([w_out.astype(BF), w_up.astype(BF)], 1)
    chunk_three = jnp.concatenate([w_down.astype(BF), quarter_head], 1)
    lines = gather_lines(chunk_one)
    chunk_two, lines = tie(chunk_two, lines)
    planes = gather_planes(lines)
    lines_two = gather_lines(chunk_two)
    planes, lines_two = tie(planes, lines_two)
    ends = gather_ends(planes)
    planes_two = gather_planes(lines_two)
    both_small, full_qkv = gather_last(planes, ends, (small, qkv_width))
    full_patch, table = all_quarters(both_small, extra_width)
    chunk_three, full_patch = tie(chunk_three, full_patch)
    lines_three = gather_lines(chunk_three)

    class_row = grid_low
    vec = table[grid_low + 1 : grid_low + 11].astype(F32)
    pos_low = table[:low_rows].astype(F32)
    pos_high = dot(interp, table[:grid_low])
    row_low = jnp.arange(low_rows)[:, None]
    row_high = jnp.arange(high_rows)[:, None]
    class_add = table[class_row].astype(F32) + vec[9]
    add_low = jnp.where(
        row_low < grid_low, pos_low + vec[6], jnp.where(row_low == grid_low, class_add, 0.0)
    )
    pos_high = jnp.pad(pos_high, ((0, high_rows - grid_high), (0, 0)))
    add_high = jnp.where(
        row_high < grid_high, pos_high + vec[6], jnp.where(row_high == grid_high, class_add, 0.0)
    )
    added = jnp.concatenate([add_low, add_high], 0)
    is_patch = jnp.concatenate([row_low < grid_low, row_high < grid_high], 0)
    is_token = jnp.concatenate([row_low <= grid_low, row_high <= grid_high], 0)
    patches = jnp.concatenate(
        [
            jnp.pad(at(low_patches, side), ((0, low_rows - grid_low), (0, 0))),
            jnp.pad(at(high_patches, side), ((0, high_rows - grid_high), (0, 0))),
        ],
        0,
    )
    initial = dot(patches, full_patch) + added
    unit_one, _ = normalize(initial)
    normed = (unit_one * vec[0] + vec[1]).astype(BF)
    packed = dot(normed, full_qkv).astype(BF)
    packed, planes_two, lines_three = tie(packed, planes_two, lines_three)
    ends_two = gather_ends(planes_two)
    planes_three = gather_planes(lines_three)
    spans = ((0, low_rows, grid_low + 1), (low_rows, high_rows, grid_high + 1))
    blended = attention(attend_kernel, spans, packed)
    full_out, full_up = gather_last(planes_two, ends_two, (out_width, hidden))
    branch = dot(blended, full_out, 1, 1).astype(BF)
    block_rows = 160
    middle, normed_two, middle_sums = row_grid(
        middle_kernel, spans, (initial, branch, swap_core(branch)), block_rows, (vec,), (F32, BF)
    )
    normed_two, planes_three = tie(normed_two, planes_three)
    ends_three = gather_ends(planes_three)
    slope, active_sums = hidden_layer(spans, normed_two, full_up)
    active_sums = active_sums[:2]
    full_down, both_head = gather_last(planes_three, ends_three, (hidden, head_width))
    (full_head,) = all_quarters(both_head)
    held = jnp.concatenate([mom_qkv, mom_out, mom_up, mom_down], 1).astype(BF)
    held, full_down = tie(held, full_down)
    full_old = lax.all_gather(held, "batch", axis=0, tiled=True)

    lengths = jnp.array([[grid_low + 1.0], [grid_high + 1.0]], F32)
    active_means = active_sums / lengths
    means_high = active_means.astype(BF)
    means_low = (active_means - means_high.astype(F32)).astype(BF)
    down_parts = dot(jnp.concatenate([means_high, means_low]), full_down, 1, 1)
    down_part = down_parts[:2] + down_parts[2:]
    down_part = down_part + swap_core(down_part)
    pooled_own = middle_sums[:2] / lengths + vec[8] + down_part

    ids = jnp.stack([side, low_patches.shape[0] + side])
    own_labels, own_partners = labels[ids], partner[ids]
    tags = jnp.stack([own_labels // 8, own_labels % 8, own_partners // 8, own_partners % 8], 1)
    pooled_high = pooled_own.astype(BF)
    pooled_low = (pooled_own - pooled_high.astype(F32)).astype(BF)
    tags = jnp.pad(tags.astype(BF), ((0, 0), (0, 124)))
    common = jnp.concatenate([pooled_high, pooled_low, tags], 1)
    active_low = active_sums.astype(BF)
    came = swap_side(jnp.concatenate([common, active_low[:, hidden:]], 1))
    came, full_head = tie(came, full_head)
    mine = jnp.concatenate([common, active_low[:, :hidden]], 1)
    both_sides = in_order(jnp.stack([mine, came]), side, 1)
    everyone = gather_small(both_sides.transpose(1, 0, 2))
    images = batch_size * 4
    everyone = everyone.reshape(images, 2 * D + 128 + hidden)
    pooled = everyone[:, :D].astype(F32) + everyone[:, D : 2 * D].astype(F32)
    all_tags = everyone[:, 2 * D : 2 * D + 4].astype(jnp.int32)
    all_labels = all_tags[:, 0] * 8 + all_tags[:, 1]
    all_partners = all_tags[:, 2] * 8 + all_tags[:, 3]
    all_sums = everyone[:, 2 * D + 128 :]
    unit_final, scale_final = normalize(pooled)
    features = (unit_final * vec[4] + vec[5]).astype(BF)
    outputs = dot(features, full_head)
    logits, projected = outputs[:, :CLS], outputs[:, CLS:head_columns]
    picked = jnp.arange(CLS)[None, :] == all_labels[:, None]
    logit_top = jnp.max(logits, -1, keepdims=True)
    logit_log = logit_top + jnp.log(jnp.sum(jnp.exp(logits - logit_top), -1, keepdims=True))
    class_terms = logit_log - jnp.sum(jnp.where(picked, logits, 0.0), -1, keepdims=True)
    grad_logits = (jnp.exp(logits - logit_log) - picked.astype(F32)) * (1.0 / images)
    length_inverse = lax.rsqrt(jnp.sum(projected * projected, -1, keepdims=True) + 1e-06)
    embedded = (projected * length_inverse).astype(BF)
    similar = dot(embedded, embedded, 1, 1) / SOFTMAX_TEMP
    image_ids = jnp.arange(images, dtype=jnp.int32)
    masked = jnp.where(image_ids[:, None] == image_ids[None, :], -1e30, similar)
    similar_top = jnp.max(masked, -1, keepdims=True)
    similar_log = similar_top + jnp.log(jnp.sum(jnp.exp(masked - similar_top), -1, keepdims=True))
    target = image_ids[None, :] == all_partners[:, None]
    pair_terms = similar_log - jnp.sum(jnp.where(target, similar, 0.0), -1, keepdims=True)
    losses = jnp.sum(jnp.concatenate([pair_terms, class_terms], 1), 0)
    count = pair_count[0].astype(F32)
    grad_similar = ((jnp.exp(masked - similar_log) - target.astype(F32)) / count).astype(BF)
    grad_embedded = (dot(grad_similar, embedded) + dot(grad_similar, embedded, 0, 0)) / SOFTMAX_TEMP
    grad_embedded = grad_embedded.astype(BF).astype(F32)
    grad_projected = length_inverse * grad_embedded - projected * (
        length_inverse**3 * jnp.sum(grad_embedded * projected, -1, keepdims=True)
    )
    grad_outputs = jnp.concatenate([grad_logits, grad_projected], 1).astype(BF)
    grad_outputs = jnp.pad(grad_outputs, ((0, 0), (0, head_padded - head_columns)))
    features_here = lax.dynamic_slice_in_dim(features, batch * rows_here, rows_here, 1)
    grad_head = dot(features_here, grad_outputs, 0, 0)[:, :head_columns]
    grad_features = dot(grad_outputs, full_head, 1, 1)
    grad_pooled = normalize_back(grad_features, unit_final, scale_final, vec[4])
    complete_rows = jnp.stack(
        [
            jnp.sum(grad_features * unit_final, 0),
            jnp.sum(grad_features, 0),
            jnp.sum(grad_pooled, 0),
        ]
    )
    is_low = (image_ids % 4) < 2
    grad_token = grad_pooled / jnp.where(is_low, grid_low + 1.0, grid_high + 1.0)[:, None]
    own_rows = [batch * 4 + side, batch * 4 + 2 + side]
    grad_own = jnp.stack([at(grad_token, index) for index in own_rows])
    grad_own_low = grad_own.astype(BF)

    def spread(pair, mask):
        rows = jnp.concatenate(
            [
                jnp.broadcast_to(pair[0], (low_rows, pair.shape[1])),
                jnp.broadcast_to(pair[1], (high_rows, pair.shape[1])),
            ],
            0,
        )
        return jnp.where(mask, rows, 0.0)

    grad_active = dot(grad_own_low, full_down)
    grad_upward = (spread(grad_active, is_token) * slope.astype(F32)).astype(BF)
    grad_normed_two = dot(grad_upward, full_up, 1, 1).astype(BF)
    grad_up = dot(normed_two, grad_upward, 0, 0).astype(BF)
    kept_up, came_up = reduce_first(grad_up[:, :hidden], grad_up[:, hidden:])
    grad_middle, middle_row_sums = row_grid(
        middle_back_kernel,
        spans,
        (middle, grad_normed_two, swap_core(grad_normed_two)),
        block_rows,
        (vec, jnp.pad(grad_own, ((0, 6), (0, 0)))),
        (BF,),
    )
    grad_blend = dot(grad_middle, full_out).astype(BF)
    grad_out = dot(grad_middle, blended, 0, 0).astype(BF)
    grad_packed = attention(attend_back_kernel, spans, packed, grad_blend)
    grad_normed = dot(grad_packed, full_qkv, 1, 1).astype(BF)
    grad_normed, came_up = tie(grad_normed, came_up)
    kept_up, came_up = reduce_second(kept_up, came_up)
    grad_qkv = dot(normed, grad_packed, 0, 0).astype(BF)
    tails = [
        jnp.concatenate(
            [
                grad_qkv[:, index * qkv_width : (index + 1) * qkv_width],
                grad_out[:, index * out_width : (index + 1) * out_width],
            ],
            1,
        )
        for index in range(2)
    ]
    kept_tail, came_tail = reduce_first(*tails)
    grad_initial, initial_row_sums = row_grid(
        lambda *refs: initial_back_kernel(spans, *refs),
        spans,
        (initial, grad_normed, swap_core(grad_normed), grad_middle),
        block_rows,
        (vec,),
        (BF,),
    )
    grad_initial, came_up = tie(grad_initial, came_up)
    kept_up, came_up = reduce_third(kept_up, came_up)
    from_high = dot(interp, grad_initial[low_rows : low_rows + grid_high], 0, 0)
    zero_row = jnp.zeros((1, D), F32)
    class_both = initial_row_sums[3:4]
    table_grad = jnp.concatenate(
        [
            grad_initial[:grid_low].astype(F32) + from_high,
            class_both,
            initial_row_sums[:2],
            middle_row_sums[:2],
            zero_row,
            zero_row,
            initial_row_sums[2:3],
            middle_row_sums[2:3],
            zero_row,
            class_both,
            jnp.zeros((table_rows - grid_low - 11, D), F32),
        ],
        0,
    )
    table_grad = table_grad.astype(BF).T

    def quarter_of(values, width, index):
        return lax.dynamic_slice_in_dim(values, index * width, width, 1)

    owners = (head, head ^ 2)
    columns = [quarter_of(grad_initial, patch_width, index) for index in owners]
    grad_patch = dot(patches, jnp.concatenate(columns, 1), 0, 0).astype(BF)
    grad_small = [
        jnp.concatenate(
            [
                grad_patch[:, index * patch_width : (index + 1) * patch_width],
                quarter_of(table_grad, extra_width, owner),
            ],
            1,
        )
        for index, owner in enumerate(owners)
    ]
    kept_small, came_small = reduce_first(*grad_small)
    came_small, came_tail, full_old = tie(came_small, came_tail, full_old)

    def beside(left, right):
        return [jnp.concatenate(pair, -1) for pair in zip(left, right)]

    kept_tail, came_tail = reduce_second(
        beside(kept_tail, kept_small), beside(came_tail, came_small)
    )
    came_tail, came_up = tie(came_tail, came_up)
    reduced_up = reduce_last(kept_up, came_up)
    full_grad_up = lax.all_gather(reduced_up.astype(BF), "batch", axis=0, tiled=True)
    kept_tail, came_tail = reduce_third(kept_tail, came_tail)
    reduced_tail = reduce_last(kept_tail, came_tail)
    own_width = qkv_width + out_width
    lines_tail = gather_lines(reduced_tail[:, :own_width].astype(BF))
    reduced_qkv = reduced_tail[:, :qkv_width]
    reduced_out = reduced_tail[:, qkv_width:own_width]
    full_grad_down = dot(grad_token.astype(BF), all_sums, 0, 0)
    reduced_down = lax.dynamic_slice_in_dim(full_grad_down, batch * rows_here, rows_here, 0)

    quarter = reduced_tail[:, own_width:]
    complete_here = lax.dynamic_slice_in_dim(complete_rows, batch * rows_here, rows_here, 1)
    muon_grads = (reduced_qkv, reduced_out, reduced_up, reduced_down)
    squares = square_sum(
        (reduced_tail, reduced_up, reduced_down), (grad_head, complete_here), head_size
    )
    for axis, mask in (("head", 1), ("head", 2), ("batch", 1)):
        squares = squares + swap(squares, axis, mask)
    quarter = quarter.astype(BF)
    quarters = jnp.concatenate([quarter, swap_side(quarter)], 1)
    partner_quarters = swap_core(quarters)
    reduced_patch, reduced_table = all_quarters(quarters, extra_width, partner_quarters, False)
    reduced_patch, reduced_table = reduced_patch.astype(F32), reduced_table.astype(F32)
    reduced_pos = jnp.concatenate(
        [reduced_table[:, grid_low : grid_low + 1], reduced_table[:, :grid_low]], 1
    )
    partial_vec = reduced_table[:, grid_low + 1 : grid_low + 11]
    complete_turned = complete_here.T
    reduced_vec = jnp.concatenate(
        [
            partial_vec[:, :4],
            complete_turned[:, :2],
            partial_vec[:, 6:8],
            complete_turned[:, 2:],
            partial_vec[:, 9:],
        ],
        1,
    )
    squares, lines_tail, *adam_grads = tie(
        squares, lines_tail, reduced_patch, reduced_pos, reduced_vec
    )
    tail_x = swap_x(lines_tail) if batch_size == 8 else lines_tail
    mask = 2
    while mask < batch_size:
        squares = squares + swap(squares, "batch", mask)
        mask *= 2
    norm = jnp.sqrt(squares[0, 0])
    factor = jnp.minimum(1.0, CLIP_NORM / norm)
    factor, full_grad_up = tie(factor, full_grad_up)
    old_moments = (mom_qkv, mom_out, mom_up, mom_down)
    old_weights = (w_qkv, w_out, w_up, w_down)
    starts = (0, qkv_width, own_width)
    (moment_up, moment_down), early_pair = moment_grams(
        factor, full_old, 1, (full_grad_up, full_grad_down), ((0, hidden),)
    )
    early_pair, tail_x = tie(early_pair, tail_x)
    full_tail = gather_batch(lines_tail, tail_x)

    (moment_tail,), late_pair = moment_grams(
        factor, full_old, 0, (full_tail,), ((0, qkv_width), (qkv_width, own_width))
    )
    on_first = head % 2 == 0
    came = swap_core(jnp.where(on_first, early_pair, late_pair))
    kept = jnp.where(on_first, late_pair, early_pair)
    sent = (at(kept, 1 - side).astype(F32) + at(came, 1 - side).astype(F32)).astype(BF)
    came_side = swap_side(sent)
    middle_factor, adam_grads, firsts, seconds, _ = tie(
        factor,
        (*adam_grads, grad_head),
        (first_patch, first_pos.T, first_vec.T, first_head),
        (second_patch, second_pos.T, second_vec.T, second_head),
        sent,
    )
    adam_weights = (w_patch, pos_turned, vec_turned, head_w)
    moments = [
        MOMENTUM * old_moments[index] + middle_factor * muon_grads[index] for index in range(4)
    ]
    adam_new = [
        adam_update(
            adam_weights[index],
            middle_factor * adam_grads[index],
            firsts[index],
            seconds[index],
            ADAM_RATES[index],
            ADAM_DECAYS[index],
        )
        for index in range(4)
    ]
    for index in (1, 2):
        adam_new[index] = [part.T for part in adam_new[index]]
    rows, total_here = iterate_gram(
        jnp.stack([batch * rows_here, side]), kept, came, came_side, rows_here
    )
    rows_side = swap_side(rows)
    rows_side, total_here = tie(rows_side, total_here)
    pair = jnp.stack([rows, rows_side])
    four = jnp.concatenate([pair, swap_core(pair)])
    slots = jnp.arange(8)[:, None] == swapped(head)
    totals = sum_over_head(jnp.where(slots, total_here, 0.0))
    moment_logs = jnp.log(totals[:4, 0])
    parts = (moment_tail[:, :qkv_width], moment_tail[:, qkv_width:], moment_up, moment_down)
    new_muon = []
    for index in range(4):
        weight = old_weights[index]
        scale = 0.2 * math.sqrt(max(D, weight.shape[1] * head_size))
        iterate = dot(at(four, swapped(head ^ swapped(index))), parts[index])
        new_muon.append(weight - MUON_RATE * (scale * iterate + DECAY_RATE * weight))
    return (
        adam_new[0][0],
        adam_new[1][0],
        adam_new[2][0],
        adam_new[3][0],
        new_muon[0],
        new_muon[1],
        new_muon[2],
        new_muon[3],
        moments[0],
        moments[1],
        moments[2],
        moments[3],
        adam_new[0][1],
        adam_new[1][1],
        adam_new[2][1],
        adam_new[3][1],
        adam_new[0][2],
        adam_new[1][2],
        adam_new[2][2],
        adam_new[3][2],
        losses,
        norm[None],
        moment_logs,
    )


def solution(mesh):
    placed = (
        P("batch", None, None),
        P("batch", None, None),
        P(),
        P("batch"),
        P("batch"),
        P(),
        P("batch", None),
        P(None, "batch"),
        P(None, "batch"),
        P("batch", None),
        P("batch", "head"),
        P("batch", "head"),
        P("batch", "head"),
        P("batch", "head"),
        P("batch", "head"),
        P("batch", "head"),
        P("batch", "head"),
        P("batch", "head"),
        P("batch", None),
        P("batch", None),
        P(None, "batch"),
        P(None, "batch"),
        P(None, "batch"),
        P(None, "batch"),
        P("batch", None),
        P("batch", None),
    )
    return jax.shard_map(
        body,
        mesh=mesh,
        in_specs=placed,
        out_specs=(
            P("batch", None),
            P(None, "batch"),
            P(None, "batch"),
            P("batch", None),
            P("batch", "head"),
            P("batch", "head"),
            P("batch", "head"),
            P("batch", "head"),
            P("batch", "head"),
            P("batch", "head"),
            P("batch", "head"),
            P("batch", "head"),
            P("batch", None),
            P(None, "batch"),
            P(None, "batch"),
            P("batch", None),
            P("batch", None),
            P(None, "batch"),
            P(None, "batch"),
            P("batch", None),
            P(),
            P(),
            P(),
        ),
        check_vma=False,
    )
```

```python
import math

import jax
import jax.numpy as jnp
from jax import lax
from jax.experimental import pallas as pl
from jax.experimental.pallas import tpu as pltpu
from jax.sharding import PartitionSpec as P

D = 768
HD = 64
CLS = 1000
NS_STEPS = 3
STEP = 10

POLY_ONE = 3.4445
POLY_TWO = -4.775
POLY_THREE = 2.0315
SOFTMAX_TEMP = 0.05
CLIP_NORM = 0.05
MOMENTUM = 0.95
MUON_RATE = 0.2
DECAY_RATE = 0.05
BETA_FIRST = 0.9
BETA_SECOND = 0.99
ADAM_FLOOR = 1e-08
ADAM_RATES = (0.08, 0.3, 0.5, 0.15)
ADAM_DECAYS = (0.05, 0.05, 0.0, 0.05)

BF = jnp.bfloat16
F32 = jnp.float32


def up_to(size, step):
    return -(-size // step) * step


def dot(left, right, left_dim=1, right_dim=0, precision=None):
    return lax.dot_general(
        left,
        right,
        (((left_dim,), (right_dim,)), ((), ())),
        precision=precision,
        preferred_element_type=F32,
    )


def at(stacked, index):
    return lax.dynamic_index_in_dim(stacked, index, 0, keepdims=False)


def swap(values, axis, mask):
    count = lax.axis_size(axis)
    return lax.ppermute(values, axis, [(index, index ^ mask) for index in range(count)])


def swap_core(values):
    return swap(values, "head", 1)


def swap_side(values):
    return swap(values, "head", 2)


def swap_x(values):
    return swap(values, "batch", 1)


def place_kernel(splits, position, own, own_x, own_side, near, far, *outs):
    x = position[1]
    corner = jnp.where((position[0] ^ pl.program_id(0)) < 2, near[...], far[...])
    parts = ((own[...], x, 0), (own_x[...], 1 - x, 0), (own_side[...], x, 1), (corner, 1 - x, 1))
    for part, where, group in parts:
        start = 0
        for width, out in zip(splits, outs):
            out[0, pl.ds(where, 1), :, group * width : (group + 1) * width] = part[
                :, :, start : start + width
            ]
            start += width


def place(parts, splits):
    here = lax.axis_index("batch")
    position = jnp.stack([here // 2, here % 2]).astype(jnp.int32)
    _, rows, columns = parts[0].shape

    def block(pick_line):
        return pl.BlockSpec(
            (1, rows, columns), lambda step, spot: (pick_line(spot[0] ^ step), 0, 0)
        )

    whole = block(lambda line: line)
    near, far = block(lambda line: line & 1), block(lambda line: line & 1)
    outs = pl.pallas_call(
        lambda *refs: place_kernel(splits, *refs),
        grid_spec=pltpu.PrefetchScalarGridSpec(
            num_scalar_prefetch=1,
            grid=(4,),
            in_specs=[whole, whole, whole, near, far],
            out_specs=[
                pl.BlockSpec((1, 2, rows, 2 * width), lambda step, spot: (step, 0, 0, 0))
                for width in splits
            ],
        ),
        out_shape=[
            jax.ShapeDtypeStruct((4, 2, rows, 2 * width), parts[0].dtype) for width in splits
        ],
        compiler_params=pltpu.CompilerParams(vmem_limit_bytes=32 * 1024 * 1024),
    )(position, *parts)
    return [out.reshape(8 * rows, out.shape[-1]) for out in outs]


def tie(*values):
    return lax.optimization_barrier(values)


def gather_lines(shard):
    if lax.axis_size("batch") != 8:
        return lax.all_gather(shard, "batch", axis=0, tiled=True)
    return jnp.stack([shard] + [swap(shard, "batch", 2 * mask) for mask in (1, 2, 3)])


def gather_batch(lines, lines_x):
    if lax.axis_size("batch") != 8:
        return lines
    here = lax.axis_index("batch")
    position = jnp.stack([here // 2, here % 2]).astype(jnp.int32)
    _, rows, columns = lines.shape

    def kernel(spot, own, own_x, out):
        out[0, pl.ds(spot[1], 1)] = own[...]
        out[0, pl.ds(1 - spot[1], 1)] = own_x[...]

    line = pl.BlockSpec((1, rows, columns), lambda step, spot: (spot[0] ^ step, 0, 0))
    out = pl.pallas_call(
        kernel,
        grid_spec=pltpu.PrefetchScalarGridSpec(
            num_scalar_prefetch=1,
            grid=(4,),
            in_specs=[line, line],
            out_specs=pl.BlockSpec((1, 2, rows, columns), lambda step, spot: (step, 0, 0, 0)),
        ),
        out_shape=jax.ShapeDtypeStruct((4, 2, rows, columns), lines.dtype),
        compiler_params=pltpu.CompilerParams(vmem_limit_bytes=32 * 1024 * 1024),
    )(position, lines, lines_x)
    return out.reshape(8 * rows, columns)


def gather_came(shard):
    if lax.axis_size("batch") != 8:
        return [gather_lines(shard)]
    return [swap(shard, "batch", 2 * mask) for mask in (1, 2, 3)]


def gather_planes(lines):
    if lax.axis_size("batch") != 8:
        return lines, swap_side(lines)
    return lines, swap_x(lines), swap_side(lines)


def gather_ends(planes):
    if lax.axis_size("batch") != 8:
        return ()
    return swap_side(planes[1][:2]), swap_x(planes[2][2:])


def gather_last(planes, ends, splits):
    if lax.axis_size("batch") != 8:
        own, other = planes
        outs, start = [], 0
        for width in splits:
            pair = [own[:, start : start + width], other[:, start : start + width]]
            outs.append(jnp.concatenate(pair, 1))
            start += width
        return outs
    return place([*planes, *ends], splits)


def swapped(index):
    return (index % 2) * 2 + index // 2


def pick(blocks, index, axis):
    return lax.dynamic_index_in_dim(blocks, index, axis, keepdims=False)


def reduce_first(own, other):
    count = lax.axis_size("batch")
    if count != 8:
        return (own,), (swap_side(other),)
    rows, columns = own.shape[0] // count, own.shape[1]
    half = rows // 2
    x = lax.axis_index("batch") % 2
    own = own.reshape(4, 2, rows, columns)
    other = other.reshape(4, 2, rows, columns)
    kept = [pick(part[:, :, half:], x, 1) for part in (own, other)]
    sent = [pick(part[:, :, half:], 1 - x, 1) for part in (own, other)]
    came = swap_side(other[:, :, :half]), swap_x(jnp.stack(sent))
    return (own[:, :, :half], *kept), came


def reduce_second(kept, came):
    if lax.axis_size("batch") != 8:
        return (kept[0].astype(F32) + came[0].astype(F32),), ()
    x = lax.axis_index("batch") % 2
    first = kept[0].astype(F32) + came[0].astype(F32)
    second = kept[1].astype(F32) + came[1][0].astype(F32)
    sent = (kept[2].astype(F32) + came[1][1].astype(F32)).astype(BF)
    came = swap_x(pick(first, 1 - x, 1).astype(BF)), swap_side(sent)
    return (pick(first, x, 1), second), came


def reduce_third(kept, came):
    if lax.axis_size("batch") != 8:
        return (lax.psum_scatter(kept[0], "batch", scatter_dimension=0, tiled=True),), ()
    z = lax.axis_index("batch") // 2
    both = jnp.concatenate([part + got.astype(F32) for part, got in zip(kept, came)], 1)
    came = [swap(at(both, z ^ mask).astype(BF), "batch", 2 * mask) for mask in (1, 2, 3)]
    return (at(both, z),), came


def reduce_last(kept, came):
    total = kept[0]
    for got in came:
        total = total + got.astype(F32)
    return total


def reduce_line(kept, came, step):
    if lax.axis_size("batch") != 8:
        return reduce_second(kept, came) if step == 1 else reduce_third(kept, came)
    total = kept[0].astype(F32) + came[0].astype(F32)
    here = lax.axis_index("batch")
    if step == 1:
        total = total.reshape(4, 2, -1, total.shape[-1])
        sent = pick(total, 1 - here % 2, 1).astype(BF)
        return (pick(total, here % 2, 1),), (swap_x(sent),)
    z = here // 2
    came = [swap(at(total, z ^ mask).astype(BF), "batch", 2 * mask) for mask in (1, 2, 3)]
    return (at(total, z),), came


def in_order(stacked, here, bits):
    tail = stacked.shape[1:]
    stacked = stacked.reshape((2,) * bits + tail)
    for bit in range(bits):
        axis = bits - 1 - bit
        flag = (here >> bit) % 2 == 1
        stacked = jnp.where(flag, jnp.flip(stacked, axis), stacked)
    return stacked.reshape((2**bits,) + tail)


def gather_small(values):
    count = lax.axis_size("batch")
    if count != 8:
        return lax.all_gather(values, "batch", axis=0, tiled=False)
    pair = jnp.stack([values, swap_x(values)])
    lines = jnp.stack([pair] + [swap(pair, "batch", 2 * mask) for mask in (1, 2, 3)])
    return in_order(lines.reshape((8,) + values.shape), lax.axis_index("batch"), 3)


def sum_everywhere(values):
    for axis in ("head", "batch"):
        mask = 1
        while mask < lax.axis_size(axis):
            values = values + swap(values, axis, mask)
            mask *= 2
    return values


def sum_over_head(values):
    mask = 1
    while mask < lax.axis_size("head"):
        values = values + swap(values, "head", mask)
        mask *= 2
    return values


def order_kernel(turned, turn, position, mine, theirs, *outs):
    core, side = position[0], position[1]
    width = mine.shape[1] // 2
    plain = width - turned
    for index in range(4):
        same_core = core == index % 2
        same_side = side == index // 2
        kept = jnp.where(same_core, mine[:, :width], theirs[:, :width])
        other = jnp.where(same_core, mine[:, width:], theirs[:, width:])
        quarter = jnp.where(same_side, kept, other)
        outs[0][:, index * plain : (index + 1) * plain] = quarter[:, :plain]
        if turned and not turn:
            outs[1][:, index * turned : (index + 1) * turned] = quarter[:, plain:]
        elif turned:
            outs[1][index * turned : (index + 1) * turned, :] = (
                quarter[:, plain:].astype(F32).T.astype(BF)
            )


def all_quarters(mine, turned=0, theirs=None, turn=True):
    head = lax.axis_index("head")
    theirs = swap_core(mine) if theirs is None else theirs
    rows, both = mine.shape
    shapes = [jax.ShapeDtypeStruct((rows, 2 * both - 4 * turned), BF)]
    if turned:
        shapes.append(jax.ShapeDtypeStruct((4 * turned, rows) if turn else (rows, 4 * turned), BF))
    return pl.pallas_call(
        lambda *refs: order_kernel(turned, turn, *refs),
        in_specs=[pl.BlockSpec(memory_space=pltpu.SMEM)]
        + [pl.BlockSpec(memory_space=pltpu.VMEM)] * 2,
        out_specs=[pl.BlockSpec(memory_space=pltpu.VMEM)] * len(shapes),
        out_shape=shapes,
        compiler_params=pltpu.CompilerParams(vmem_limit_bytes=32 * 1024 * 1024),
    )(jnp.stack([head % 2, head // 2]).astype(jnp.int32), mine, theirs)


def normalize(values):
    centred = values - jnp.mean(values, -1, keepdims=True)
    scale = lax.rsqrt(jnp.mean(centred * centred, -1, keepdims=True) + 1e-06)
    return centred * scale, scale


def normalize_back(grad, unit, scale, gain):
    grad_unit = grad * gain
    return scale * (
        grad_unit
        - jnp.mean(grad_unit, -1, keepdims=True)
        - unit * jnp.mean(grad_unit * unit, -1, keepdims=True)
    )


def soft_columns(keys, queries, length):
    scores = dot(keys, queries, 1, 1)
    places = lax.broadcasted_iota(jnp.int32, (keys.shape[0], 1), 0)
    scores = jnp.where(places < length, scores, -1e30)
    scores = jnp.exp(scores - jnp.max(scores, 0, keepdims=True))
    return scores * (1.0 / jnp.sum(scores, 0, keepdims=True))


def parts_of(packed, spans):
    for head in range(packed.shape[1] // (3 * HD)):
        base = head * 3 * HD
        for start, rows, length in spans:
            span = slice(start, start + rows)
            queries = packed[span, base : base + HD] * HD ** (-0.5)
            keys = packed[span, base + HD : base + 2 * HD]
            values = packed[span, base + 2 * HD : base + 3 * HD]
            yield head, base, span, length, queries, keys, values


def attend_kernel(spans, packed, out):
    for head, _, span, length, queries, keys, values in parts_of(packed, spans):
        soft = soft_columns(keys, queries, length).astype(BF)
        out[span, head * HD : (head + 1) * HD] = dot(values, soft, 0, 0).T.astype(BF)


def attend_back_kernel(spans, packed, grad, out):
    for head, base, span, length, queries, keys, values in parts_of(packed, spans):
        grads = grad[span, head * HD : (head + 1) * HD]
        soft = soft_columns(keys, queries, length)
        out[span, base + 2 * HD : base + 3 * HD] = dot(soft.astype(BF), grads).astype(BF)
        grad_soft = dot(values, grads, 1, 1)
        grad_scores = soft * (grad_soft - jnp.sum(soft * grad_soft, 0, keepdims=True))
        grad_scores = grad_scores.astype(BF)
        grad_queries = dot(keys, grad_scores, 0, 0).T * HD ** (-0.5)
        out[span, base : base + HD] = grad_queries.astype(BF)
        out[span, base + HD : base + 2 * HD] = dot(grad_scores, queries).astype(BF)


def attention(kernel, spans, packed, *grads, begin=0, stop=None, into=None):
    tokens, width = packed.shape
    stop = width // (6 * HD) if stop is None else stop
    wide = pl.BlockSpec((tokens, 6 * HD), lambda step: (0, step + begin))
    narrow = pl.BlockSpec((tokens, 2 * HD), lambda step: (0, step + begin))
    filled = [] if into is None else [into]
    count = 1 + len(grads)

    def run(*refs):
        kernel(spans, *refs[:count], refs[-1])

    return pl.pallas_call(
        run,
        grid=(stop - begin,),
        in_specs=[wide] + [narrow] * len(grads) + [pl.BlockSpec(memory_space=pl.ANY)] * len(filled),
        out_specs=wide if grads else narrow,
        out_shape=jax.ShapeDtypeStruct((tokens, width if grads else width // 3), BF),
        input_output_aliases={count: 0} if filled else {},
        compiler_params=pltpu.CompilerParams(vmem_limit_bytes=40 * 1024 * 1024),
    )(packed, *grads, *filled)


def row_kind(first, rows, spans):
    places = first + lax.broadcasted_iota(jnp.int32, (rows, 1), 0)
    return [(places >= start) & (places < start + length) for start, _, length in spans]


def row_grid(kernel, spans, inputs, rows, tables, outs):
    tokens, width = inputs[0].shape

    def body(*refs):
        first = pl.program_id(0) * rows
        kinds = row_kind(first, rows, spans)
        sums = refs[-1]

        @pl.when(pl.program_id(0) == 0)
        def _():
            sums[...] = jnp.zeros_like(sums)

        kernel(first, kinds, *refs)

    block = pl.BlockSpec((rows, width), lambda step: (step, 0))
    return pl.pallas_call(
        body,
        grid=(tokens // rows,),
        in_specs=[block] * len(inputs)
        + [pl.BlockSpec(table.shape, lambda step: (0, 0)) for table in tables],
        out_specs=[block] * len(outs) + [pl.BlockSpec((8, width), lambda step: (0, 0))],
        out_shape=[jax.ShapeDtypeStruct((tokens, width), kind) for kind in outs]
        + [jax.ShapeDtypeStruct((8, width), F32)],
        compiler_params=pltpu.CompilerParams(vmem_limit_bytes=32 * 1024 * 1024),
    )(*inputs, *tables)


def add_row(sums, index, values):
    sums[index : index + 1, :] += jnp.sum(values, 0, keepdims=True)


def middle_kernel(first, kinds, initial, mine, theirs, vec, middle, normed, sums):
    branch = mine[...].astype(F32) + theirs[...].astype(F32)
    values = initial[...] + vec[7:8, :] + branch
    unit, _ = normalize(values)
    middle[...] = values
    normed[...] = (unit * vec[2:3, :] + vec[3:4, :]).astype(BF)
    for index, kind in enumerate(kinds):
        add_row(sums, index, jnp.where(kind, values, 0.0))


def middle_back_kernel(first, kinds, middle, mine, theirs, vec, rows, out, sums):
    grad = mine[...].astype(F32) + theirs[...].astype(F32)
    unit, scale = normalize(middle[...])
    back = normalize_back(grad, unit, scale, vec[2:3, :])
    back = back + jnp.where(kinds[0], rows[0:1, :], jnp.where(kinds[1], rows[1:2, :], 0.0))
    out[...] = back.astype(BF)
    add_row(sums, 0, grad * unit)
    add_row(sums, 1, grad)
    add_row(sums, 2, back)


def initial_back_kernel(spans, first, kinds, initial, mine, theirs, middle, vec, out, sums):
    grad = mine[...].astype(F32) + theirs[...].astype(F32)
    unit, scale = normalize(initial[...])
    back = normalize_back(grad, unit, scale, vec[0:1, :]) + middle[...].astype(F32)
    out[...] = back.astype(BF)
    places = first + lax.broadcasted_iota(jnp.int32, (back.shape[0], 1), 0)
    is_class = (places == spans[0][0] + spans[0][2] - 1) | (places == spans[1][0] + spans[1][2] - 1)
    of_class = jnp.where(is_class, back, 0.0)
    add_row(sums, 0, grad * unit)
    add_row(sums, 1, grad)
    add_row(sums, 2, jnp.where(kinds[0] | kinds[1], back, 0.0) - of_class)
    add_row(sums, 3, of_class)


def hidden_kernel(spans, normed, weight, slope, sums):
    upward = dot(normed[...], weight[...])
    cumulative = 0.5 * (1.0 + lax.erf(upward * (0.5**0.5)))
    bell = jnp.exp(-0.5 * upward * upward) * (2.0 * math.pi) ** (-0.5)
    slope[...] = (cumulative + upward * bell).astype(BF)
    active = (upward * cumulative).astype(BF).astype(F32)
    sums[...] = jnp.zeros_like(sums)
    for index, (start, _, length) in enumerate(spans):
        rows = up_to(length, 16)
        part = active[start : start + rows]
        kept = lax.broadcasted_iota(jnp.int32, (rows, 1), 0) < length
        sums[index : index + 1, :] = jnp.sum(jnp.where(kept, part, 0.0), 0, keepdims=True)


def hidden_layer(spans, normed, weight):
    tokens, width = normed.shape
    columns = weight.shape[1]
    step = 256
    return pl.pallas_call(
        lambda *refs: hidden_kernel(spans, *refs),
        grid=(columns // step,),
        in_specs=[
            pl.BlockSpec((tokens, width), lambda index: (0, 0)),
            pl.BlockSpec((width, step), lambda index: (0, index)),
        ],
        out_specs=[
            pl.BlockSpec((tokens, step), lambda index: (0, index)),
            pl.BlockSpec((8, step), lambda index: (0, index)),
        ],
        out_shape=[
            jax.ShapeDtypeStruct((tokens, columns), BF),
            jax.ShapeDtypeStruct((8, columns), F32),
        ],
        compiler_params=pltpu.CompilerParams(vmem_limit_bytes=40 * 1024 * 1024),
    )(normed, weight)


def iterate_kernel(start, kept, came, came_side, rows_out, total_out):
    step = D // 3
    rows = rows_out.shape[0]
    parts = kept[start[1]], came[start[1]], came_side[...]
    blocks = [sum(part[index].astype(F32) for part in parts) for index in range(6)]
    same = lax.broadcasted_iota(jnp.int32, (step, step), 0) == lax.broadcasted_iota(
        jnp.int32, (step, step), 1
    )
    total = jnp.sum(jnp.where(same, blocks[0] + blocks[3] + blocks[5], 0.0))
    inverse = 1.0 / (jnp.sqrt(jnp.full((1, 1), total, F32)) + 1e-07)
    total_out[...] = jnp.full(total_out.shape, total, F32)
    aa, ab, ac, bb, bc, cc = [blocks[index] * (inverse * inverse) for index in range(6)]
    gram = jnp.concatenate(
        [
            jnp.concatenate([aa, ab, ac], 1),
            jnp.concatenate([ab.T, bb, bc], 1),
            jnp.concatenate([ac.T, bc.T, cc], 1),
        ],
        0,
    )
    eye = (
        lax.broadcasted_iota(jnp.int32, (D, D), 0) == lax.broadcasted_iota(jnp.int32, (D, D), 1)
    ).astype(F32)
    chosen = (
        lax.broadcasted_iota(jnp.int32, (rows, D), 0) + start[0]
        == lax.broadcasted_iota(jnp.int32, (rows, D), 1)
    ).astype(F32)
    polynomials = []
    for _ in range(NS_STEPS - 1):
        low = gram.astype(BF)
        polynomial = POLY_ONE * eye + POLY_TWO * gram + POLY_THREE * dot(low, low)
        polynomial = polynomial.astype(BF)
        polynomials.append(polynomial)
        gram = dot(dot(low, polynomial).astype(BF), polynomial)
    low = gram.astype(BF)
    gram_rows = dot(chosen.astype(BF), low)
    out = POLY_ONE * chosen + POLY_TWO * gram_rows + POLY_THREE * dot(gram_rows.astype(BF), low)
    for polynomial in polynomials[::-1]:
        out = dot(out.astype(BF), polynomial)
    rows_out[...] = (out * inverse).astype(BF)


def iterate_gram(start, kept, came, came_side, rows):
    vmem = pl.BlockSpec(memory_space=pltpu.VMEM)
    return pl.pallas_call(
        iterate_kernel,
        in_specs=[pl.BlockSpec(memory_space=pltpu.SMEM)] + [vmem] * 3,
        out_specs=[vmem] * 2,
        out_shape=[
            jax.ShapeDtypeStruct((rows, D), BF),
            jax.ShapeDtypeStruct((8, 128), F32),
        ],
        compiler_params=pltpu.CompilerParams(vmem_limit_bytes=48 * 1024 * 1024),
    )(start.astype(jnp.int32), kept, came, came_side)


def adam_update(weight, gradient, first, second, rate, decay):
    first = BETA_FIRST * first + (1.0 - BETA_FIRST) * gradient
    second = BETA_SECOND * second + (1.0 - BETA_SECOND) * gradient * gradient
    direction = (
        first
        / (1.0 - BETA_FIRST**STEP)
        / (jnp.sqrt(second / (1.0 - BETA_SECOND**STEP)) + ADAM_FLOOR)
    )
    return (weight - rate * (direction + decay * weight), first, second)


def square_sum(own, shared, count):
    arrays = (*own, *shared)

    def kernel(*refs):
        total = jnp.zeros((1, 1), F32)
        for index, ref in enumerate(refs[:-1]):
            values = ref[...]
            rows = jnp.sum(values * values, 1, keepdims=True)
            part = jnp.sum(rows, 0, keepdims=True)
            total = total + (part if index < len(own) else part / count)
        refs[-1][...] = jnp.broadcast_to(total, (8, 128))

    vmem = pl.BlockSpec(memory_space=pltpu.VMEM)
    return pl.pallas_call(
        kernel,
        in_specs=[vmem] * len(arrays),
        out_specs=vmem,
        out_shape=jax.ShapeDtypeStruct((8, 128), F32),
    )(*arrays)


def moment_kernel(pieces, count, factor, *refs):
    olds, grads, moments = (refs[index * count : (index + 1) * count] for index in range(3))
    blocks = refs[-1]
    step = D // 3
    place = 0
    for old, grad, moment in zip(olds, grads, moments):
        before = old[...].astype(F32)
        moment[...] = (MOMENTUM * before + factor[0] * grad[...].astype(F32)).astype(BF)
        for low, top in pieces:
            matrix = moment[:, low:top]
            for row, column in ((0, 0), (0, 1), (0, 2), (1, 1), (1, 2), (2, 2)):
                left = matrix[row * step : (row + 1) * step]
                right = matrix[column * step : (column + 1) * step]
                blocks[place // 6, place % 6] = dot(left, right, 1, 1).astype(BF)
                place += 1


def moment_grams(factor, old, block, grads, pieces):
    count, rows = len(grads), old.shape[0]
    width = grads[0].shape[1]
    whole = pl.BlockSpec((rows, width), lambda step: (0, 0))
    olds = [
        pl.BlockSpec((rows, width), lambda step, index=block + place: (0, index))
        for place in range(count)
    ]
    shape = (count * len(pieces), 6, D // 3, D // 3)
    *moments, blocks = pl.pallas_call(
        lambda *refs: moment_kernel(pieces, count, *refs),
        grid=(1,),
        in_specs=[pl.BlockSpec(memory_space=pltpu.SMEM)] + olds + [whole] * count,
        out_specs=[whole] * count + [pl.BlockSpec(shape, lambda step: (0, 0, 0, 0))],
        out_shape=[jax.ShapeDtypeStruct((rows, width), BF)] * count
        + [jax.ShapeDtypeStruct(shape, BF)],
        compiler_params=pltpu.CompilerParams(vmem_limit_bytes=56 * 1024 * 1024),
    )(jnp.reshape(factor, (1,)), *[old] * count, *grads)
    return moments, blocks


def body(
    low_patches,
    high_patches,
    interp,
    labels,
    partner,
    pair_count,
    w_patch,
    pos_table,
    vectors,
    head_w,
    w_qkv,
    w_out,
    w_up,
    w_down,
    mom_qkv,
    mom_out,
    mom_up,
    mom_down,
    first_patch,
    second_patch,
    first_pos,
    second_pos,
    first_vec,
    second_vec,
    first_head,
    second_head,
):
    batch = lax.axis_index("batch")
    head = lax.axis_index("head")
    side = head // 2
    batch_size = lax.axis_size("batch")
    head_size = lax.axis_size("head")
    rows_here = w_patch.shape[0]
    grid_low, grid_high = low_patches.shape[1], high_patches.shape[1]
    low_rows = up_to(grid_low + 1, 16)
    high_rows = up_to(grid_high + 1, 16)
    tokens = low_rows + high_rows
    qkv_width, out_width = w_qkv.shape[1], w_out.shape[1]
    hidden = w_up.shape[1]
    patch_width = D // head_size
    extra_width = 64
    head_columns = head_w.shape[1]
    head_padded = up_to(head_columns, 64 * head_size)
    head_width = head_padded // head_size
    table_rows = extra_width * head_size

    pos_turned, vec_turned = pos_table.T, vectors.T
    table = jnp.concatenate([pos_turned[:, 1:], pos_turned[:, :1], vec_turned], 1).astype(BF)
    table = jnp.pad(table, ((0, 0), (0, table_rows - table.shape[1])))
    quarter_patch = lax.dynamic_slice_in_dim(w_patch, head * patch_width, patch_width, 1)
    quarter_table = lax.dynamic_slice_in_dim(table, head * extra_width, extra_width, 1)
    padded_head = jnp.pad(head_w.astype(BF), ((0, 0), (0, head_padded - head_columns)))
    quarter_head = lax.dynamic_slice_in_dim(padded_head, head * head_width, head_width, 1)
    small = patch_width + extra_width
    chunk_one = jnp.concatenate([quarter_patch.astype(BF), quarter_table, w_qkv.astype(BF)], 1)
    chunk_two = jnp.concatenate([w_out.astype(BF), w_up.astype(BF)], 1)
    chunk_three, chunk_four = w_down.astype(BF), quarter_head
    lines = gather_lines(chunk_one)
    patches = jnp.concatenate(
        [
            jnp.pad(at(low_patches, side), ((0, low_rows - grid_low), (0, 0))),
            jnp.pad(at(high_patches, side), ((0, high_rows - grid_high), (0, 0))),
        ],
        0,
    )
    chunk_two, chunk_four, lines, patches = tie(chunk_two, chunk_four, lines, patches)
    planes = gather_planes(lines)
    lines_two = gather_lines(chunk_two)
    planes, lines_two = tie(planes, lines_two)
    ends = gather_ends(planes)
    planes_two = gather_planes(lines_two)
    both_small, full_qkv = gather_last(planes, ends, (small, qkv_width))
    full_patch, table = all_quarters(both_small, extra_width)
    chunk_three, full_patch = tie(chunk_three, full_patch)
    lines_three = gather_lines(chunk_three)

    class_row = grid_low
    vec = table[grid_low + 1 : grid_low + 11].astype(F32)
    pos_low = table[:low_rows].astype(F32)
    pos_high = dot(interp, table[:grid_low])
    row_low = jnp.arange(low_rows)[:, None]
    row_high = jnp.arange(high_rows)[:, None]
    class_add = table[class_row].astype(F32) + vec[9]
    add_low = jnp.where(
        row_low < grid_low, pos_low + vec[6], jnp.where(row_low == grid_low, class_add, 0.0)
    )
    pos_high = jnp.pad(pos_high, ((0, high_rows - grid_high), (0, 0)))
    add_high = jnp.where(
        row_high < grid_high, pos_high + vec[6], jnp.where(row_high == grid_high, class_add, 0.0)
    )
    added = jnp.concatenate([add_low, add_high], 0)
    is_patch = jnp.concatenate([row_low < grid_low, row_high < grid_high], 0)
    is_token = jnp.concatenate([row_low <= grid_low, row_high <= grid_high], 0)
    initial = dot(patches, full_patch) + added
    unit_one, _ = normalize(initial)
    normed = (unit_one * vec[0] + vec[1]).astype(BF)
    packed = dot(normed, full_qkv).astype(BF)
    packed, planes_two, lines_three, chunk_four = tie(
        packed, planes_two, lines_three, chunk_four
    )
    came_four = gather_came(chunk_four)
    ends_two = gather_ends(planes_two)
    planes_three = gather_planes(lines_three)
    spans = ((0, low_rows, grid_low + 1), (low_rows, high_rows, grid_high + 1))
    blended = attention(attend_kernel, spans, packed)
    full_out, full_up = gather_last(planes_two, ends_two, (out_width, hidden))
    branch = dot(blended, full_out, 1, 1).astype(BF)
    block_rows = 160
    middle, normed_two, middle_sums = row_grid(
        middle_kernel, spans, (initial, branch, swap_core(branch)), block_rows, (vec,), (F32, BF)
    )
    normed_two, planes_three = tie(normed_two, planes_three)
    ends_three = gather_ends(planes_three)
    slope, active_sums = hidden_layer(spans, normed_two, full_up)
    active_sums = active_sums[:2]
    slope, ends_three, came_four = tie(slope, ends_three, came_four)
    planes_four = gather_planes(jnp.stack([chunk_four, *came_four]) if batch_size == 8 else came_four[0])
    (full_down,) = gather_last(planes_three, ends_three, (hidden,))
    (both_head,) = gather_last(planes_four, gather_ends(planes_four), (head_width,))
    (full_head,) = all_quarters(both_head)
    held = jnp.concatenate([mom_qkv, mom_out, mom_up, mom_down], 1).astype(BF)
    held, full_down = tie(held, full_down)
    full_old = lax.all_gather(held, "batch", axis=0, tiled=True)

    lengths = jnp.array([[grid_low + 1.0], [grid_high + 1.0]], F32)
    active_means = active_sums / lengths
    means_high = active_means.astype(BF)
    means_low = (active_means - means_high.astype(F32)).astype(BF)
    down_parts = dot(jnp.concatenate([means_high, means_low]), full_down, 1, 1)
    down_part = down_parts[:2] + down_parts[2:]
    down_part = down_part + swap_core(down_part)
    pooled_own = middle_sums[:2] / lengths + vec[8] + down_part

    ids = jnp.stack([side, low_patches.shape[0] + side])
    own_labels, own_partners = labels[ids], partner[ids]
    tags = jnp.stack([own_labels // 8, own_labels % 8, own_partners // 8, own_partners % 8], 1)
    pooled_high = pooled_own.astype(BF)
    pooled_low = (pooled_own - pooled_high.astype(F32)).astype(BF)
    tags = jnp.pad(tags.astype(BF), ((0, 0), (0, 124)))
    common = jnp.concatenate([pooled_high, pooled_low, tags], 1)
    active_low = active_sums.astype(BF)
    came = swap_side(jnp.concatenate([common, active_low[:, hidden:]], 1))
    mine = jnp.concatenate([common, active_low[:, :hidden]], 1)
    both_sides = in_order(jnp.stack([mine, came]), side, 1)
    everyone = gather_small(both_sides.transpose(1, 0, 2))
    everyone, full_head = tie(everyone, full_head)
    images = batch_size * 4
    everyone = everyone.reshape(images, 2 * D + 128 + hidden)
    pooled = everyone[:, :D].astype(F32) + everyone[:, D : 2 * D].astype(F32)
    all_tags = everyone[:, 2 * D : 2 * D + 4].astype(jnp.int32)
    all_labels = all_tags[:, 0] * 8 + all_tags[:, 1]
    all_partners = all_tags[:, 2] * 8 + all_tags[:, 3]
    all_sums = everyone[:, 2 * D + 128 :]
    unit_final, scale_final = normalize(pooled)
    features = (unit_final * vec[4] + vec[5]).astype(BF)
    outputs = dot(features, full_head)
    logits, projected = outputs[:, :CLS], outputs[:, CLS:head_columns]
    picked = jnp.arange(CLS)[None, :] == all_labels[:, None]
    logit_top = jnp.max(logits, -1, keepdims=True)
    logit_log = logit_top + jnp.log(jnp.sum(jnp.exp(logits - logit_top), -1, keepdims=True))
    class_terms = logit_log - jnp.sum(jnp.where(picked, logits, 0.0), -1, keepdims=True)
    grad_logits = (jnp.exp(logits - logit_log) - picked.astype(F32)) * (1.0 / images)
    length_inverse = lax.rsqrt(jnp.sum(projected * projected, -1, keepdims=True) + 1e-06)
    embedded = (projected * length_inverse).astype(BF)
    similar = dot(embedded, embedded, 1, 1) / SOFTMAX_TEMP
    image_ids = jnp.arange(images, dtype=jnp.int32)
    masked = jnp.where(image_ids[:, None] == image_ids[None, :], -1e30, similar)
    similar_top = jnp.max(masked, -1, keepdims=True)
    similar_log = similar_top + jnp.log(jnp.sum(jnp.exp(masked - similar_top), -1, keepdims=True))
    target = image_ids[None, :] == all_partners[:, None]
    pair_terms = similar_log - jnp.sum(jnp.where(target, similar, 0.0), -1, keepdims=True)
    losses = jnp.sum(jnp.concatenate([pair_terms, class_terms], 1), 0)
    count = pair_count[0].astype(F32)
    grad_similar = ((jnp.exp(masked - similar_log) - target.astype(F32)) / count).astype(BF)
    grad_embedded = (dot(grad_similar, embedded) + dot(grad_similar, embedded, 0, 0)) / SOFTMAX_TEMP
    grad_embedded = grad_embedded.astype(BF).astype(F32)
    grad_projected = length_inverse * grad_embedded - projected * (
        length_inverse**3 * jnp.sum(grad_embedded * projected, -1, keepdims=True)
    )
    grad_outputs = jnp.concatenate([grad_logits, grad_projected], 1).astype(BF)
    grad_outputs = jnp.pad(grad_outputs, ((0, 0), (0, head_padded - head_columns)))
    features_here = lax.dynamic_slice_in_dim(features, batch * rows_here, rows_here, 1)
    grad_head = dot(features_here, grad_outputs, 0, 0)[:, :head_columns]
    grad_features = dot(grad_outputs, full_head, 1, 1)
    grad_pooled = normalize_back(grad_features, unit_final, scale_final, vec[4])
    complete_rows = jnp.stack(
        [
            jnp.sum(grad_features * unit_final, 0),
            jnp.sum(grad_features, 0),
            jnp.sum(grad_pooled, 0),
        ]
    )
    is_low = (image_ids % 4) < 2
    grad_token = grad_pooled / jnp.where(is_low, grid_low + 1.0, grid_high + 1.0)[:, None]
    own_rows = [batch * 4 + side, batch * 4 + 2 + side]
    grad_own = jnp.stack([at(grad_token, index) for index in own_rows])
    grad_own_low = grad_own.astype(BF)

    def spread(pair, mask):
        rows = jnp.concatenate(
            [
                jnp.broadcast_to(pair[0], (low_rows, pair.shape[1])),
                jnp.broadcast_to(pair[1], (high_rows, pair.shape[1])),
            ],
            0,
        )
        return jnp.where(mask, rows, 0.0)

    grad_active = dot(grad_own_low, full_down)
    grad_upward = (spread(grad_active, is_token) * slope.astype(F32)).astype(BF)
    grad_normed_two = dot(grad_upward, full_up, 1, 1).astype(BF)
    grad_up = dot(normed_two, grad_upward, 0, 0).astype(BF)
    kept_up, came_up = reduce_first(grad_up[:, :hidden], grad_up[:, hidden:])
    grad_middle, middle_row_sums = row_grid(
        middle_back_kernel,
        spans,
        (middle, grad_normed_two, swap_core(grad_normed_two)),
        block_rows,
        (vec, jnp.pad(grad_own, ((0, 6), (0, 0)))),
        (BF,),
    )
    grad_blend = dot(grad_middle, full_out).astype(BF)
    grad_out = dot(grad_middle, blended, 0, 0).astype(BF)
    grad_packed = attention(attend_back_kernel, spans, packed, grad_blend)
    grad_normed = dot(grad_packed, full_qkv, 1, 1).astype(BF)
    grad_normed, came_up = tie(grad_normed, came_up)
    kept_up, came_up = reduce_second(kept_up, came_up)
    grad_qkv = dot(normed, grad_packed, 0, 0).astype(BF)
    tails = [
        jnp.concatenate(
            [
                grad_qkv[:, index * qkv_width : (index + 1) * qkv_width],
                grad_out[:, index * out_width : (index + 1) * out_width],
            ],
            1,
        )
        for index in range(2)
    ]
    kept_tail, came_tail = reduce_first(*tails)
    grad_initial, initial_row_sums = row_grid(
        lambda *refs: initial_back_kernel(spans, *refs),
        spans,
        (initial, grad_normed, swap_core(grad_normed), grad_middle),
        block_rows,
        (vec,),
        (BF,),
    )
    grad_initial, came_up = tie(grad_initial, came_up)
    kept_up, came_up = reduce_third(kept_up, came_up)
    from_high = dot(interp, grad_initial[low_rows : low_rows + grid_high], 0, 0)
    zero_row = jnp.zeros((1, D), F32)
    class_both = initial_row_sums[3:4]
    table_grad = jnp.concatenate(
        [
            grad_initial[:grid_low].astype(F32) + from_high,
            class_both,
            initial_row_sums[:2],
            middle_row_sums[:2],
            zero_row,
            zero_row,
            initial_row_sums[2:3],
            middle_row_sums[2:3],
            zero_row,
            class_both,
            jnp.zeros((table_rows - grid_low - 11, D), F32),
        ],
        0,
    )
    table_grad = table_grad.astype(BF).T

    def quarter_of(values, width, index):
        return lax.dynamic_slice_in_dim(values, index * width, width, 1)

    owners = (head, head ^ 2)
    columns = [quarter_of(grad_initial, patch_width, index) for index in owners]
    grad_patch = dot(patches, jnp.concatenate(columns, 1), 0, 0).astype(BF)
    grad_small = [
        jnp.concatenate(
            [
                grad_patch[:, index * patch_width : (index + 1) * patch_width],
                quarter_of(table_grad, extra_width, owner),
            ],
            1,
        )
        for index, owner in enumerate(owners)
    ]
    kept_small, came_small = reduce_first(*grad_small)
    came_small, came_tail, full_old = tie(came_small, came_tail, full_old)

    def beside(left, right):
        return [jnp.concatenate(pair, -1) for pair in zip(left, right)]

    kept_tail, came_tail = reduce_second(
        beside(kept_tail, kept_small), beside(came_tail, came_small)
    )
    came_tail, came_up = tie(came_tail, came_up)
    reduced_up = reduce_last(kept_up, came_up)
    full_grad_up = lax.all_gather(reduced_up.astype(BF), "batch", axis=0, tiled=True)
    kept_tail, came_tail = reduce_third(kept_tail, came_tail)
    reduced_tail = reduce_last(kept_tail, came_tail)
    own_width = qkv_width + out_width
    lines_tail = gather_lines(reduced_tail[:, :own_width].astype(BF))
    reduced_qkv = reduced_tail[:, :qkv_width]
    reduced_out = reduced_tail[:, qkv_width:own_width]
    full_grad_down = dot(grad_token.astype(BF), all_sums, 0, 0)
    reduced_down = lax.dynamic_slice_in_dim(full_grad_down, batch * rows_here, rows_here, 0)

    quarter = reduced_tail[:, own_width:]
    complete_here = lax.dynamic_slice_in_dim(complete_rows, batch * rows_here, rows_here, 1)
    muon_grads = (reduced_qkv, reduced_out, reduced_up, reduced_down)
    squares = square_sum(
        (reduced_tail, reduced_up, reduced_down), (grad_head, complete_here), head_size
    )
    for axis, mask in (("head", 1), ("head", 2), ("batch", 1)):
        squares = squares + swap(squares, axis, mask)
    quarter = quarter.astype(BF)
    quarters = jnp.concatenate([quarter, swap_side(quarter)], 1)
    partner_quarters = swap_core(quarters)
    reduced_patch, reduced_table = all_quarters(quarters, extra_width, partner_quarters, False)
    reduced_patch, reduced_table = reduced_patch.astype(F32), reduced_table.astype(F32)
    reduced_pos = jnp.concatenate(
        [reduced_table[:, grid_low : grid_low + 1], reduced_table[:, :grid_low]], 1
    )
    partial_vec = reduced_table[:, grid_low + 1 : grid_low + 11]
    complete_turned = complete_here.T
    reduced_vec = jnp.concatenate(
        [
            partial_vec[:, :4],
            complete_turned[:, :2],
            partial_vec[:, 6:8],
            complete_turned[:, 2:],
            partial_vec[:, 9:],
        ],
        1,
    )
    squares, lines_tail, *adam_grads = tie(
        squares, lines_tail, reduced_patch, reduced_pos, reduced_vec
    )
    tail_x = swap_x(lines_tail) if batch_size == 8 else lines_tail
    mask = 2
    while mask < batch_size:
        squares = squares + swap(squares, "batch", mask)
        mask *= 2
    norm = jnp.sqrt(squares[0, 0])
    factor = jnp.minimum(1.0, CLIP_NORM / norm)
    factor, full_grad_up = tie(factor, full_grad_up)
    old_moments = (mom_qkv, mom_out, mom_up, mom_down)
    old_weights = (w_qkv, w_out, w_up, w_down)
    starts = (0, qkv_width, own_width)
    (moment_up, moment_down), early_pair = moment_grams(
        factor, full_old, 1, (full_grad_up, full_grad_down), ((0, hidden),)
    )
    early_pair, tail_x = tie(early_pair, tail_x)
    full_tail = gather_batch(lines_tail, tail_x)

    (moment_tail,), late_pair = moment_grams(
        factor, full_old, 0, (full_tail,), ((0, qkv_width), (qkv_width, own_width))
    )
    on_first = head % 2 == 0
    came = swap_core(jnp.where(on_first, early_pair, late_pair))
    kept = jnp.where(on_first, late_pair, early_pair)
    sent = (at(kept, 1 - side).astype(F32) + at(came, 1 - side).astype(F32)).astype(BF)
    came_side = swap_side(sent)
    middle_factor, adam_grads, firsts, seconds, _ = tie(
        factor,
        (*adam_grads, grad_head),
        (first_patch, first_pos.T, first_vec.T, first_head),
        (second_patch, second_pos.T, second_vec.T, second_head),
        sent,
    )
    adam_weights = (w_patch, pos_turned, vec_turned, head_w)
    moments = [
        MOMENTUM * old_moments[index] + middle_factor * muon_grads[index] for index in range(4)
    ]
    adam_new = [
        adam_update(
            adam_weights[index],
            middle_factor * adam_grads[index],
            firsts[index],
            seconds[index],
            ADAM_RATES[index],
            ADAM_DECAYS[index],
        )
        for index in range(4)
    ]
    for index in (1, 2):
        adam_new[index] = [part.T for part in adam_new[index]]
    rows, total_here = iterate_gram(
        jnp.stack([batch * rows_here, side]), kept, came, came_side, rows_here
    )
    rows_side = swap_side(rows)
    rows_side, total_here = tie(rows_side, total_here)
    pair = jnp.stack([rows, rows_side])
    four = jnp.concatenate([pair, swap_core(pair)])
    slots = jnp.arange(8)[:, None] == swapped(head)
    totals = sum_over_head(jnp.where(slots, total_here, 0.0))
    moment_logs = jnp.log(totals[:4, 0])
    parts = (moment_tail[:, :qkv_width], moment_tail[:, qkv_width:], moment_up, moment_down)
    new_muon = []
    for index in range(4):
        weight = old_weights[index]
        scale = 0.2 * math.sqrt(max(D, weight.shape[1] * head_size))
        iterate = dot(at(four, swapped(head ^ swapped(index))), parts[index])
        new_muon.append(weight - MUON_RATE * (scale * iterate + DECAY_RATE * weight))
    return (
        adam_new[0][0],
        adam_new[1][0],
        adam_new[2][0],
        adam_new[3][0],
        new_muon[0],
        new_muon[1],
        new_muon[2],
        new_muon[3],
        moments[0],
        moments[1],
        moments[2],
        moments[3],
        adam_new[0][1],
        adam_new[1][1],
        adam_new[2][1],
        adam_new[3][1],
        adam_new[0][2],
        adam_new[1][2],
        adam_new[2][2],
        adam_new[3][2],
        losses,
        norm[None],
        moment_logs,
    )


def solution(mesh):
    placed = (
        P("batch", None, None),
        P("batch", None, None),
        P(),
        P("batch"),
        P("batch"),
        P(),
        P("batch", None),
        P(None, "batch"),
        P(None, "batch"),
        P("batch", None),
        P("batch", "head"),
        P("batch", "head"),
        P("batch", "head"),
        P("batch", "head"),
        P("batch", "head"),
        P("batch", "head"),
        P("batch", "head"),
        P("batch", "head"),
        P("batch", None),
        P("batch", None),
        P(None, "batch"),
        P(None, "batch"),
        P(None, "batch"),
        P(None, "batch"),
        P("batch", None),
        P("batch", None),
    )
    return jax.shard_map(
        body,
        mesh=mesh,
        in_specs=placed,
        out_specs=(
            P("batch", None),
            P(None, "batch"),
            P(None, "batch"),
            P("batch", None),
            P("batch", "head"),
            P("batch", "head"),
            P("batch", "head"),
            P("batch", "head"),
            P("batch", "head"),
            P("batch", "head"),
            P("batch", "head"),
            P("batch", "head"),
            P("batch", None),
            P(None, "batch"),
            P(None, "batch"),
            P("batch", None),
            P("batch", None),
            P(None, "batch"),
            P(None, "batch"),
            P("batch", None),
            P(),
            P(),
            P(),
        ),
        check_vma=False,
    )
```
